32 devices in a mesh: dp: 4 (over y, x), fsdp: 8 (over z, core).
Axes of the slice: x: 2, y: 2, z: 4, core: 2. Of those that a mesh axis runs over, the one named last changes fastest.
Arguments:
- mel: bfloat16 [32768, 80], P(('dp', 'fsdp')), may hold values from -6 to 6
- cotangent: bfloat16 [4096, 512], P(('dp', 'fsdp')), may hold values from -6 to 6
- lengths: int32 [128], replicated, may hold values from 8 to 104, as said below
- assignment: int32 [128], replicated, may hold values from 0 to 31, as said below
- time_spans: int32 [32, 2, 2], P(('dp', 'fsdp')), may hold values from 0 to 984, as said below
- freq_spans: int32 [32, 2, 2], P(('dp', 'fsdp')), may hold values from 0 to 53, as said below
- contexts: int32 [8], replicated, may hold values from 16 to 128
- stem_kernels: bfloat16 [3, 9, 256], P(None, None, ('dp', 'fsdp')), may hold values from -2 to 2
- stem_point: bfloat16 [2, 256, 256], P(None, ('dp', 'fsdp')), may hold values from -0.375 to 0.375
- stem_out: bfloat16 [2560, 512], P(('dp', 'fsdp')), may hold values from -0.125 to 0.125
- ffn_in: bfloat16 [2, 512, 2048], P(None, ('dp', 'fsdp')), may hold values from -0.25 to 0.25
- ffn_out: bfloat16 [2, 2048, 512], P(None, ('dp', 'fsdp')), may hold values from -1 to 1
- qkv: bfloat16 [512, 1536], P(('dp', 'fsdp')), may hold values from -0.25 to 0.25
- attn_out: bfloat16 [512, 512], P(('dp', 'fsdp')), may hold values from -2 to 2
- conv_in: bfloat16 [512, 1024], P(('dp', 'fsdp')), may hold values from -0.25 to 0.25
- conv_depth: bfloat16 [9, 512], P(None, ('dp', 'fsdp')), may hold values from -2 to 2
- conv_out: bfloat16 [512, 512], P(('dp', 'fsdp')), may hold values from -0.75 to 0.75
- norm_gains: bfloat16 [6, 512], P(None, ('dp', 'fsdp')), may hold values from 0.25 to 1.75
- norm_shifts: bfloat16 [5, 512], P(None, ('dp', 'fsdp')), may hold values from -1.5 to 1.5
- final_shift: bfloat16 [512], P(('dp', 'fsdp')), may hold values from -1.5 to 1.5
Outputs:
- activations: bfloat16 [4096, 512], P(('dp', 'fsdp'))
- mel_grad: float32 [32768, 80], P(('dp', 'fsdp'))
- grad_stem_kernels: float32 [3, 9, 256], P(None, None, ('dp', 'fsdp'))
- grad_stem_point: float32 [2, 256, 256], P(None, ('dp', 'fsdp'))
- grad_stem_out: float32 [2560, 512], P(('dp', 'fsdp'))
- grad_ffn_in: float32 [2, 512, 2048], P(None, ('dp', 'fsdp'))
- grad_ffn_out: float32 [2, 2048, 512], P(None, ('dp', 'fsdp'))
- grad_qkv: float32 [512, 1536], P(('dp', 'fsdp'))
- grad_attn_out: float32 [512, 512], P(('dp', 'fsdp'))
- grad_conv_in: float32 [512, 1024], P(('dp', 'fsdp'))
- grad_conv_depth: float32 [9, 512], P(None, ('dp', 'fsdp'))
- grad_conv_out: float32 [512, 512], P(('dp', 'fsdp'))
- grad_norm_gains: float32 [6, 512], P(None, ('dp', 'fsdp'))
- grad_norm_shifts: float32 [5, 512], P(None, ('dp', 'fsdp'))
- grad_final_shift: float32 [512], P(('dp', 'fsdp'))
The draws below stay inside these ranges and needn't reach their ends.
Inputs may be any that keep to these rules, and one draw needn't show every extreme that they name: Each device holds exactly 4 utterances whose lengths sum to between 64 and 128; some device holds one utterance of the largest length. `assignment`: device numbers d = dp index * 8 + fsdp index; every device receives exactly 4 utterances. `time_spans`: pairs (first input frame counted from the device's first input frame, width); widths are 0 to 40. `freq_spans`: pairs (first bin, width); widths are 0 to 27.
All inputs are finite; a program needn't handle non-finite values.
Results may differ from the reference program's by a relative error of at most 0.033.
Values may be sent and summed in bfloat16 or wider, within the bound.
A program may use at most 320 MiB of HBM per device.

```python
import jax
import jax.numpy as jnp
from jax import lax

MEL = 80
CH = 256
D = 512
HEADS = 8
FF = 2048
KERNEL = 9
CTX = 128
TOK_DEV = 128
SLOTS = 4
SHORT = 8
TWIDTH = 40
FWIDTH = 27
TIME_MASKS = 2
FREQ_MASKS = 2
FRAMES = 4096
STEM_IN = 2560
N_DP = 4
N_FSDP = 8


def utterance_layout(key):
    devices = N_DP * N_FSDP
    pieces = jax.random.split(jax.random.fold_in(key, 11), 5)
    longest = TOK_DEV - (SLOTS - 1) * SHORT
    chosen = jax.random.randint(pieces[0], (devices,), 0, 4) == 0
    forced = jax.random.randint(pieces[1], (), 0, devices)
    chosen = chosen | (jnp.arange(devices, dtype=jnp.int32) == forced)
    filled = jnp.where(chosen, TOK_DEV, jax.random.randint(pieces[2], (devices,), TOK_DEV // 2, TOK_DEV + 1))
    shares = jax.random.randint(pieces[3], (devices, SLOTS), 1, 100)
    spare = filled - SLOTS * SHORT
    portions = spare[:, None] * shares // jnp.sum(shares, axis=1, keepdims=True)
    portions = portions.at[:, 0].add(spare - jnp.sum(portions, axis=1))
    long_row = jnp.concatenate([jnp.full((1,), longest, jnp.int32), jnp.full((SLOTS - 1,), SHORT, jnp.int32)])
    table = jnp.where(chosen[:, None], long_row[None, :], SHORT + portions).astype(jnp.int32)
    ordering = jax.random.permutation(pieces[4], devices * SLOTS)
    return (table.reshape(-1)[ordering], (ordering // SLOTS).astype(jnp.int32))


def draw_lengths(key, part):
    return utterance_layout(key)[0]


def draw_assignment(key, part):
    return utterance_layout(key)[1]


def span_table(key, masks_each, latest, widest):
    devices = N_DP * N_FSDP
    entries = devices * masks_each
    pieces = jax.random.split(key, 3)
    starts = jax.random.randint(pieces[0], (entries,), 0, latest + 1)
    widths = jax.random.randint(pieces[1], (entries,), 0, widest + 1)
    picks = jax.random.randint(pieces[2], (2,), 0, entries)
    starts = starts.at[picks[0]].set(latest)
    starts = starts.at[(picks[0] + 1) % entries].set(0)
    widths = widths.at[picks[1]].set(widest)
    return jnp.stack([starts, widths], axis=1).reshape(devices, masks_each, 2).astype(jnp.int32)


def draw_time_spans(key, part):
    key = jax.random.fold_in(key, 3)
    return span_table(key, TIME_MASKS, 8 * TOK_DEV - TWIDTH, TWIDTH)


def draw_freq_spans(key, part):
    key = jax.random.fold_in(key, 5)
    return span_table(key, FREQ_MASKS, MEL - FWIDTH, FWIDTH)


def draw_contexts(key, part):
    key = jax.random.fold_in(key, 7)
    pieces = jax.random.split(key, 3)
    lowest = max(1, CTX // 8)
    reaches = jax.random.randint(pieces[0], (HEADS,), lowest, CTX + 1)
    widest = jax.random.randint(pieces[1], (), 0, HEADS)
    narrow = (widest + 1 + jax.random.randint(pieces[2], (), 0, HEADS - 1)) % HEADS
    return reaches.at[widest].set(CTX).at[narrow].set(lowest).astype(jnp.int32)


def level_of(key, extent, cuts, smallest, high):
    gain, own = 1.0, jax.random.fold_in(key, 6)
    for axis_at, parts in cuts:
        heights = jnp.exp(jax.random.uniform(jax.random.fold_in(own, axis_at), (parts,), jnp.float32, smallest / len(cuts), high / len(cuts)))
        gain = gain * jnp.repeat(heights, extent[axis_at] // parts).reshape([-1 if axis == axis_at else 1 for axis in range(len(extent))])
    return gain


def gaussian(stream_key, extent, width, most, cuts=(), held_as=jnp.bfloat16):
    level = level_of(stream_key, extent, cuts, -0.22, 0.18) if cuts else 1.0
    values = jax.random.normal(stream_key, extent, jnp.float32) * width * level
    return jnp.minimum(jnp.maximum(values, -most), most).astype(held_as)


def setup_inputs(seed: int = 0) -> dict:
    key_list = jax.random.split(jax.random.key(seed), 21)
    return {
        "mel": gaussian(key_list[0], (8 * FRAMES, MEL), 1.0, 6.0, ((0, 32),)),
        "cotangent": gaussian(key_list[1], (FRAMES, D), 1.0, 6.0, ((0, 32),)),
        "lengths": draw_lengths(jax.random.fold_in(key_list[20], 71), 0),
        "assignment": draw_assignment(jax.random.fold_in(key_list[20], 71), 0),
        "time_spans": draw_time_spans(jax.random.fold_in(key_list[20], 71), 0),
        "freq_spans": draw_freq_spans(jax.random.fold_in(key_list[20], 71), 0),
        "contexts": draw_contexts(jax.random.fold_in(key_list[20], 71), 0),
        "stem_kernels": gaussian(key_list[7], (3, 9, CH), 9 ** -0.5, 2.0, ((2, 32),)),
        "stem_point": gaussian(key_list[8], (2, CH, CH), CH ** -0.5, 0.375, ((1, 32),)),
        "stem_out": gaussian(key_list[9], (STEM_IN, D), STEM_IN ** -0.5, 0.125, ((0, 32),)),
        "ffn_in": gaussian(key_list[10], (2, D, FF), D ** -0.5, 0.25, ((1, 32),)),
        "ffn_out": gaussian(key_list[11], (2, FF, D), (FF // 64) ** -0.5, 1.0, ((1, 32),)),
        "qkv": gaussian(key_list[12], (D, 3 * D), D ** -0.5, 0.25, ((0, 32),)),
        "attn_out": gaussian(key_list[13], (D, D), (D // 64) ** -0.5, 2.0, ((0, 32),)),
        "conv_in": gaussian(key_list[14], (D, 2 * D), D ** -0.5, 0.25, ((0, 32),)),
        "conv_depth": gaussian(key_list[15], (KERNEL, D), KERNEL ** -0.5, 2.0, ((1, 32),)),
        "conv_out": gaussian(key_list[16], (D, D), (D // 8) ** -0.5, 0.75, ((0, 32),)),
        "norm_gains": jnp.clip(1.0 + 0.15 * jax.random.normal(key_list[17], (6, D), jnp.float32), 0.25, 1.75).astype(jnp.bfloat16),
        "norm_shifts": gaussian(key_list[18], (5, D), 0.3, 1.5, ((1, 32),)),
        "final_shift": gaussian(key_list[19], (D,), 0.3, 1.5, ((0, 32),)),
    }


EPSILON = 1e-05
MASKED_LOGIT = -1e+30

@jax.custom_vjp
def low(v):
    return lax.optimization_barrier(v.astype(jnp.bfloat16)).astype(jnp.float32)

@jax.custom_vjp
def low_back(v):
    return v

def low_keep(v):
    return (low(v), None)

def low_pass(kept, grad):
    return (grad,)

def back_keep(v):
    return (v, None)

def back_low(kept, grad):
    return (low(grad),)
low.defvjp(low_keep, low_pass)
low_back.defvjp(back_keep, back_low)

def frame_segments(lengths, assignment, device, frames):
    belongs = assignment == device
    own_sizes = jnp.where(belongs, lengths, 0).astype(jnp.int32)
    finishes = jnp.cumsum(own_sizes, dtype=jnp.int32)
    beginnings = finishes - own_sizes
    position = jnp.arange(frames, dtype=jnp.int32)[:, None]
    inside = belongs[None, :] & (position >= beginnings[None, :]) & (position < finishes[None, :])
    number = jnp.arange(lengths.shape[0], dtype=jnp.int32)[None, :] + 1
    return lax.optimization_barrier(jnp.sum(jnp.where(inside, number, 0), axis=1, dtype=jnp.int32)) - 1

def feature_keep(segments, time_spans, freq_spans, mel_bins):
    frames = segments.shape[0] * 8
    position = jnp.arange(frames, dtype=jnp.int32)[:, None]
    covered = (position >= time_spans[None, :, 0]) & (position < time_spans[None, :, 0] + time_spans[None, :, 1])
    time_keep = jnp.repeat(segments >= 0, 8) & jnp.logical_not(jnp.any(covered, axis=1))
    channel = jnp.arange(mel_bins, dtype=jnp.int32)[:, None]
    banned = (channel >= freq_spans[None, :, 0]) & (channel < freq_spans[None, :, 0] + freq_spans[None, :, 1])
    freq_keep = jnp.logical_not(jnp.any(banned, axis=1))
    return (time_keep[:, None] & freq_keep[None, :]).astype(jnp.float32)

def time_taps(values, seg_in, seg_out):
    out_len = seg_out.shape[0]
    paired = values.reshape((out_len, 2) + values.shape[1:])
    even_part = paired[:, 0]
    odd_part = paired[:, 1]
    prior_part = jnp.concatenate([jnp.zeros_like(odd_part[:1]), odd_part[:-1]], axis=0)
    seg_pairs = seg_in.reshape(out_len, 2)
    prior_segs = jnp.concatenate([jnp.full((1,), -2, jnp.int32), seg_pairs[:-1, 1]])
    opening = ((prior_segs == seg_out) & (seg_out >= 0)).astype(values.dtype)
    opening = opening.reshape((out_len,) + (1,) * (values.ndim - 1))
    return (prior_part * opening, even_part, odd_part)

def freq_taps(values):
    frames, bins_in = (values.shape[0], values.shape[1])
    paired = values.reshape((frames, bins_in // 2, 2) + values.shape[2:])
    even_part = paired[:, :, 0]
    odd_part = paired[:, :, 1]
    prior_part = jnp.concatenate([jnp.zeros_like(odd_part[:, :1]), odd_part[:, :-1]], axis=1)
    return (prior_part, even_part, odd_part)

def strided_conv(values, kernel, seg_in, seg_out):
    summed = None
    for tap_row, tap_rows in enumerate(time_taps(values, seg_in, seg_out)):
        for tap_col, tap_piece in enumerate(freq_taps(tap_rows)):
            if tap_piece.ndim == 2:
                tap_piece = tap_piece[:, :, None]
            addend = tap_piece * kernel[3 * tap_row + tap_col]
            summed = addend if summed is None else summed + addend
    present = (seg_out >= 0).astype(summed.dtype)
    return summed * present[:, None, None]

def layer_norm(values, norm_gain, norm_shift):
    average = lax.optimization_barrier(jnp.mean(values, axis=-1, keepdims=True))
    centred = values - average
    spread = lax.optimization_barrier(jnp.mean(centred * centred, axis=-1, keepdims=True))
    return centred * lax.rsqrt(spread + EPSILON) * norm_gain + norm_shift

def depth_glu(gated_rows, kernel, segments):
    model_width = gated_rows.shape[1] // 2
    merged = gated_rows[:, :model_width] * jax.nn.sigmoid(gated_rows[:, model_width:])
    radius = kernel.shape[0] // 2
    frames = gated_rows.shape[0]
    padded = jnp.pad(merged, ((radius, radius), (0, 0)))
    padded_segs = jnp.pad(segments, (radius, radius), constant_values=-2)
    summed = jnp.zeros_like(merged)
    for tap_index in range(kernel.shape[0]):
        same_segment = (padded_segs[tap_index:tap_index + frames] == segments).astype(merged.dtype)
        summed = summed + padded[tap_index:tap_index + frames] * same_segment[:, None] * kernel[tap_index]
    return summed

def exact_product(operand, matrix):
    return jnp.dot(operand, matrix, precision=lax.Precision.HIGHEST)

def linear(operand, matrix):
    return low_back(exact_product(low(operand), matrix))

def feed_forward(stream, norm_gain, norm_shift, inner_weight, outer_weight):
    normed = low(layer_norm(stream, norm_gain, norm_shift))
    hidden = low_back(exact_product(normed, inner_weight))
    return low_back(exact_product(low(jax.nn.silu(hidden)), outer_weight))

def attention_branch(stream, norm_gain, norm_shift, qkv_weight, out_weight, segments, contexts):
    frames = stream.shape[0]
    normed = low(layer_norm(stream, norm_gain, norm_shift))
    joined = low(low_back(exact_product(normed, qkv_weight)))
    model_width = joined.shape[1] // 3
    head_count = contexts.shape[0]
    shaped = joined.reshape(frames, 3, head_count, model_width // head_count)
    queries, key_rows, value_rows = (shaped[:, 0], shaped[:, 1], shaped[:, 2])
    scores = low_back(jnp.einsum('qhd,khd->hqk', queries, key_rows, precision=lax.Precision.HIGHEST))
    position = jnp.arange(frames, dtype=jnp.int32)
    distance = jnp.abs(position[:, None] - position[None, :])
    allowed = (segments[:, None] == segments[None, :])[None] & (distance[None] <= contexts[:, None, None])
    logits = jnp.where(allowed, scores * queries.shape[2] ** (-0.5), MASKED_LOGIT)
    highest = lax.optimization_barrier(jnp.max(logits, axis=-1, keepdims=True))
    exponent = jnp.exp(logits - highest)
    weights = exponent / lax.optimization_barrier(jnp.sum(exponent, axis=-1, keepdims=True))
    mixed_heads = low(low_back(jnp.einsum('hqk,khd->qhd', low(weights), value_rows, precision=lax.Precision.HIGHEST)))
    return low_back(exact_product(mixed_heads.reshape(frames, model_width), out_weight))

def front_section(params, masked, segments, contexts):
    kernels, point_weight, stem_weight, ffn_inner, ffn_outer, qkv_weight, out_weight, conv_inner, conv_taps, conv_outer, norm_rows, shift_rows, final_row = params
    seg_zero = jnp.repeat(segments, 8)
    seg_one = jnp.repeat(segments, 4)
    seg_two = jnp.repeat(segments, 2)
    level_one = jax.nn.silu(strided_conv(masked, kernels[0], seg_zero, seg_one))
    level_two = strided_conv(level_one, kernels[1], seg_one, seg_two)
    channels = level_two.shape[2]
    point_two = linear(level_two.reshape(-1, channels), point_weight[0])
    level_three = strided_conv(jax.nn.silu(point_two).reshape(level_two.shape), kernels[2], seg_two, segments)
    point_three = linear(level_three.reshape(-1, channels), point_weight[1])
    after_stem = linear(jax.nn.silu(point_three).reshape(segments.shape[0], -1), stem_weight)
    after_ffn = after_stem + 0.5 * feed_forward(after_stem, norm_rows[0], shift_rows[0], ffn_inner[0], ffn_outer[0])
    after_attn = after_ffn + attention_branch(after_ffn, norm_rows[1], shift_rows[1], qkv_weight, out_weight, segments, contexts)
    gated_rows = low_back(exact_product(low(layer_norm(after_attn, norm_rows[2], shift_rows[2])), conv_inner))
    return (after_attn, depth_glu(gated_rows, conv_taps, segments))

def back_section(params, after_attn, depthwise, segments, average, inv_spread):
    kernels, point_weight, stem_weight, ffn_inner, ffn_outer, qkv_weight, out_weight, conv_inner, conv_taps, conv_outer, norm_rows, shift_rows, final_row = params
    present = (segments >= 0).astype(after_attn.dtype)[:, None]
    batch_normed = (depthwise - average) * inv_spread * norm_rows[3] + shift_rows[3]
    after_conv = after_attn + low_back(exact_product(low(jax.nn.silu(batch_normed)), conv_outer))
    after_second = after_conv + 0.5 * feed_forward(after_conv, norm_rows[4], shift_rows[4], ffn_inner[1], ffn_outer[1])
    return layer_norm(after_second, norm_rows[5], final_row) * present

def forward(params, mel_blocks, keep_table, segment_table, contexts, counted):
    front_step = jax.checkpoint(lambda entries: front_section(params, entries[0] * entries[1], entries[2], contexts))
    after_attn, depthwise = lax.map(front_step, (mel_blocks, keep_table, segment_table))
    present = (segment_table >= 0).astype(depthwise.dtype)[:, :, None]
    average = lax.optimization_barrier(jnp.sum(depthwise * present, axis=(0, 1))) / counted
    spread = lax.optimization_barrier(jnp.sum(depthwise * depthwise * present, axis=(0, 1))) / counted - average * average
    inv_spread = lax.rsqrt(spread + EPSILON)
    back_step = jax.checkpoint(lambda entries: back_section(params, entries[0], entries[1], entries[2], average, inv_spread))
    outputs = lax.map(back_step, (after_attn, depthwise, segment_table))
    return outputs.reshape(-1, outputs.shape[2])

def reference(mel, cotangent, lengths, assignment, time_spans, freq_spans, contexts, stem_kernels, stem_point, stem_out, ffn_in, ffn_out, qkv, attn_out, conv_in, conv_depth, conv_out, norm_gains, norm_shifts, final_shift):
    devices = N_DP * N_FSDP
    device_ids = jnp.arange(devices, dtype=jnp.int32)
    segment_table = jax.vmap(lambda device: frame_segments(lengths, assignment, device, TOK_DEV))(device_ids)
    keep_table = jax.vmap(lambda segments, spans_time, spans_freq: feature_keep(segments, spans_time, spans_freq, MEL))(segment_table, time_spans, freq_spans)
    counted = jnp.sum(lengths).astype(jnp.float32)
    params = (stem_kernels.astype(jnp.float32), stem_point.astype(jnp.float32), stem_out.astype(jnp.float32), ffn_in.astype(jnp.float32), ffn_out.astype(jnp.float32), qkv.astype(jnp.float32), attn_out.astype(jnp.float32), conv_in.astype(jnp.float32), conv_depth.astype(jnp.float32), conv_out.astype(jnp.float32), norm_gains.astype(jnp.float32), norm_shifts.astype(jnp.float32), final_shift.astype(jnp.float32))
    mel_blocks = mel.astype(jnp.float32).reshape(devices, 8 * TOK_DEV, MEL)
    outputs, pullback = jax.vjp(lambda weights, blocks: forward(weights, blocks, keep_table, segment_table, contexts, counted), params, mel_blocks)
    weight_grads, mel_grad = pullback(cotangent.astype(jnp.float32))
    return (outputs.astype(jnp.bfloat16), mel_grad.reshape(-1, MEL), weight_grads[0], weight_grads[1], weight_grads[2], weight_grads[3], weight_grads[4], weight_grads[5], weight_grads[6], weight_grads[7], weight_grads[8], weight_grads[9], weight_grads[10], weight_grads[11], weight_grads[12])
```

```python
import functools

import jax
import jax.numpy as jnp
from jax import lax
from jax.experimental import pallas as pl
from jax.experimental.pallas import tpu as pltpu
from jax.sharding import PartitionSpec as P

MESH = pl.DeviceIdType.MESH
CORES = 2


def grid_sizes():
    dp, fsdp = lax.axis_size("dp"), lax.axis_size("fsdp")
    high = 2 if dp % 2 == 0 else 1
    return (high, dp // high, fsdp // CORES, CORES)


def own_place(sizes):
    dp, fsdp = lax.axis_index("dp"), lax.axis_index("fsdp")
    return (dp // sizes[1], dp % sizes[1], fsdp // CORES, fsdp % CORES)


def peer_on(place, sizes, digit, step):
    other = list(place)
    other[digit] = (place[digit] + step) % sizes[digit]
    return tuple(other)


def device_of(place, sizes):
    return (place[0] * sizes[1] + place[1], place[2] * CORES + place[3])


def greet(place, sizes):
    barrier = pltpu.get_barrier_semaphore()
    met = 0
    for digit in range(4):
        for step in range(1, sizes[digit]):
            other = peer_on(place, sizes, digit, step)
            pl.semaphore_signal(
                barrier, inc=1, device_id=device_of(other, sizes), device_id_type=MESH
            )
            met += 1
    pl.semaphore_wait(barrier, met)


def send(src, dst, sizes, other, send_sem, recv_sem):
    copy = pltpu.make_async_remote_copy(
        src_ref=src,
        dst_ref=dst,
        send_sem=send_sem,
        recv_sem=recv_sem,
        device_id=device_of(other, sizes),
        device_id_type=MESH,
    )
    copy.start()
    return copy


def gather_kernel(sizes, *refs):
    count = (len(refs) - 6) // 2
    sources, gathered = refs[:count], refs[count : 2 * count]
    local_sem, z_send, z_recv, hop_send, hop_recv, core_sem = refs[2 * count :]
    place = own_place(sizes)
    a, b, z, c = place
    greet(place, sizes)
    pending = []

    def stage_z(i):
        own = gathered[i].at[a, b, z, c]
        keep = pltpu.make_async_copy(sources[i], own, local_sem.at[i])
        keep.start()
        copies = [
            send(
                sources[i],
                own,
                sizes,
                peer_on(place, sizes, 2, step),
                z_send.at[i, step - 1],
                z_recv.at[i, step - 1],
            )
            for step in range(1, sizes[2])
        ]
        return keep, copies

    def stage_hop(i, hop, digit, part):
        return [
            send(
                part,
                part,
                sizes,
                peer_on(place, sizes, digit, step),
                hop_send.at[i, hop, step - 1],
                hop_recv.at[i, hop, step - 1],
            )
            for step in range(1, sizes[digit])
        ]

    def finish(copies):
        for copy in copies:
            copy.wait_recv()
        pending.extend(copies)

    opened = [stage_z(i) for i in range(count)]
    first, second, third = {}, {}, {}
    for turn in range(count + 3):
        if turn < count:
            i = turn
            opened[i][0].wait()
            finish(opened[i][1])
            first[i] = stage_hop(i, 0, 1 - i % 2, gathered[i].at[a, b, :, c])
        i = turn - 1
        if 0 <= i < count:
            finish(first[i])
            part = gathered[i].at[:, b, :, c] if i % 2 else gathered[i].at[a, :, :, c]
            second[i] = stage_hop(i, 1, i % 2, part)
        i = turn - 2
        if 0 <= i < count:
            finish(second[i])
            part = gathered[i].at[:, :, :, c]
            third[i] = [
                send(
                    part,
                    part,
                    sizes,
                    peer_on(place, sizes, 3, 1),
                    core_sem.at[i, 0],
                    core_sem.at[i, 1],
                )
            ]
        i = turn - 3
        if 0 <= i < count:
            finish(third[i])
    for copy in pending:
        copy.wait_send()


def gather_all(shards):
    sizes = grid_sizes()
    count = len(shards)
    steps = max(1, sizes[2] - 1)
    wide = max(1, sizes[0] - 1, sizes[1] - 1)
    dma = pltpu.SemaphoreType.DMA
    return pl.pallas_call(
        functools.partial(gather_kernel, sizes),
        out_shape=[jax.ShapeDtypeStruct(sizes + s.shape, s.dtype) for s in shards],
        in_specs=[pl.BlockSpec(memory_space=pl.ANY)] * count,
        out_specs=[pl.BlockSpec(memory_space=pl.ANY)] * count,
        scratch_shapes=[
            dma((count,)),
            dma((count, steps)),
            dma((count, steps)),
            dma((count, 2, wide)),
            dma((count, 2, wide)),
            dma((count, 2)),
        ],
        compiler_params=pltpu.CompilerParams(collective_id=0, has_side_effects=True),
        name="gather_weights",
    )(*shards)


def scatter_kernel(sizes, *refs):
    count = (len(refs) - 6) // 7
    parts, owned = refs[:count], refs[count : 2 * count]
    held, land_c, land_one, land_two, land_z = (
        refs[(2 + j) * count : (3 + j) * count] for j in range(5)
    )
    core_sem, hop_send, hop_recv, z_send, z_recv, local_sem = refs[7 * count :]
    place = own_place(sizes)
    a, b, z, c = place
    greet(place, sizes)
    pending = []

    def finish(copies):
        for copy in copies:
            copy.wait_recv()
        pending.extend(copies)

    def add_rows(total, pieces):
        lead = total.shape[:-2]
        steps = 1
        for extent in lead:
            steps *= extent

        def body(at, carry):
            index = []
            rest = at
            for extent in reversed(lead):
                index.append(rest % extent)
                rest = rest // extent
            index = tuple(reversed(index))
            value = total[index].astype(jnp.float32)
            for piece in pieces:
                value = value + piece[index].astype(jnp.float32)
            total[index] = value.astype(total.dtype)
            return carry

        lax.fori_loop(0, steps, body, 0)

    core_copies, keeps = [], []
    for i in range(count):
        core_copies.append(
            [
                send(
                    parts[i].at[:, :, :, 1 - c],
                    land_c[i],
                    sizes,
                    peer_on(place, sizes, 3, 1),
                    core_sem.at[i, 0],
                    core_sem.at[i, 1],
                )
            ]
        )
        keep = pltpu.make_async_copy(parts[i].at[:, :, :, c], held[i], local_sem.at[i])
        keep.start()
        keeps.append(keep)

    def view(ref, digit, value):
        return ref.at[value] if digit == 0 else ref.at[:, value]

    def stage_hop(i, hop, digit, ref, axis, land):
        copies = []
        for step in range(1, sizes[digit]):
            other = peer_on(place, sizes, digit, step)
            copies.append(
                send(
                    view(ref, axis, other[digit]),
                    land.at[step - 1],
                    sizes,
                    other,
                    hop_send.at[i, hop, step - 1],
                    hop_recv.at[i, hop, step - 1],
                )
            )
        return copies

    first, second, third = {}, {}, {}
    for turn in range(count + 3):
        if turn < count:
            i = turn
            keeps[i].wait()
            finish(core_copies[i])
            add_rows(held[i], [land_c[i]])
            first[i] = stage_hop(i, 0, 1 - i % 2, held[i], 1 - i % 2, land_one[i])
        i = turn - 1
        if 0 <= i < count:
            digit = 1 - i % 2
            finish(first[i])
            mine = view(held[i], digit, place[digit])
            add_rows(mine, [land_one[i].at[s] for s in range(sizes[digit] - 1)])
            second[i] = stage_hop(i, 1, 1 - digit, mine, 0, land_two[i])
        i = turn - 2
        if 0 <= i < count:
            digit = 1 - i % 2
            finish(second[i])
            mine = view(held[i], digit, place[digit]).at[place[1 - digit]]
            add_rows(mine, [land_two[i].at[s] for s in range(sizes[1 - digit] - 1)])
            third[i] = []
            for step in range(1, sizes[2]):
                other = peer_on(place, sizes, 2, step)
                third[i].append(
                    send(
                        mine.at[other[2]],
                        land_z[i].at[step - 1],
                        sizes,
                        other,
                        z_send.at[i, step - 1],
                        z_recv.at[i, step - 1],
                    )
                )
        i = turn - 3
        if 0 <= i < count:
            finish(third[i])
            total = held[i][a, b, z].astype(jnp.float32)
            for step in range(1, sizes[2]):
                total = total + land_z[i][step - 1].astype(jnp.float32)
            owned[i][...] = total
    for copy in pending:
        copy.wait_send()


def scatter_all(parts):
    sizes = grid_sizes()
    count = len(parts)
    steps = max(1, sizes[2] - 1)
    wide = max(1, sizes[0] - 1, sizes[1] - 1)
    dma = pltpu.SemaphoreType.DMA
    blocks = [p.shape[4:] for p in parts]
    lands = [[], [], [], [], []]
    for i, block in enumerate(blocks):
        digit = 1 - i % 2
        other = sizes[1 - digit]
        lands[0].append(pltpu.VMEM(sizes[:3] + block, jnp.bfloat16))
        lands[1].append(pltpu.VMEM(sizes[:3] + block, jnp.bfloat16))
        lands[2].append(
            pltpu.VMEM((max(1, sizes[digit] - 1), other, sizes[2]) + block, jnp.bfloat16)
        )
        lands[3].append(pltpu.VMEM((max(1, other - 1), sizes[2]) + block, jnp.bfloat16))
        lands[4].append(pltpu.VMEM((steps,) + block, jnp.bfloat16))
    return pl.pallas_call(
        functools.partial(scatter_kernel, sizes),
        out_shape=[jax.ShapeDtypeStruct(block, jnp.float32) for block in blocks],
        in_specs=[pl.BlockSpec(memory_space=pl.ANY)] * count,
        out_specs=[pl.BlockSpec(memory_space=pltpu.VMEM)] * count,
        scratch_shapes=lands[0]
        + lands[1]
        + lands[2]
        + lands[3]
        + lands[4]
        + [
            dma((count, 2)),
            dma((count, 2, wide)),
            dma((count, 2, wide)),
            dma((count, steps)),
            dma((count, steps)),
            dma((count,)),
        ],
        compiler_params=pltpu.CompilerParams(
            collective_id=1, has_side_effects=True, vmem_limit_bytes=56 * 2**20
        ),
        name="scatter_grads",
    )(*parts)


def total_kernel(sizes, value_ref, total_ref, *rest):
    lands, (send_sem, recv_sem) = rest[:4], rest[4:]
    place = own_place(sizes)
    greet(place, sizes)
    total_ref[...] = value_ref[...]
    for stage, digit in enumerate((3, 2, 1, 0)):
        if sizes[digit] == 1:
            continue
        copies = [
            send(
                total_ref,
                lands[stage].at[step - 1],
                sizes,
                peer_on(place, sizes, digit, step),
                send_sem.at[stage, step - 1],
                recv_sem.at[stage, step - 1],
            )
            for step in range(1, sizes[digit])
        ]
        for copy in copies:
            copy.wait()
        total = total_ref[...]
        for step in range(1, sizes[digit]):
            total = total + lands[stage][step - 1]
        total_ref[...] = total


def total_of(values, ident):
    sizes = grid_sizes()
    dma = pltpu.SemaphoreType.DMA
    return pl.pallas_call(
        functools.partial(total_kernel, sizes),
        out_shape=jax.ShapeDtypeStruct(values.shape, jnp.float32),
        in_specs=[pl.BlockSpec(memory_space=pltpu.VMEM)],
        out_specs=pl.BlockSpec(memory_space=pltpu.VMEM),
        scratch_shapes=[
            pltpu.VMEM((max(1, sizes[digit] - 1),) + values.shape, jnp.float32)
            for digit in (3, 2, 1, 0)
        ]
        + [dma((4, max(sizes))), dma((4, max(sizes)))],
        compiler_params=pltpu.CompilerParams(collective_id=ident, has_side_effects=True),
        name=f"total_{ident}",
    )(values)


CTX = 128


EPSILON = 1e-05
MASKED_LOGIT = -1e30


def frame_segments(lengths, assignment, device, frames):
    belongs = assignment == device
    own_sizes = jnp.where(belongs, lengths, 0)
    finishes = jnp.cumsum(own_sizes, dtype=jnp.int32)
    beginnings = finishes - own_sizes
    position = jnp.arange(frames, dtype=jnp.int32)[:, None]
    inside = belongs[None, :] & (position >= beginnings[None, :]) & (position < finishes[None, :])
    number = jnp.arange(lengths.shape[0], dtype=jnp.int32)[None, :] + 1
    return jnp.sum(jnp.where(inside, number, 0), axis=1, dtype=jnp.int32) - 1


def feature_keep(segments, time_spans, freq_spans, mel_bins):
    frames = segments.shape[0] * 8
    position = jnp.arange(frames, dtype=jnp.int32)[:, None]
    covered = (position >= time_spans[None, :, 0]) & (
        position < time_spans[None, :, 0] + time_spans[None, :, 1]
    )
    time_keep = jnp.repeat(segments >= 0, 8) & jnp.logical_not(jnp.any(covered, axis=1))
    channel = jnp.arange(mel_bins, dtype=jnp.int32)[:, None]
    banned = (channel >= freq_spans[None, :, 0]) & (
        channel < freq_spans[None, :, 0] + freq_spans[None, :, 1]
    )
    freq_keep = jnp.logical_not(jnp.any(banned, axis=1))
    return (time_keep[:, None] & freq_keep[None, :]).astype(jnp.float32)


def time_taps(values, seg_in, seg_out):
    out_len = seg_out.shape[0]
    paired = values.reshape((out_len, 2) + values.shape[1:])
    even_part = paired[:, 0]
    odd_part = paired[:, 1]
    prior_part = jnp.concatenate([jnp.zeros_like(odd_part[:1]), odd_part[:-1]], axis=0)
    seg_pairs = seg_in.reshape(out_len, 2)
    prior_segs = jnp.concatenate([jnp.full((1,), -2, jnp.int32), seg_pairs[:-1, 1]])
    opening = ((prior_segs == seg_out) & (seg_out >= 0)).astype(values.dtype)
    opening = opening.reshape((out_len,) + (1,) * (values.ndim - 1))
    return (prior_part * opening, even_part, odd_part)


def freq_taps(values):
    frames, bins_in = (values.shape[0], values.shape[1])
    paired = values.reshape((frames, bins_in // 2, 2) + values.shape[2:])
    even_part = paired[:, :, 0]
    odd_part = paired[:, :, 1]
    prior_part = jnp.concatenate([jnp.zeros_like(odd_part[:, :1]), odd_part[:, :-1]], axis=1)
    return (prior_part, even_part, odd_part)


def strided_conv(values, kernel, seg_in, seg_out):
    summed = None
    for tap_row, tap_rows in enumerate(time_taps(values, seg_in, seg_out)):
        for tap_col, tap_piece in enumerate(freq_taps(tap_rows)):
            if tap_piece.ndim == 2:
                tap_piece = tap_piece[:, :, None]
            addend = tap_piece * kernel[3 * tap_row + tap_col]
            summed = addend if summed is None else summed + addend
    present = (seg_out >= 0).astype(summed.dtype)
    return summed * present[:, None, None]


def layer_norm(values, norm_gain, norm_shift):
    average = jnp.mean(values, axis=-1, keepdims=True)
    centred = values - average
    spread = jnp.mean(centred * centred, axis=-1, keepdims=True)
    return centred * lax.rsqrt(spread + EPSILON) * norm_gain + norm_shift


def depth_glu(gated_rows, kernel, segments):
    model_width = gated_rows.shape[1] // 2
    merged = gated_rows[:, :model_width] * jax.nn.sigmoid(gated_rows[:, model_width:])
    radius = kernel.shape[0] // 2
    frames = gated_rows.shape[0]
    padded = jnp.pad(merged, ((radius, radius), (0, 0)))
    padded_segs = jnp.pad(segments, (radius, radius), constant_values=-2)
    summed = jnp.zeros_like(merged)
    for tap_index in range(kernel.shape[0]):
        same_segment = (padded_segs[tap_index : tap_index + frames] == segments).astype(
            merged.dtype
        )
        summed = (
            summed
            + padded[tap_index : tap_index + frames] * same_segment[:, None] * kernel[tap_index]
        )
    return summed


def stem_front(masked, first_kernel, second_kernel, segments):
    seg_zero = jnp.repeat(segments, 8)
    seg_one = jnp.repeat(segments, 4)
    seg_two = jnp.repeat(segments, 2)
    level_one = jax.nn.silu(strided_conv(masked, first_kernel, seg_zero, seg_one))
    return strided_conv(level_one, second_kernel, seg_one, seg_two)


def stem_middle(point_two, third_kernel, segments):
    frames = segments.shape[0]
    channels = point_two.shape[1]
    hidden = jax.nn.silu(point_two).reshape(frames * 2, -1, channels)
    return strided_conv(hidden, third_kernel, jnp.repeat(segments, 2), segments)


def matmul(operand, matrix):
    return jnp.dot(operand, matrix, preferred_element_type=jnp.float32)


def over_rows(operand, matrix):
    return lax.dot_general(
        operand, matrix, (((0,), (0,)), ((), ())), preferred_element_type=jnp.float32
    )


def against(operand, matrix):
    return lax.dot_general(
        operand, matrix, (((1,), (1,)), ((), ())), preferred_element_type=jnp.float32
    )


def ffn_forward(stream, norm_gain, norm_shift, inner_weight, outer_weight):
    normed = layer_norm(stream, norm_gain, norm_shift).astype(jnp.bfloat16)
    hidden = matmul(normed, inner_weight)
    active = jax.nn.silu(hidden).astype(jnp.bfloat16)
    return (matmul(active, outer_weight), (normed, hidden, active))


def ffn_backward(stream, norm_gain, norm_shift, inner_weight, outer_weight, kept_values, grad_out):
    normed, hidden, active = kept_values
    grad_outer = over_rows(active, grad_out)
    grad_active = against(grad_out, outer_weight)
    grad_hidden = jax.vjp(jax.nn.silu, hidden)[1](grad_active)[0].astype(jnp.bfloat16)
    grad_inner = over_rows(normed, grad_hidden)
    grad_normed = against(grad_hidden, inner_weight)
    pullback = jax.vjp(layer_norm, stream, norm_gain, norm_shift)[1]
    grad_stream, grad_gain, grad_shift = pullback(grad_normed)
    return (grad_stream, grad_gain, grad_shift, grad_inner, grad_outer)


def split_heads(joined, head_count):
    frames = joined.shape[0]
    model_width = joined.shape[1] // 3
    shaped = joined.reshape(frames, 3, head_count, model_width // head_count)
    return (shaped[:, 0], shaped[:, 1], shaped[:, 2])


def block_logits(queries, key_rows, query_segs, key_segs, anchor, frames, contexts):
    scores = jnp.einsum("qhd,khd->hqk", queries, key_rows, preferred_element_type=jnp.float32)
    radius = (key_rows.shape[0] - queries.shape[0]) // 2
    query_pos = anchor + jnp.arange(queries.shape[0], dtype=jnp.int32)
    key_pos = anchor - radius + jnp.arange(key_rows.shape[0], dtype=jnp.int32)
    distance = jnp.abs(query_pos[:, None] - key_pos[None, :])
    allowed = (
        (query_segs[:, None] == key_segs[None, :])
        & (key_pos[None, :] >= 0)
        & (key_pos[None, :] < frames)
    )
    allowed = allowed[None] & (distance[None] <= contexts[:, None, None])
    return jnp.where(allowed, scores * queries.shape[2] ** (-0.5), MASKED_LOGIT)


def attend_forward(joined, segments, contexts):
    frames = joined.shape[0]
    queries, key_rows, value_rows = split_heads(joined, contexts.shape[0])
    padded_keys = jnp.pad(key_rows, ((CTX, CTX), (0, 0), (0, 0)))
    padded_values = jnp.pad(value_rows, ((CTX, CTX), (0, 0), (0, 0)))
    padded_segs = jnp.pad(segments, (CTX, CTX), constant_values=-2)
    logits = block_logits(queries, padded_keys, segments, padded_segs, 0, frames, contexts)
    highest = jnp.max(logits, axis=-1, keepdims=True)
    exponent = jnp.exp(logits - highest)
    summed = jnp.sum(exponent, axis=-1, keepdims=True)
    weights = (exponent / summed).astype(jnp.bfloat16)
    outputs = jnp.einsum("hqk,khd->qhd", weights, padded_values, preferred_element_type=jnp.float32)
    log_parts = highest[:, :, 0] + jnp.log(summed[:, :, 0])
    return (outputs, log_parts)


def attend_backward(joined, segments, contexts, log_totals, grad_mixed):
    frames = joined.shape[0]
    queries, key_rows, value_rows = split_heads(joined, contexts.shape[0])
    padded_keys = jnp.pad(key_rows, ((CTX, CTX), (0, 0), (0, 0)))
    padded_values = jnp.pad(value_rows, ((CTX, CTX), (0, 0), (0, 0)))
    padded_segs = jnp.pad(segments, (CTX, CTX), constant_values=-2)
    block_rows = min(frames, 512)
    grad_keys = jnp.zeros(padded_keys.shape, jnp.float32)
    grad_values = jnp.zeros(padded_values.shape, jnp.float32)
    query_span = slice(0, block_rows)
    key_span = slice(0, block_rows + 2 * CTX)
    logits = block_logits(queries, padded_keys, segments, padded_segs, 0, frames, contexts)
    weights = jnp.exp(logits - log_totals[:, query_span, None])
    grad_weights = jnp.einsum(
        "qhd,khd->hqk", grad_mixed, padded_values, preferred_element_type=jnp.float32
    )
    row_dot = jnp.sum(weights * grad_weights, axis=-1, keepdims=True)
    grad_scores = (weights * (grad_weights - row_dot) * queries.shape[2] ** (-0.5)).astype(
        jnp.bfloat16
    )
    grad_queries = jnp.einsum(
        "hqk,khd->qhd", grad_scores, padded_keys, preferred_element_type=jnp.float32
    )
    grad_keys = grad_keys.at[key_span].add(
        jnp.einsum("hqk,qhd->khd", grad_scores, queries, preferred_element_type=jnp.float32)
    )
    grad_values = grad_values.at[key_span].add(
        jnp.einsum(
            "hqk,qhd->khd",
            weights.astype(jnp.bfloat16),
            grad_mixed,
            preferred_element_type=jnp.float32,
        )
    )
    stacked = jnp.stack(
        [grad_queries, grad_keys[CTX : CTX + frames], grad_values[CTX : CTX + frames]], axis=1
    )
    return stacked.reshape(frames, -1)


def local(
    mel,
    cotangent,
    lengths,
    assignment,
    time_spans,
    freq_spans,
    contexts,
    stem_kernels,
    stem_point,
    stem_out,
    ffn_in,
    ffn_out,
    qkv,
    attn_out,
    conv_in,
    conv_depth,
    conv_out,
    norm_gains,
    norm_shifts,
    final_shift,
):
    device = lax.axis_index("dp") * lax.axis_size("fsdp") + lax.axis_index("fsdp")
    frames = cotangent.shape[0]
    segments = frame_segments(lengths, assignment, device, frames)
    feature_mask = feature_keep(segments, time_spans[0], freq_spans[0], mel.shape[1])
    present = (segments >= 0).astype(jnp.float32)[:, None]
    counted = jnp.sum(lengths).astype(jnp.float32)
    small = jnp.concatenate(
        [
            part.astype(jnp.float32).reshape(-1)
            for part in (stem_kernels, conv_depth, norm_gains, norm_shifts, final_shift)
        ]
    )
    small = jnp.pad(small, (0, 1024 - small.shape[0])).reshape(8, 128)
    bulk = gather_all(
        [
            small,
            stem_point.astype(jnp.float32),
            stem_out,
            ffn_in[0],
            ffn_out[0],
            qkv,
            attn_out,
            conv_in,
            conv_out,
            ffn_in[1],
            ffn_out[1],
        ]
    )
    devices = lax.axis_size("dp") * lax.axis_size("fsdp")
    flat = bulk[0].reshape(devices, 1024)
    taken = 0

    def spread(like):
        nonlocal taken
        size = like.size
        piece = flat[:, taken : taken + size].reshape((devices,) + like.shape)
        taken += size
        piece = jnp.moveaxis(piece, 0, -2)
        return piece.reshape(like.shape[:-1] + (devices * like.shape[-1],))

    kernels = spread(stem_kernels)
    conv_taps = spread(conv_depth)
    norm_rows = spread(norm_gains)
    shift_rows = spread(norm_shifts)
    final_row = spread(final_shift)
    point_weight = jnp.moveaxis(bulk[1].reshape((devices,) + stem_point.shape), 0, 1)
    point_weight = point_weight.reshape(2, -1, stem_point.shape[2]).astype(jnp.bfloat16)

    def rows_of(value):
        return value.reshape(-1, value.shape[-1])

    stem_weight = rows_of(bulk[2])
    ffn_inner = (rows_of(bulk[3]), rows_of(bulk[9]))
    ffn_outer = (rows_of(bulk[4]), rows_of(bulk[10]))
    qkv_weight = rows_of(bulk[5])
    out_weight = rows_of(bulk[6])
    conv_inner = rows_of(bulk[7])
    conv_outer = rows_of(bulk[8])
    kernels_wide = kernels.astype(jnp.float32)
    gains_wide = norm_rows.astype(jnp.float32)
    shifts_wide = shift_rows.astype(jnp.float32)
    final_wide = final_row.astype(jnp.float32)
    masked = mel.astype(jnp.float32) * feature_mask
    level_two, front_pullback = jax.vjp(
        lambda masked_input, first_taps, second_taps: stem_front(
            masked_input, first_taps, second_taps, segments
        ),
        masked,
        kernels_wide[0],
        kernels_wide[1],
    )
    channels = level_two.shape[2]
    level_two_low = level_two.reshape(-1, channels).astype(jnp.bfloat16)
    point_two = matmul(level_two_low, point_weight[0])
    level_three, middle_pullback = jax.vjp(
        lambda point_input, third_taps: stem_middle(point_input, third_taps, segments),
        point_two,
        kernels_wide[2],
    )
    level_three_low = level_three.reshape(-1, channels).astype(jnp.bfloat16)
    point_three = matmul(level_three_low, point_weight[1])
    stem_hidden = jax.nn.silu(point_three).reshape(frames, -1).astype(jnp.bfloat16)
    after_stem = matmul(stem_hidden, stem_weight)
    ffn_result_one, ffn_kept_one = ffn_forward(
        after_stem, gains_wide[0], shifts_wide[0], ffn_inner[0], ffn_outer[0]
    )
    after_ffn = after_stem + 0.5 * ffn_result_one
    attn_normed = layer_norm(after_ffn, gains_wide[1], shifts_wide[1]).astype(jnp.bfloat16)
    joined = matmul(attn_normed, qkv_weight).astype(jnp.bfloat16)
    mixed_heads, log_totals = attend_forward(joined, segments, contexts)
    mixed_low = mixed_heads.reshape(frames, -1).astype(jnp.bfloat16)
    after_attn = after_ffn + matmul(mixed_low, out_weight)
    conv_normed = layer_norm(after_attn, gains_wide[2], shifts_wide[2]).astype(jnp.bfloat16)
    gated_rows = matmul(conv_normed, conv_inner)
    taps_wide = conv_taps.astype(jnp.float32)
    depthwise, depth_pullback = jax.vjp(
        lambda gate_input, taps_input: depth_glu(gate_input, taps_input, segments),
        gated_rows,
        taps_wide,
    )
    first_sum, second_sum = total_of(
        jnp.stack(
            [jnp.sum(depthwise * present, axis=0), jnp.sum(depthwise * depthwise * present, axis=0)]
        ),
        2,
    )
    average = first_sum / counted
    spread = second_sum / counted - average * average
    inv_spread = lax.rsqrt(spread + EPSILON)
    standard = (depthwise - average) * inv_spread
    batch_normed = standard * gains_wide[3] + shifts_wide[3]
    conv_active = jax.nn.silu(batch_normed).astype(jnp.bfloat16)
    after_conv = after_attn + matmul(conv_active, conv_outer)
    ffn_result_two, ffn_kept_two = ffn_forward(
        after_conv, gains_wide[4], shifts_wide[4], ffn_inner[1], ffn_outer[1]
    )
    after_second = after_conv + 0.5 * ffn_result_two
    activations = (layer_norm(after_second, gains_wide[5], final_wide) * present).astype(
        jnp.bfloat16
    )
    back_point, back_stem, back_inner, back_outer = point_weight, stem_weight, ffn_inner, ffn_outer
    back_qkv, back_attn, back_conv_in, back_conv_out = qkv_weight, out_weight, conv_inner, conv_outer
    back_gains, back_shifts, back_final = norm_rows, shift_rows, final_row
    back_gains_wide = back_gains.astype(jnp.float32)
    back_shifts_wide = back_shifts.astype(jnp.float32)
    back_final_wide = back_final.astype(jnp.float32)
    grad_final = cotangent.astype(jnp.float32) * present
    pullback = jax.vjp(layer_norm, after_second, back_gains_wide[5], back_final_wide)[1]
    grad_stream, grad_gain_final, grad_shift_final = pullback(grad_final)
    ffn_two = ffn_backward(
        after_conv,
        back_gains_wide[4],
        back_shifts_wide[4],
        back_inner[1],
        back_outer[1],
        ffn_kept_two,
        (0.5 * grad_stream).astype(jnp.bfloat16),
    )
    grad_stream = grad_stream + ffn_two[0]
    grad_conv_low = grad_stream.astype(jnp.bfloat16)
    grad_conv_out = over_rows(conv_active, grad_conv_low)
    grad_active = against(grad_conv_low, back_conv_out)
    grad_batch = jax.vjp(jax.nn.silu, batch_normed)[1](grad_active)[0]
    beta_sum, gamma_sum = total_of(
        jnp.stack(
            [
                jnp.sum(grad_batch * present, axis=0),
                jnp.sum(grad_batch * standard * present, axis=0),
            ]
        ),
        3,
    )
    bn_gain = back_gains_wide[3]
    grad_first = (
        inv_spread * inv_spread * bn_gain * gamma_sum * average - inv_spread * bn_gain * beta_sum
    ) / counted
    grad_second = -0.5 * inv_spread * inv_spread * bn_gain * gamma_sum / counted
    grad_depth = bn_gain * inv_spread * grad_batch + present * (
        grad_first + 2.0 * depthwise * grad_second
    )
    grad_gated, grad_taps = depth_pullback(grad_depth)
    grad_gated_low = grad_gated.astype(jnp.bfloat16)
    grad_conv_in = over_rows(conv_normed, grad_gated_low)
    pullback = jax.vjp(layer_norm, after_attn, back_gains_wide[2], back_shifts_wide[2])[1]
    conv_norm_grads = pullback(against(grad_gated_low, back_conv_in))
    grad_stream = grad_stream + conv_norm_grads[0]
    grad_attn_low = grad_stream.astype(jnp.bfloat16)
    grad_attn_out = over_rows(mixed_low, grad_attn_low)
    grad_mixed = against(grad_attn_low, back_attn).astype(jnp.bfloat16).reshape(mixed_heads.shape)
    grad_joined = attend_backward(joined, segments, contexts, log_totals, grad_mixed).astype(
        jnp.bfloat16
    )
    grad_qkv = over_rows(attn_normed, grad_joined)
    pullback = jax.vjp(layer_norm, after_ffn, back_gains_wide[1], back_shifts_wide[1])[1]
    attn_norm_grads = pullback(against(grad_joined, back_qkv))
    grad_stream = grad_stream + attn_norm_grads[0]
    ffn_one = ffn_backward(
        after_stem,
        back_gains_wide[0],
        back_shifts_wide[0],
        back_inner[0],
        back_outer[0],
        ffn_kept_one,
        (0.5 * grad_stream).astype(jnp.bfloat16),
    )
    grad_stream = grad_stream + ffn_one[0]
    grad_stem_low = grad_stream.astype(jnp.bfloat16)
    grad_stem_out = over_rows(stem_hidden, grad_stem_low)
    grad_hidden = against(grad_stem_low, back_stem).reshape(point_three.shape)
    grad_point_three = jax.vjp(jax.nn.silu, point_three)[1](grad_hidden)[0].astype(jnp.bfloat16)
    grad_third_point = over_rows(level_three_low, grad_point_three)
    grad_level_three = against(grad_point_three, back_point[1]).reshape(level_three.shape)
    grad_point_two, grad_third_kernel = middle_pullback(grad_level_three)
    grad_point_two_low = grad_point_two.astype(jnp.bfloat16)
    grad_second_point = over_rows(level_two_low, grad_point_two_low)
    grad_level_two = against(grad_point_two_low, back_point[0]).reshape(level_two.shape)
    grad_masked, grad_first_kernel, grad_second_kernel = front_pullback(grad_level_two)
    mel_grad = grad_masked * feature_mask
    zero_row = jnp.zeros_like(grad_gain_final)
    grad_gains = jnp.stack(
        [ffn_one[1], attn_norm_grads[1], conv_norm_grads[1], zero_row, ffn_two[1], grad_gain_final]
    )
    grad_shifts = jnp.stack(
        [ffn_one[2], attn_norm_grads[2], conv_norm_grads[2], zero_row, ffn_two[2]]
    )
    grad_kernels = jnp.stack([grad_first_kernel, grad_second_kernel, grad_third_kernel])
    grad_points = jnp.stack([grad_second_point, grad_third_point])
    sizes = grid_sizes()

    def blocks_of(value):
        rows = value.shape[0] // devices
        return value.astype(jnp.bfloat16).reshape(sizes + (rows, value.shape[1]))

    points_low = grad_points.astype(jnp.bfloat16).reshape(2, devices, -1, channels)
    points_low = jnp.moveaxis(points_low, 0, 1).reshape(sizes + (-1, channels))
    owned = scatter_all(
        [
            blocks_of(ffn_two[3]),
            blocks_of(ffn_two[4]),
            blocks_of(grad_conv_out),
            blocks_of(grad_conv_in),
            blocks_of(grad_attn_out),
            blocks_of(grad_qkv),
            blocks_of(ffn_one[3]),
            blocks_of(ffn_one[4]),
            blocks_of(grad_stem_out),
            points_low,
        ]
    )
    pieces = [
        grad_kernels.reshape(-1),
        grad_taps.reshape(-1),
        grad_gains.reshape(-1),
        grad_shifts.reshape(-1),
        grad_shift_final.reshape(-1),
    ]
    joined_small = jnp.concatenate(pieces)
    extra = -joined_small.shape[0] % 4096
    summed_small = total_of(jnp.pad(joined_small, (0, extra)).reshape(-1, 512), 4).reshape(-1)
    taken = 0

    def own_share(like):
        nonlocal taken
        size = like.size
        piece = summed_small[taken : taken + size].reshape(like.shape)
        taken += size
        width = like.shape[-1] // devices
        return lax.dynamic_slice_in_dim(piece, device * width, width, axis=like.ndim - 1)

    own_kernels = own_share(grad_kernels)
    own_taps = own_share(grad_taps)
    own_gains = own_share(grad_gains)
    own_shifts = own_share(grad_shifts)
    own_final = own_share(grad_shift_final)
    share_width = gamma_sum.shape[0] // devices
    own_gamma = lax.dynamic_slice_in_dim(gamma_sum, device * share_width, share_width)
    own_beta = lax.dynamic_slice_in_dim(beta_sum, device * share_width, share_width)
    return (
        activations,
        mel_grad,
        own_kernels,
        owned[9].reshape(stem_point.shape),
        owned[8],
        jnp.stack([owned[6], owned[0]]),
        jnp.stack([owned[7], owned[1]]),
        owned[5],
        owned[4],
        owned[3],
        own_taps,
        owned[2],
        own_gains.at[3].add(own_gamma),
        own_shifts.at[3].add(own_beta),
        own_final,
    )


def solution(mesh):
    return jax.shard_map(
        local,
        mesh=mesh,
        in_specs=(
            P(("dp", "fsdp"), None),
            P(("dp", "fsdp"), None),
            P(),
            P(),
            P(("dp", "fsdp"), None, None),
            P(("dp", "fsdp"), None, None),
            P(),
            P(None, None, ("dp", "fsdp")),
            P(None, ("dp", "fsdp"), None),
            P(("dp", "fsdp"), None),
            P(None, ("dp", "fsdp"), None),
            P(None, ("dp", "fsdp"), None),
            P(("dp", "fsdp"), None),
            P(("dp", "fsdp"), None),
            P(("dp", "fsdp"), None),
            P(None, ("dp", "fsdp")),
            P(("dp", "fsdp"), None),
            P(None, ("dp", "fsdp")),
            P(None, ("dp", "fsdp")),
            P(("dp", "fsdp")),
        ),
        out_specs=(
            P(("dp", "fsdp"), None),
            P(("dp", "fsdp"), None),
            P(None, None, ("dp", "fsdp")),
            P(None, ("dp", "fsdp"), None),
            P(("dp", "fsdp"), None),
            P(None, ("dp", "fsdp"), None),
            P(None, ("dp", "fsdp"), None),
            P(("dp", "fsdp"), None),
            P(("dp", "fsdp"), None),
            P(("dp", "fsdp"), None),
            P(None, ("dp", "fsdp")),
            P(("dp", "fsdp"), None),
            P(None, ("dp", "fsdp")),
            P(None, ("dp", "fsdp")),
            P(("dp", "fsdp")),
        ),
        check_vma=False,
    )
```

```python
import functools
import types

import jax
import jax.numpy as jnp
from jax import lax
from jax.experimental import pallas as pl
from jax.experimental.pallas import tpu as pltpu
from jax.sharding import PartitionSpec as P

CTX = 128


EPSILON = 1e-05
MASKED_LOGIT = -1e30
MESH = pl.DeviceIdType.MESH
CORES = 2
AXES = ("dp", "fsdp")
LANES = 128
BINS = 24
GROUPS = 5
TILE = 16
PART = 32
F32 = jnp.float32
BF16 = jnp.bfloat16


def grid_sizes():
    dp, fsdp = lax.axis_size(AXES[0]), lax.axis_size(AXES[1])
    high = 2 if dp % 2 == 0 else 1
    return (high, dp // high, fsdp // CORES, CORES)


def own_place(sizes):
    dp, fsdp = lax.axis_index(AXES[0]), lax.axis_index(AXES[1])
    return (dp // sizes[1], dp % sizes[1], fsdp // CORES, fsdp % CORES)


def peer_on(place, sizes, digit, step):
    other = list(place)
    other[digit] = (place[digit] + step) % sizes[digit]
    return tuple(other)


def device_of(place, sizes):
    return (place[0] * sizes[1] + place[1], place[2] * CORES + place[3])


def send(src, dst, device, send_sem, recv_sem):
    copy = pltpu.make_async_remote_copy(
        src_ref=src,
        dst_ref=dst,
        send_sem=send_sem,
        recv_sem=recv_sem,
        device_id=device,
        device_id_type=MESH,
    )
    copy.start()
    return copy


def group_peers(sizes):
    dp, fsdp = lax.axis_index(AXES[0]), lax.axis_index(AXES[1])
    dp_size, fsdp_size = sizes[0] * sizes[1], sizes[2] * CORES
    near = [(dp, (fsdp + step) % fsdp_size) for step in range(1, fsdp_size)]
    far = [((dp + step) % dp_size, fsdp) for step in range(1, dp_size)]
    return near, far


def greet(sizes):
    barrier = pltpu.get_barrier_semaphore()
    near, far = group_peers(sizes)
    for device in near + far:
        pl.semaphore_signal(barrier, inc=1, device_id=device, device_id_type=MESH)
    pl.semaphore_wait(barrier, len(near) + len(far))


def iota(shape, axis):
    return lax.broadcasted_iota(jnp.int32, shape, axis)


def flags(condition):
    return jnp.where(condition, 1.0, 0.0)


def mm(left, right):
    return jnp.dot(left, right, preferred_element_type=F32)


def mm_t(left, right):
    return lax.dot_general(left, right, (((1,), (1,)), ((), ())), preferred_element_type=F32)


def rows_of(value):
    return value.reshape(-1, value.shape[-1])


def sigmoid(value):
    return 0.5 + 0.5 * jnp.tanh(0.5 * value)


def silu(value):
    half = 0.5 * value
    return half + half * jnp.tanh(half)


def silu_and_slope(value):
    gate = sigmoid(value)
    out = value * gate
    return out, gate + out * (1.0 - gate)


def normalized(value):
    centred = value - jnp.mean(value, axis=-1, keepdims=True)
    scale = lax.rsqrt(jnp.mean(centred * centred, axis=-1, keepdims=True) + EPSILON)
    return centred * scale, scale


def layer_norm(value, gain, shift):
    return normalized(value)[0] * gain + shift


def layer_norm_back(value, gain, grad):
    unit, scale = normalized(value)
    inner = grad * gain
    centre = jnp.mean(inner, axis=-1, keepdims=True)
    along = jnp.mean(inner * unit, axis=-1, keepdims=True)
    grad_value = scale * (inner - centre - unit * along)
    return grad_value, column_sum(grad * unit), column_sum(grad)


def column_sum(value):
    return jnp.sum(value, axis=0, keepdims=True)


def shift_rows(value, step):
    rows = value.shape[0]
    step = step % rows
    return value if step == 0 else pltpu.roll(value, step, 0)


TAP_ROW, GAIN_ROW, SHIFT_ROW, FINAL_ROW = 0, 9, 15, 20


def layer_kernel(plan, *refs):
    fields, at = {}, 0
    for tree in plan.trees:
        fields |= tree.unflatten(refs[at : at + tree.num_leaves])
        at += tree.num_leaves
    v = types.SimpleNamespace(**fields)
    sizes, frames, bins = plan.sizes, plan.frames, plan.bins
    place = own_place(sizes)
    a, b, z, c = place
    mate = device_of(peer_on(place, sizes, 3, 1), sizes)
    device = lax.axis_index(AXES[0]) * (sizes[2] * CORES) + lax.axis_index(AXES[1])
    count = plan.count
    pending = []

    def arrive(copies):
        for copy in copies:
            copy.wait_recv()
        pending.extend(copies)


    sources = plan.sources(v)
    held = v.held
    opened, first, second, third = {}, {}, {}, {}

    def halves(width):
        half = width // 2
        return (pl.ds(0, half), pl.ds(half, half)) if half % LANES == 0 else (pl.ds(0, width),)

    def open_item(i):
        own = held[i].at[a, b, z, c]
        keep = pltpu.make_async_copy(sources[i], own, v.g_local.at[i])
        keep.start()
        opened[i] = (
            keep,
            [
                send(
                    sources[i],
                    own,
                    device_of(peer_on(place, sizes, 2, step), sizes),
                    v.g_z.at[0, i, step - 1],
                    v.g_z.at[1, i, step - 1],
                )
                for step in range(1, sizes[2])
            ],
        )

    def hop_item(i, hop):
        copies = []
        for order, lanes in enumerate(halves(held[i].shape[-1])):
            digit = 1 - order if hop == 0 else order
            if hop == 0:
                part = held[i].at[a, b, :, c, :, lanes]
            elif order == 0:
                part = held[i].at[a, :, :, c, :, lanes]
            else:
                part = held[i].at[:, b, :, c, :, lanes]
            for step in range(1, sizes[digit]):
                copies.append(
                    send(
                        part,
                        part,
                        device_of(peer_on(place, sizes, digit, step), sizes),
                        v.g_hop.at[0, i, hop, order, step - 1],
                        v.g_hop.at[1, i, hop, order, step - 1],
                    )
                )
        return copies

    state = types.SimpleNamespace(turn=0)

    def turn():
        at = state.turn
        state.turn += 1
        if at + 2 < count:
            open_item(at + 2)
        if at < count:
            opened[at][0].wait()
            arrive(opened[at][1])
            first[at] = hop_item(at, 0)
        if 0 <= at - 1 < count:
            arrive(first[at - 1])
            second[at - 1] = hop_item(at - 1, 1)
        if 0 <= at - 2 < count:
            arrive(second[at - 2])
            part = held[at - 2].at[:, :, :, c]
            third[at - 2] = [
                send(part, part, mate, v.g_core.at[0, at - 2], v.g_core.at[1, at - 2])
            ]
        if 0 <= at - 3 < count:
            arrive(third[at - 3])

    def need(i):
        while state.turn < i + 4:
            turn()

    greet(sizes)
    open_item(0)
    open_item(1)


    own_len = jnp.where(v.assignment[...] == device, v.lengths[...], 0)
    utterances = own_len.shape[1]
    upto = flags(
        iota((utterances, utterances), 0) <= iota((utterances, utterances), 1)
    ).astype(BF16)
    own_low = jnp.broadcast_to(own_len.astype(F32), (TILE, utterances)).astype(BF16)
    finish = mm(own_low, upto)[:1]
    begin = finish - own_len.astype(F32)
    at_frame = iota((frames, utterances), 0).astype(F32)
    inside = flags((at_frame >= begin) & (at_frame < finish))
    same = mm_t(inside.astype(BF16), inside.astype(BF16))
    present = jnp.sum(inside, axis=1, keepdims=True)
    ahead = iota((frames, frames), 1) - iota((frames, frames), 0)

    def same_at(step):
        return jnp.sum(jnp.where(ahead == step, same, 0.0), axis=1, keepdims=True)

    joint = same_at(-1)
    counted = jnp.sum(v.lengths[...].astype(F32), axis=1, keepdims=True)


    bin_at = iota((1, LANES), 1)
    bin_keep = bin_at < bins
    for mask in range(plan.freq_masks):
        start, width = v.freq_spans[2 * mask], v.freq_spans[2 * mask + 1]
        bin_keep = bin_keep & jnp.logical_not((bin_at >= start) & (bin_at < start + width))
    bin_keep = flags(bin_keep)

    def keep_of(phase):
        at = iota((frames, 1), 0) * 8 + phase
        keep = present
        for mask in range(plan.time_masks):
            start, width = v.time_spans[2 * mask], v.time_spans[2 * mask + 1]
            keep = jnp.where((at >= start) & (at < start + width), 0.0, keep)
        return keep * bin_keep

    for phase in range(8):
        masked = v.mel[phase].astype(F32) * keep_of(phase)
        v.feats[phase + 1] = masked
        if phase == 7:
            v.feats[0] = shift_rows(masked, 1) * joint
    lane = iota((1, LANES), 1)

    def band(tap):
        return (lane >= BINS * tap) & (lane < BINS * tap + 17)

    for group in range(GROUPS):
        for phase in range(4):
            total = jnp.zeros((frames, LANES), F32)
            for tap in range(3):
                moved = pltpu.roll(
                    v.feats[2 * phase + tap], (BINS * tap - 16 * group + 1) % LANES, 1
                )
                total = jnp.where(band(tap), moved, total)
            v.windows[group, pl.ds(phase * frames, frames)] = total.astype(BF16)


    need(0)
    devices = sizes[0] * sizes[1] * sizes[2] * CORES

    def spread(rows, width, target):
        each = width // devices
        per_tile = LANES // each
        for tile in range(width // LANES):
            total = jnp.zeros((32, LANES), F32)
            for k in range(per_tile):
                d = tile * per_tile + k
                index = (
                    d // (sizes[1] * sizes[2] * CORES),
                    d // (sizes[2] * CORES) % sizes[1],
                    d // CORES % sizes[2],
                    d % CORES,
                )
                piece = held[0][index][rows : rows + 32].astype(F32)
                total = total + (pltpu.roll(piece, each * k, 1) if k else piece)
            target[:, tile * LANES : (tile + 1) * LANES] = total

    width = plan.width
    channels = plan.channels
    spread(0, width, v.params)
    spread(32, channels, v.kernels)

    def param(row):
        return v.params[row : row + 1]

    def kernel_row(layer, tap, lanes):
        return v.kernels[9 * layer + tap : 9 * layer + tap + 1, lanes]

    every = pl.ds(0, channels)
    for f in range(8):
        v.band_wide[...] = jnp.zeros((LANES, channels), F32)
        for tap in range(9):
            row = BINS * (tap // 3) + 2 * f + tap % 3
            v.band_wide[row : row + 1] = kernel_row(0, tap, every)
        v.banded[f] = v.band_wide[...].astype(BF16)

    need(1)
    point = held[1][...]
    point = point.reshape(-1, point.shape[-1])
    v.points[0] = point[:, :channels].astype(BF16)
    v.points[1] = point[:, channels:].astype(BF16)

    def wide_chunks(extent):
        step = min(extent, 4 * LANES)
        return [slice(start, start + step) for start in range(0, extent, step)]


    def phase_rows(ref, phase, lanes):
        return ref[pl.ds(phase * frames, frames), lanes]

    chunks = [pl.ds(LANES * k, LANES) for k in range(channels // LANES)]
    v.one_odd[1] = jnp.zeros(v.one_odd.shape[1:], F32)
    v.two_odd[1] = jnp.zeros(v.two_odd.shape[1:], F32)

    def stem_step(group, half):
        three = 2 * group + half
        for side in range(2):
            two = 2 * three + side
            low = 4 * half + 2 * side
            window = v.windows[group]
            v.one_even[...] = silu(mm(window, v.banded[low]))
            v.one_odd[side] = silu(mm(window, v.banded[low + 1]))
            pieces = (v.one_odd.at[1 - side], v.one_even, v.one_odd.at[side])
            for lanes in chunks:
                late = early = odd = None
                for column, piece in enumerate(pieces):
                    w0, w1, w2 = (kernel_row(1, 3 * row + column, lanes) for row in range(3))
                    p0, p1, p2, p3 = (phase_rows(piece, phase, lanes) for phase in range(4))
                    carried = w0 * p3
                    even = w1 * p0 + w2 * p1
                    after = w0 * p1 + w1 * p2 + w2 * p3
                    late = carried if late is None else late + carried
                    early = even if early is None else early + even
                    odd = after if odd is None else odd + after
                early = early + shift_rows(late, 1) * joint
                v.level_two[two, pl.ds(0, frames), lanes] = early.astype(BF16)
                v.level_two[two, pl.ds(frames, frames), lanes] = odd.astype(BF16)
            point_two = mm(v.level_two[two], v.points[0])
            v.point_two[two] = point_two.astype(BF16)
            hidden = silu(point_two)
            if side == 0:
                v.two_even[...] = hidden
            else:
                v.two_odd[half] = hidden
        pieces = (v.two_odd.at[1 - half], v.two_even, v.two_odd.at[half])
        for lanes in chunks:
            late = total = None
            for column, piece in enumerate(pieces):
                w0, w1, w2 = (kernel_row(2, 3 * row + column, lanes) for row in range(3))
                p0, p1 = (phase_rows(piece, phase, lanes) for phase in range(2))
                carried = w0 * p1
                now = w1 * p0 + w2 * p1
                late = carried if late is None else late + carried
                total = now if total is None else total + now
            total = total + shift_rows(late, 1) * joint
            v.level_three[three, :, lanes] = total.astype(BF16)
        point_three = mm(v.level_three[three], v.points[1])
        v.point_three[three] = point_three.astype(BF16)
        at = pl.multiple_of(three * channels, channels)
        v.stem_hidden[:, pl.ds(at, channels)] = silu(point_three).astype(BF16)

    for group in range(GROUPS):
        lax.fori_loop(0, 2, lambda half, carry: (stem_step(group, half), carry)[1], 0)
        turn()

    bins_three = 2 * GROUPS


    need(2)
    v.after_stem[...] = mm(v.stem_hidden[...], rows_of(held[2][...]))

    def ffn(stream, row, inner, outer, normed_ref, hidden_ref, active_ref):
        normed_ref[...] = layer_norm(stream, param(GAIN_ROW + row), param(SHIFT_ROW + row)).astype(BF16)
        need(inner)
        for lanes in wide_chunks(hidden_ref.shape[1]):
            hidden = mm(normed_ref[...], rows_of(held[inner][:, :, :, :, :, lanes]))
            hidden_ref[:, lanes] = hidden.astype(BF16)
            active_ref[:, lanes] = silu(hidden).astype(BF16)
        need(outer)
        return mm(active_ref[...], rows_of(held[outer][...]))

    v.after_ffn[...] = v.after_stem[...] + 0.5 * ffn(
        v.after_stem[...], 0, 3, 4, v.normed0, v.hidden0, v.active0
    )
    v.normed1[...] = layer_norm(
        v.after_ffn[...], param(GAIN_ROW + 1), param(SHIFT_ROW + 1)
    ).astype(BF16)
    need(5)
    for lanes in wide_chunks(3 * width):
        v.joined[:, lanes] = mm(v.normed1[...], rows_of(held[5][:, :, :, :, :, lanes])).astype(BF16)
    heads = plan.heads
    per_tile = LANES * heads // width
    head_width = width // heads
    apart = jnp.abs(ahead)

    def head_lanes(head):
        inner = head % per_tile
        return (lane >= inner * head_width) & (lane < (inner + 1) * head_width)

    def tile_of(ref, part, head):
        start = part * width + head // per_tile * LANES
        return ref[:, start : start + LANES]

    def only(value, head):
        return jnp.where(head_lanes(head), value.astype(F32), 0.0).astype(BF16)

    for tile in range(width // LANES):
        mixed = jnp.zeros((frames, LANES), F32)
        for head in range(tile * per_tile, (tile + 1) * per_tile):
            scores = mm_t(only(tile_of(v.joined, 0, head), head), tile_of(v.joined, 1, head))
            allowed = (same > 0.5) & (apart <= v.contexts[head])
            logits = jnp.where(allowed, scores * head_width ** (-0.5), MASKED_LOGIT)
            exponent = jnp.exp(logits - jnp.max(logits, axis=-1, keepdims=True))
            weights = exponent / jnp.sum(exponent, axis=-1, keepdims=True)
            v.weights[head] = weights
            out = mm(weights.astype(BF16), tile_of(v.joined, 2, head))
            mixed = jnp.where(head_lanes(head), out, mixed)
        v.mixed[:, tile * LANES : (tile + 1) * LANES] = mixed.astype(BF16)
    need(6)
    v.after_attn[...] = v.after_ffn[...] + mm(v.mixed[...], rows_of(held[6][...]))
    v.normed2[...] = layer_norm(
        v.after_attn[...], param(GAIN_ROW + 2), param(SHIFT_ROW + 2)
    ).astype(BF16)
    need(7)
    for lanes in wide_chunks(2 * width):
        v.gated[:, lanes] = mm(v.normed2[...], rows_of(held[7][:, :, :, :, :, lanes]))
    radius = plan.radius
    merged = v.gated[:, :width] * sigmoid(v.gated[:, width:])
    v.merged[...] = merged
    depthwise = jnp.zeros((frames, width), F32)
    for tap in range(2 * radius + 1):
        step = tap - radius
        depthwise = depthwise + shift_rows(merged, -step) * same_at(step) * param(TAP_ROW + tap)
    v.depthwise[...] = depthwise

    near, far = group_peers(sizes)
    blocks = width // LANES

    def open_total(which, rows):
        for row, value in enumerate(rows):
            for k in range(blocks):
                at = row * blocks + k
                v.t_own[which, at : at + 1] = value[:, k * LANES : (k + 1) * LANES]
        return [
            send(
                v.t_own.at[which],
                v.t_near.at[which, k],
                peer,
                v.t_sem.at[0, which, k],
                v.t_sem.at[1, which, k],
            )
            for k, peer in enumerate(near)
        ]

    def close_total(which, copies):
        arrive(copies)
        total = v.t_own[which]
        for k in range(len(near)):
            total = total + v.t_near[which, k]
        v.t_mid[which] = total
        copies = [
            send(
                v.t_mid.at[which],
                v.t_far.at[which, k],
                peer,
                v.t_sem.at[0, which, len(near) + k],
                v.t_sem.at[1, which, len(near) + k],
            )
            for k, peer in enumerate(far)
        ]
        arrive(copies)
        for k in range(len(far)):
            total = total + v.t_far[which, k]
        return [
            jnp.concatenate(
                [total[row * blocks + k : row * blocks + k + 1] for k in range(blocks)], axis=1
            )
            for row in range(2)
        ]

    counts = open_total(
        0, [column_sum(depthwise * present), column_sum(depthwise * depthwise * present)]
    )
    turn()
    first_sum, second_sum = close_total(0, counts)
    average = first_sum / counted
    spread_out = second_sum / counted - average * average
    inv_spread = lax.rsqrt(spread_out + EPSILON)
    v.standard[...] = (v.depthwise[...] - average) * inv_spread
    v.batch_normed[...] = v.standard[...] * param(GAIN_ROW + 3) + param(SHIFT_ROW + 3)
    v.conv_active[...] = silu(v.batch_normed[...]).astype(BF16)
    need(8)
    v.after_conv[...] = v.after_attn[...] + mm(v.conv_active[...], rows_of(held[8][...]))
    v.after_second[...] = v.after_conv[...] + 0.5 * ffn(
        v.after_conv[...], 4, 9, 10, v.normed4, v.hidden1, v.active1
    )
    gain_last, shift_last = param(GAIN_ROW + 5), param(FINAL_ROW)
    v.activations[...] = (
        layer_norm(v.after_second[...], gain_last, shift_last) * present
    ).astype(BF16)


    need(count - 1)
    for copy in pending:
        copy.wait_send()
    pending.clear()
    core_sent, hop_one, hop_two, z_sent = {}, {}, {}, {}
    grads = plan.grads

    def block_of(i):
        spec = grads[i]
        return held[spec.weight].at[:, :, :, 0] if spec.weight else v.kept[i]

    def transposed(value):
        return jnp.transpose(value.astype(F32)).astype(BF16)

    def right_of(i):
        return v.right[i].at[pl.ds(0, frames)]

    def start_product(i, left):
        right = right_of(i)
        columns = v.columns[i]
        per_part = left.shape[1] // (sizes[0] * sizes[1])
        for high in range(sizes[0]):
            for low in range(sizes[1]):
                start = (high * sizes[1] + low) * per_part
                part = transposed(left[:, start : start + per_part])
                columns[high, low] = part.reshape(columns.shape[2:])
        core_sent[i] = [
            send(
                columns.at[:, :, :, 1 - c],
                v.mates[i],
                mate,
                v.s_core.at[0, i, 0],
                v.s_core.at[1, i, 0],
            ),
            send(
                right,
                v.right[i].at[pl.ds(frames, frames)],
                mate,
                v.s_core.at[0, i, 1],
                v.s_core.at[1, i, 1],
            ),
        ]

    def start_sum(i):
        own = v.parts[i]
        core_sent[i] = [
            send(
                own.at[:, :, :, 1 - c],
                v.mates[i],
                mate,
                v.s_core.at[0, i, 0],
                v.s_core.at[1, i, 0],
            )
        ]

    def lanes_of(i):
        return halves(grads[i].block[-1])

    def send_hop(i, hop):
        block = block_of(i)
        copies = []
        for order, lanes in enumerate(lanes_of(i)):
            digit = 1 - order if hop == 0 else order
            for step in range(1, sizes[digit]):
                other = peer_on(place, sizes, digit, step)
                if hop == 0:
                    part = block.at[:, other[1]] if order == 0 else block.at[other[0]]
                else:
                    part = block.at[other[0], b] if order == 0 else block.at[a, other[1]]
                part = part.at[:, :, :, lanes] if hop == 0 else part.at[:, :, lanes]
                copies.append(
                    send(
                        part,
                        v.landed[i][order][hop].at[step - 1],
                        device_of(other, sizes),
                        v.s_hop.at[0, i, hop, order, step - 1],
                        v.s_hop.at[1, i, hop, order, step - 1],
                    )
                )
        return copies

    def add_hop(i, hop):
        block = block_of(i)
        for order, lanes in enumerate(lanes_of(i)):
            digit = 1 - order if hop == 0 else order
            landed = v.landed[i][order][hop]
            if hop == 0:
                mine = block.at[:, b] if order == 0 else block.at[a]
                mine = mine.at[:, :, :, lanes]
            else:
                mine = block.at[a, b].at[:, :, lanes]
            lead = mine.shape[:-2]

            def add(at, carry):
                index = (at,) if len(lead) == 1 else (at // lead[1], at % lead[1])
                total = mine[index].astype(F32)
                for step in range(1, sizes[digit]):
                    total = total + landed[(step - 1,) + index].astype(F32)
                mine[index] = total.astype(BF16)
                return carry

            lax.fori_loop(0, lead[0] * (lead[1] if len(lead) > 1 else 1), add, 0)

    def first_hop(i):
        spec = grads[i]
        arrive(core_sent[i])
        block = block_of(i)
        if spec.product:
            own, mates, right = v.columns[i], v.mates[i], v.right[i]
            split = spec.block[0] > 2 * TILE
            columns = 2 * LANES
            steps = spec.block[1] // columns
            parts = sizes[0] * (sizes[1] if split else 1)

            def multiply(at, carry):
                part, lanes = at // steps, pl.ds(pl.multiple_of(at % steps * columns, columns), columns)
                index = (part // sizes[1], part % sizes[1]) if split else (part,)
                middle = (slice(None),) * (3 - len(index))
                left = jnp.concatenate(
                    [rows_of(own[index + middle + (c,)]), rows_of(mates[index])], axis=1
                )
                product = mm(left, right[:, lanes]).astype(BF16)
                target = block.at[index + middle + (slice(None), lanes)]
                target[...] = product.reshape(target.shape)
                return carry

            lax.fori_loop(0, parts * steps, multiply, 0)
        else:
            own = v.parts[i][:, :, :, c].astype(F32)
            block[...] = (own + v.mates[i][...].astype(F32)).astype(BF16)
        hop_one[i] = send_hop(i, 0)

    def second_hop(i):
        arrive(hop_one[i])
        add_hop(i, 0)
        hop_two[i] = send_hop(i, 1)

    def third_hop(i):
        arrive(hop_two[i])
        add_hop(i, 1)
        block = block_of(i)
        z_sent[i] = []
        for step in range(1, sizes[2]):
            other = peer_on(place, sizes, 2, step)
            z_sent[i].append(
                send(
                    block.at[a, b, other[2]],
                    v.landed_z[i].at[step - 1],
                    device_of(other, sizes),
                    v.s_z.at[0, i, step - 1],
                    v.s_z.at[1, i, step - 1],
                )
            )

    def last_sum(i):
        arrive(z_sent[i])
        total = block_of(i)[a, b, z].astype(F32)
        for step in range(1, sizes[2]):
            total = total + v.landed_z[i][step - 1].astype(F32)
        return total

    owned = (
        v.grad_outer.at[1],
        v.grad_inner.at[1],
        v.grad_conv_out,
        v.grad_conv_in,
        v.grad_attn,
        v.grad_qkv,
        v.grad_outer.at[0],
        v.grad_inner.at[0],
        v.grad_stem,
        v.grad_point,
    )

    def finish_grad(i):
        owned[i][...] = last_sum(i)

    OUTER1, INNER1, CONV_OUT, CONV_IN, ATTN, QKV, OUTER0, INNER0, STEM, POINT, WIDE, TAPS = range(12)

    def add_param(row, value):
        v.d_params[row : row + 1] = value

    v.d_params[...] = jnp.zeros(v.d_params.shape, F32)

    grad = v.cotangent[...].astype(F32) * present
    grad_stream, gain_part, shift_part = layer_norm_back(v.after_second[...], gain_last, grad)
    add_param(GAIN_ROW + 5, gain_part)
    add_param(FINAL_ROW, shift_part)
    v.stream[...] = grad_stream

    def norm_back(row, value_ref, grad_normed):
        grad_value, gain_part, shift_part = layer_norm_back(
            value_ref[...], param(GAIN_ROW + row), grad_normed
        )
        add_param(GAIN_ROW + row, gain_part)
        add_param(SHIFT_ROW + row, shift_part)
        v.stream[...] = v.stream[...] + grad_value

    def ffn_back(row, stream_ref, inner, outer, normed, hidden, active, items):
        out_grad, hidden_grad = right_of(items[0]), right_of(items[1])
        out_grad[...] = (0.5 * v.stream[...]).astype(BF16)
        start_product(items[0], active)
        start = 0
        for high in range(sizes[0]):
            for low in range(sizes[1]):
                rows = rows_of(held[outer][high, low])
                lanes = slice(start, start + rows.shape[0])
                start += rows.shape[0]
                slope = silu_and_slope(hidden[:, lanes].astype(F32))[1]
                hidden_grad[:, lanes] = (mm_t(out_grad[...], rows) * slope).astype(BF16)
        start_product(items[1], normed)
        norm_back(row, stream_ref, mm_t(hidden_grad[...], rows_of(held[inner][...])))

    ffn_back(
        4,
        v.after_conv,
        9,
        10,
        v.normed4,
        v.hidden1,
        v.active1,
        (OUTER1, INNER1),
    )
    right_of(CONV_OUT)[...] = v.stream[...].astype(BF16)
    start_product(CONV_OUT, v.conv_active)
    grad_active = mm_t(right_of(CONV_OUT)[...], rows_of(held[8][...]))
    grad_batch = grad_active * silu_and_slope(v.batch_normed[...])[1] * present
    v.grad_batch[...] = grad_batch
    beta_own = column_sum(grad_batch)
    gamma_own = column_sum(grad_batch * v.standard[...])
    add_param(GAIN_ROW + 3, gamma_own)
    add_param(SHIFT_ROW + 3, beta_own)
    sums = open_total(1, [beta_own, gamma_own])
    first_hop(OUTER1)
    first_hop(INNER1)
    beta_sum, gamma_sum = close_total(1, sums)
    bn_gain = param(GAIN_ROW + 3)
    grad_first = (
        inv_spread * inv_spread * bn_gain * gamma_sum * average - inv_spread * bn_gain * beta_sum
    ) / counted
    grad_second = -0.5 * inv_spread * inv_spread * bn_gain * gamma_sum / counted
    grad_depth = bn_gain * inv_spread * v.grad_batch[...] + present * (
        grad_first + 2.0 * v.depthwise[...] * grad_second
    )
    grad_merged = jnp.zeros((frames, width), F32)
    for tap in range(2 * radius + 1):
        step = tap - radius
        part = grad_depth * same_at(step)
        add_param(TAP_ROW + tap, column_sum(part * shift_rows(v.merged[...], -step)))
        grad_merged = grad_merged + shift_rows(part, step) * param(TAP_ROW + tap)
    gate = sigmoid(v.gated[:, width:])
    right_of(CONV_IN)[:, :width] = (grad_merged * gate).astype(BF16)
    right_of(CONV_IN)[:, width:] = (grad_merged * v.merged[...] * (1.0 - gate)).astype(BF16)
    start_product(CONV_IN, v.normed2)
    first_hop(CONV_OUT)
    norm_back(2, v.after_attn, mm_t(right_of(CONV_IN)[...], rows_of(held[7][...])))

    right_of(ATTN)[...] = v.stream[...].astype(BF16)
    start_product(ATTN, v.mixed)
    v.g_mixed[...] = mm_t(right_of(ATTN)[...], rows_of(held[6][...])).astype(BF16)
    first_hop(CONV_IN)
    for tile in range(width // LANES):
        parts = [jnp.zeros((frames, LANES), F32) for _ in range(3)]
        mixed_grad = v.g_mixed[:, tile * LANES : (tile + 1) * LANES]
        for head in range(tile * per_tile, (tile + 1) * per_tile):
            weights = v.weights[head]
            grad_weights = mm_t(only(mixed_grad, head), tile_of(v.joined, 2, head))
            row_dot = jnp.sum(weights * grad_weights, axis=-1, keepdims=True)
            grad_scores = weights * (grad_weights - row_dot) * head_width ** (-0.5)
            pieces = (
                mm(grad_scores.astype(BF16), tile_of(v.joined, 1, head)),
                mm(transposed(grad_scores), tile_of(v.joined, 0, head)),
                mm(transposed(weights), mixed_grad),
            )
            parts = [
                jnp.where(head_lanes(head), piece, part) for piece, part in zip(pieces, parts)
            ]
        for k, part in enumerate(parts):
            start = k * width + tile * LANES
            right_of(QKV)[:, start : start + LANES] = part.astype(BF16)
    start_product(QKV, v.normed1)
    first_hop(ATTN)
    second_hop(OUTER1)
    norm_back(1, v.after_ffn, mm_t(right_of(QKV)[...], rows_of(held[5][...])))
    ffn_back(
        0,
        v.after_stem,
        3,
        4,
        v.normed0,
        v.hidden0,
        v.active0,
        (OUTER0, INNER0),
    )
    first_hop(QKV)
    right_of(STEM)[...] = v.stream[...].astype(BF16)
    start_product(STEM, v.stem_hidden)
    first_hop(OUTER0)
    first_hop(INNER0)
    start = 0
    for high in range(sizes[0]):
        for low in range(sizes[1]):
            rows = rows_of(held[2][high, low])
            lanes = slice(start, start + rows.shape[0])
            start += rows.shape[0]
            v.g_three[:, lanes] = mm_t(right_of(STEM)[...], rows).astype(BF16)
    first_hop(STEM)
    second_hop(INNER1)


    v.d_kernels[...] = jnp.zeros(v.d_kernels.shape, F32)
    v.d_points[...] = jnp.zeros(v.d_points.shape, F32)
    v.d_windows[...] = jnp.zeros(v.d_windows.shape, F32)
    v.d_banded[...] = jnp.zeros(v.d_banded.shape, F32)
    v.d_three[0] = jnp.zeros(v.d_three.shape[1:], F32)
    v.d_two_even[0] = jnp.zeros(v.d_two_even.shape[1:], F32)

    def add_kernel(layer, tap, lanes, value):
        folded = jnp.sum(value.reshape(-1, 8, LANES), axis=0)
        v.d_kernels[9 * layer + tap, :, lanes] += folded

    def stem_back(group, half):
        three = 2 * group + half
        at = pl.multiple_of(three * channels, channels)
        slope = silu_and_slope(v.point_three[three].astype(F32))[1]
        grad_point = (v.g_three[:, pl.ds(at, channels)].astype(F32) * slope).astype(BF16)
        v.d_points[1] += mm(transposed(v.level_three[three]), grad_point)
        level_grad = mm_t(grad_point, v.points[1])
        v.d_three[half, pl.ds(0, frames)] = level_grad
        v.d_three[half, pl.ds(frames, frames)] = shift_rows(level_grad * joint, -1)
        here, above = v.d_three.at[half], v.d_three.at[1 - half]
        for lanes in chunks:
            k = [kernel_row(2, tap, lanes) for tap in range(9)]
            d, ds = (phase_rows(here, phase, lanes) for phase in range(2))
            n, ns = (phase_rows(above, phase, lanes) for phase in range(2))
            two = 2 * three
            h0, s0 = silu_and_slope(v.point_two[two, pl.ds(0, frames), lanes].astype(F32))
            h1, s1 = silu_and_slope(v.point_two[two, pl.ds(frames, frames), lanes].astype(F32))
            v.g_two[0, pl.ds(0, frames), lanes] = (k[4] * d * s0).astype(BF16)
            v.g_two[0, pl.ds(frames, frames), lanes] = ((k[7] * d + k[1] * ds) * s1).astype(BF16)
            add_kernel(2, 1, lanes, ds * h1)
            add_kernel(2, 4, lanes, d * h0)
            add_kernel(2, 7, lanes, d * h1)
            two = 2 * three + 1
            h0, s0 = silu_and_slope(v.point_two[two, pl.ds(0, frames), lanes].astype(F32))
            h1, s1 = silu_and_slope(v.point_two[two, pl.ds(frames, frames), lanes].astype(F32))
            v.g_two[1, pl.ds(0, frames), lanes] = ((k[5] * d + k[3] * n) * s0).astype(BF16)
            v.g_two[1, pl.ds(frames, frames), lanes] = (
                (k[8] * d + k[2] * ds + k[6] * n + k[0] * ns) * s1
            ).astype(BF16)
            add_kernel(2, 2, lanes, ds * h1)
            add_kernel(2, 5, lanes, d * h0)
            add_kernel(2, 8, lanes, d * h1)
            add_kernel(2, 0, lanes, ns * h1)
            add_kernel(2, 3, lanes, n * h0)
            add_kernel(2, 6, lanes, n * h1)
        for side in range(2):
            low_grad = v.g_two[side]
            v.d_points[0] += mm(transposed(v.level_two[2 * three + side]), low_grad)
            level_grad = mm_t(low_grad, v.points[0])
            target = v.d_two_odd if side else v.d_two_even.at[half]
            target[pl.ds(0, 2 * frames)] = level_grad
            target[pl.ds(2 * frames, frames)] = shift_rows(level_grad[:frames] * joint, -1)
        for side in (1, 0):
            low = 4 * half + 2 * side
            window = v.windows[group]
            v.one_even[...] = mm(window, v.banded[low])
            v.one_odd[0] = mm(window, v.banded[low + 1])
            here = v.d_two_odd if side else v.d_two_even.at[half]
            above = v.d_two_even.at[1 - half] if side else v.d_two_odd
            def convolve_back(part, carry, low=low, here=here, above=above):
                def part_at(phase):
                    return pl.ds(pl.multiple_of(phase * frames + part * PART, PART), PART)

                def part_rows(ref, phase, lanes):
                    return ref[part_at(phase), lanes]

                for lanes in chunks:
                    k = [kernel_row(1, tap, lanes) for tap in range(9)]
                    d0, d1, ds = (part_rows(here, phase, lanes) for phase in range(3))
                    n0, n1, ns = (part_rows(above, phase, lanes) for phase in range(3))

                    def level_one(ref, phase):
                        return silu_and_slope(part_rows(ref, phase, lanes))

                    def put(which, phase, value):
                        v.g_one[which, part_at(phase), lanes] = value.astype(BF16)

                    even, odd = v.one_even, v.one_odd.at[0]
                    h, s = level_one(even, 0)
                    put(0, 0, k[4] * d0 * s)
                    middle = d0 * h
                    h, s = level_one(even, 1)
                    put(0, 1, (k[7] * d0 + k[1] * d1) * s)
                    before, behind = d1 * h, d0 * h
                    h, s = level_one(even, 2)
                    put(0, 2, k[4] * d1 * s)
                    middle = middle + d1 * h
                    h, s = level_one(even, 3)
                    put(0, 3, (k[7] * d1 + k[1] * ds) * s)
                    add_kernel(1, 1, lanes, before + ds * h)
                    add_kernel(1, 4, lanes, middle)
                    add_kernel(1, 7, lanes, behind + d1 * h)
                    h, s = level_one(odd, 0)
                    put(1, 0, (k[5] * d0 + k[3] * n0) * s)
                    middle, middle_n = d0 * h, n0 * h
                    h, s = level_one(odd, 1)
                    put(1, 1, (k[8] * d0 + k[2] * d1 + k[6] * n0 + k[0] * n1) * s)
                    before, behind = d1 * h, d0 * h
                    before_n, behind_n = n1 * h, n0 * h
                    h, s = level_one(odd, 2)
                    put(1, 2, (k[5] * d1 + k[3] * n1) * s)
                    middle, middle_n = middle + d1 * h, middle_n + n1 * h
                    h, s = level_one(odd, 3)
                    put(1, 3, (k[8] * d1 + k[2] * ds + k[6] * n1 + k[0] * ns) * s)
                    add_kernel(1, 2, lanes, before + ds * h)
                    add_kernel(1, 5, lanes, middle)
                    add_kernel(1, 8, lanes, behind + d1 * h)
                    add_kernel(1, 0, lanes, before_n + ns * h)
                    add_kernel(1, 3, lanes, middle_n)
                    add_kernel(1, 6, lanes, behind_n + n1 * h)
                return carry

            lax.fori_loop(0, frames // PART, convolve_back, 0)
            v.d_windows[group] += mm_t(v.g_one[0], v.banded[low]) + mm_t(
                v.g_one[1], v.banded[low + 1]
            )
            v.d_banded[low] += mm(v.window_turned[...], v.g_one[0])
            v.d_banded[low + 1] += mm(v.window_turned[...], v.g_one[1])

    hooks = (
        ((second_hop, CONV_OUT), (third_hop, OUTER1)),
        ((second_hop, CONV_IN), (third_hop, INNER1)),
        ((second_hop, ATTN), (third_hop, CONV_OUT), (finish_grad, OUTER1)),
        ((second_hop, QKV), (third_hop, CONV_IN), (finish_grad, INNER1)),
        ((second_hop, OUTER0), (third_hop, ATTN), (finish_grad, CONV_OUT)),
    )
    for number, group in enumerate(reversed(range(GROUPS))):
        v.window_turned[...] = transposed(v.windows[group])
        lax.fori_loop(0, 2, lambda at, carry: (stem_back(group, 1 - at), carry)[1], 0)
        for step, item in hooks[number]:
            step(item)


    for layer in range(1, 3):
        for tap in range(9):
            row = 9 * layer + tap
            v.d_taps[row : row + 1] = column_sum(v.d_kernels[row])
    for tap in range(9):
        total = None
        for f in range(8):
            row = BINS * (tap // 3) + 2 * f + tap % 3
            piece = v.d_banded[f, row : row + 1]
            total = piece if total is None else total + piece
        v.d_taps[tap : tap + 1] = total
    v.d_taps[27:32] = jnp.zeros((5, channels), F32)

    def gather_columns(i, source, width):
        each = width // devices
        for d in range(devices):
            index = (
                d // (sizes[1] * sizes[2] * CORES),
                d // (sizes[2] * CORES) % sizes[1],
                d // CORES % sizes[2],
                d % CORES,
            )
            tile, k = d * each // LANES, d * each % LANES
            piece = source[:, tile * LANES : (tile + 1) * LANES]
            piece = pltpu.roll(piece, LANES - k, 1) if k else piece
            v.parts[i][index] = jnp.where(lane < each, piece, 0.0).astype(BF16)

    gather_columns(WIDE, v.d_params, width)
    gather_columns(TAPS, v.d_taps, channels)
    shape = sizes + (channels // devices, channels)
    v.parts[POINT][...] = jnp.concatenate(
        [v.d_points[0].reshape(shape), v.d_points[1].reshape(shape)], axis=4
    ).astype(BF16)
    for i in (POINT, WIDE, TAPS):
        start_sum(i)
    second_hop(INNER0)
    third_hop(QKV)
    for i in (POINT, WIDE, TAPS):
        first_hop(i)
    second_hop(STEM)
    third_hop(OUTER0)


    for phase in range(9):
        v.feats[phase] = jnp.zeros((frames, LANES), F32)
    for group in range(GROUPS):
        for phase in range(4):
            rows = v.d_windows[group, pl.ds(phase * frames, frames)]
            for tap in range(3):
                piece = jnp.where(band(tap), rows, 0.0)
                back = (16 * group - 1 - BINS * tap) % LANES
                v.feats[2 * phase + tap] += pltpu.roll(piece, back, 1)
    for phase in range(8):
        total = v.feats[phase + 1]
        if phase == 7:
            total = total + shift_rows(v.feats[0] * joint, -1)
        v.mel_grad[phase] = total * keep_of(phase)

    for i in (POINT, WIDE, TAPS):
        second_hop(i)
    third_hop(INNER0)
    finish_grad(CONV_IN)
    finish_grad(ATTN)
    finish_grad(QKV)
    third_hop(STEM)
    for i in (POINT, WIDE, TAPS):
        third_hop(i)
    finish_grad(OUTER0)
    finish_grad(INNER0)
    finish_grad(STEM)
    finish_grad(POINT)
    wide = last_sum(WIDE)
    each = width // devices
    v.grad_depth[...] = wide[TAP_ROW:GAIN_ROW, :each]
    v.grad_gains[...] = wide[GAIN_ROW:SHIFT_ROW, :each]
    v.grad_shifts[...] = wide[SHIFT_ROW:FINAL_ROW, :each]
    v.grad_final[...] = wide[FINAL_ROW : FINAL_ROW + 1, :each]
    v.grad_kernels[...] = last_sum(TAPS)[:27, : channels // devices]
    for copy in pending:
        copy.wait_send()


def frame_segments(lengths, assignment, device, frames):
    belongs = assignment == device
    own_sizes = jnp.where(belongs, lengths, 0)
    finishes = jnp.cumsum(own_sizes, dtype=jnp.int32)
    beginnings = finishes - own_sizes
    position = jnp.arange(frames, dtype=jnp.int32)[:, None]
    inside = belongs[None, :] & (position >= beginnings[None, :]) & (position < finishes[None, :])
    number = jnp.arange(lengths.shape[0], dtype=jnp.int32)[None, :] + 1
    return jnp.sum(jnp.where(inside, number, 0), axis=1, dtype=jnp.int32) - 1


def feature_keep(segments, time_spans, freq_spans, mel_bins):
    frames = segments.shape[0] * 8
    position = jnp.arange(frames, dtype=jnp.int32)[:, None]
    covered = (position >= time_spans[None, :, 0]) & (
        position < time_spans[None, :, 0] + time_spans[None, :, 1]
    )
    time_keep = jnp.repeat(segments >= 0, 8) & jnp.logical_not(jnp.any(covered, axis=1))
    channel = jnp.arange(mel_bins, dtype=jnp.int32)[:, None]
    banned = (channel >= freq_spans[None, :, 0]) & (
        channel < freq_spans[None, :, 0] + freq_spans[None, :, 1]
    )
    freq_keep = jnp.logical_not(jnp.any(banned, axis=1))
    return (time_keep[:, None] & freq_keep[None, :]).astype(jnp.float32)


def time_taps(values, seg_in, seg_out):
    out_len = seg_out.shape[0]
    paired = values.reshape((out_len, 2) + values.shape[1:])
    even_part = paired[:, 0]
    odd_part = paired[:, 1]
    prior_part = jnp.concatenate([jnp.zeros_like(odd_part[:1]), odd_part[:-1]], axis=0)
    seg_pairs = seg_in.reshape(out_len, 2)
    prior_segs = jnp.concatenate([jnp.full((1,), -2, jnp.int32), seg_pairs[:-1, 1]])
    opening = ((prior_segs == seg_out) & (seg_out >= 0)).astype(values.dtype)
    opening = opening.reshape((out_len,) + (1,) * (values.ndim - 1))
    return (prior_part * opening, even_part, odd_part)


def freq_taps(values):
    frames, bins_in = (values.shape[0], values.shape[1])
    paired = values.reshape((frames, bins_in // 2, 2) + values.shape[2:])
    even_part = paired[:, :, 0]
    odd_part = paired[:, :, 1]
    prior_part = jnp.concatenate([jnp.zeros_like(odd_part[:, :1]), odd_part[:, :-1]], axis=1)
    return (prior_part, even_part, odd_part)


def strided_conv(values, kernel, seg_in, seg_out):
    summed = None
    for tap_row, tap_rows in enumerate(time_taps(values, seg_in, seg_out)):
        for tap_col, tap_piece in enumerate(freq_taps(tap_rows)):
            if tap_piece.ndim == 2:
                tap_piece = tap_piece[:, :, None]
            addend = tap_piece * kernel[3 * tap_row + tap_col]
            summed = addend if summed is None else summed + addend
    present = (seg_out >= 0).astype(summed.dtype)
    return summed * present[:, None, None]


def depth_glu(gated_rows, kernel, segments):
    model_width = gated_rows.shape[1] // 2
    merged = gated_rows[:, :model_width] * jax.nn.sigmoid(gated_rows[:, model_width:])
    radius = kernel.shape[0] // 2
    frames = gated_rows.shape[0]
    padded = jnp.pad(merged, ((radius, radius), (0, 0)))
    padded_segs = jnp.pad(segments, (radius, radius), constant_values=-2)
    summed = jnp.zeros_like(merged)
    for tap_index in range(kernel.shape[0]):
        same_segment = (padded_segs[tap_index : tap_index + frames] == segments).astype(
            merged.dtype
        )
        summed = (
            summed
            + padded[tap_index : tap_index + frames] * same_segment[:, None] * kernel[tap_index]
        )
    return summed


def stem_front(masked, first_kernel, second_kernel, segments):
    seg_zero = jnp.repeat(segments, 8)
    seg_one = jnp.repeat(segments, 4)
    seg_two = jnp.repeat(segments, 2)
    level_one = jax.nn.silu(strided_conv(masked, first_kernel, seg_zero, seg_one))
    return strided_conv(level_one, second_kernel, seg_one, seg_two)


def stem_middle(point_two, third_kernel, segments):
    frames = segments.shape[0]
    channels = point_two.shape[1]
    hidden = jax.nn.silu(point_two).reshape(frames * 2, -1, channels)
    return strided_conv(hidden, third_kernel, jnp.repeat(segments, 2), segments)


def matmul(operand, matrix):
    return jnp.dot(operand, matrix, preferred_element_type=jnp.float32)


def over_rows(operand, matrix):
    return lax.dot_general(
        operand, matrix, (((0,), (0,)), ((), ())), preferred_element_type=jnp.float32
    )


def against(operand, matrix):
    return lax.dot_general(
        operand, matrix, (((1,), (1,)), ((), ())), preferred_element_type=jnp.float32
    )


def ffn_forward(stream, norm_gain, norm_shift, inner_weight, outer_weight):
    normed = layer_norm(stream, norm_gain, norm_shift).astype(jnp.bfloat16)
    hidden = matmul(normed, inner_weight)
    active = jax.nn.silu(hidden).astype(jnp.bfloat16)
    return (matmul(active, outer_weight), (normed, hidden, active))


def ffn_backward(stream, norm_gain, norm_shift, inner_weight, outer_weight, kept_values, grad_out):
    normed, hidden, active = kept_values
    grad_outer = over_rows(active, grad_out)
    grad_active = against(grad_out, outer_weight)
    grad_hidden = jax.vjp(jax.nn.silu, hidden)[1](grad_active)[0].astype(jnp.bfloat16)
    grad_inner = over_rows(normed, grad_hidden)
    grad_normed = against(grad_hidden, inner_weight)
    pullback = jax.vjp(layer_norm, stream, norm_gain, norm_shift)[1]
    grad_stream, grad_gain, grad_shift = pullback(grad_normed)
    return (grad_stream, grad_gain, grad_shift, grad_inner, grad_outer)


def split_heads(joined, head_count):
    frames = joined.shape[0]
    model_width = joined.shape[1] // 3
    shaped = joined.reshape(frames, 3, head_count, model_width // head_count)
    return (shaped[:, 0], shaped[:, 1], shaped[:, 2])


def block_logits(queries, key_rows, query_segs, key_segs, anchor, frames, contexts):
    scores = jnp.einsum("qhd,khd->hqk", queries, key_rows, preferred_element_type=jnp.float32)
    radius = (key_rows.shape[0] - queries.shape[0]) // 2
    query_pos = anchor + jnp.arange(queries.shape[0], dtype=jnp.int32)
    key_pos = anchor - radius + jnp.arange(key_rows.shape[0], dtype=jnp.int32)
    distance = jnp.abs(query_pos[:, None] - key_pos[None, :])
    allowed = (
        (query_segs[:, None] == key_segs[None, :])
        & (key_pos[None, :] >= 0)
        & (key_pos[None, :] < frames)
    )
    allowed = allowed[None] & (distance[None] <= contexts[:, None, None])
    return jnp.where(allowed, scores * queries.shape[2] ** (-0.5), MASKED_LOGIT)


def attend_forward(joined, segments, contexts):
    frames = joined.shape[0]
    queries, key_rows, value_rows = split_heads(joined, contexts.shape[0])
    padded_keys = jnp.pad(key_rows, ((CTX, CTX), (0, 0), (0, 0)))
    padded_values = jnp.pad(value_rows, ((CTX, CTX), (0, 0), (0, 0)))
    padded_segs = jnp.pad(segments, (CTX, CTX), constant_values=-2)
    logits = block_logits(queries, padded_keys, segments, padded_segs, 0, frames, contexts)
    highest = jnp.max(logits, axis=-1, keepdims=True)
    exponent = jnp.exp(logits - highest)
    summed = jnp.sum(exponent, axis=-1, keepdims=True)
    weights = (exponent / summed).astype(jnp.bfloat16)
    outputs = jnp.einsum("hqk,khd->qhd", weights, padded_values, preferred_element_type=jnp.float32)
    log_parts = highest[:, :, 0] + jnp.log(summed[:, :, 0])
    return (outputs, log_parts)


def attend_backward(joined, segments, contexts, log_totals, grad_mixed):
    frames = joined.shape[0]
    queries, key_rows, value_rows = split_heads(joined, contexts.shape[0])
    padded_keys = jnp.pad(key_rows, ((CTX, CTX), (0, 0), (0, 0)))
    padded_values = jnp.pad(value_rows, ((CTX, CTX), (0, 0), (0, 0)))
    padded_segs = jnp.pad(segments, (CTX, CTX), constant_values=-2)
    block_rows = min(frames, 512)
    grad_keys = jnp.zeros(padded_keys.shape, jnp.float32)
    grad_values = jnp.zeros(padded_values.shape, jnp.float32)
    query_span = slice(0, block_rows)
    key_span = slice(0, block_rows + 2 * CTX)
    logits = block_logits(queries, padded_keys, segments, padded_segs, 0, frames, contexts)
    weights = jnp.exp(logits - log_totals[:, query_span, None])
    grad_weights = jnp.einsum(
        "qhd,khd->hqk", grad_mixed, padded_values, preferred_element_type=jnp.float32
    )
    row_dot = jnp.sum(weights * grad_weights, axis=-1, keepdims=True)
    grad_scores = (weights * (grad_weights - row_dot) * queries.shape[2] ** (-0.5)).astype(
        jnp.bfloat16
    )
    grad_queries = jnp.einsum(
        "hqk,khd->qhd", grad_scores, padded_keys, preferred_element_type=jnp.float32
    )
    grad_keys = grad_keys.at[key_span].add(
        jnp.einsum("hqk,qhd->khd", grad_scores, queries, preferred_element_type=jnp.float32)
    )
    grad_values = grad_values.at[key_span].add(
        jnp.einsum(
            "hqk,qhd->khd",
            weights.astype(jnp.bfloat16),
            grad_mixed,
            preferred_element_type=jnp.float32,
        )
    )
    stacked = jnp.stack(
        [grad_queries, grad_keys[CTX : CTX + frames], grad_values[CTX : CTX + frames]], axis=1
    )
    return stacked.reshape(frames, -1)


def local_plain(
    mel,
    cotangent,
    lengths,
    assignment,
    time_spans,
    freq_spans,
    contexts,
    stem_kernels,
    stem_point,
    stem_out,
    ffn_in,
    ffn_out,
    qkv,
    attn_out,
    conv_in,
    conv_depth,
    conv_out,
    norm_gains,
    norm_shifts,
    final_shift,
):
    device = lax.axis_index(AXES[0]) * lax.axis_size(AXES[1]) + lax.axis_index(AXES[1])
    frames = cotangent.shape[0]
    segments = frame_segments(lengths, assignment, device, frames)
    feature_mask = feature_keep(segments, time_spans[0], freq_spans[0], mel.shape[1])
    present = (segments >= 0).astype(jnp.float32)[:, None]
    counted = jnp.sum(lengths).astype(jnp.float32)
    gathered = (
        lax.all_gather(stem_kernels, AXES, axis=2, tiled=True),
        lax.all_gather(stem_point, AXES, axis=1, tiled=True),
        lax.all_gather(stem_out, AXES, axis=0, tiled=True),
        lax.all_gather(ffn_in, AXES, axis=1, tiled=True),
        lax.all_gather(ffn_out, AXES, axis=1, tiled=True),
        lax.all_gather(qkv, AXES, axis=0, tiled=True),
        lax.all_gather(attn_out, AXES, axis=0, tiled=True),
        lax.all_gather(conv_in, AXES, axis=0, tiled=True),
        lax.all_gather(conv_depth, AXES, axis=1, tiled=True),
        lax.all_gather(conv_out, AXES, axis=0, tiled=True),
        lax.all_gather(norm_gains, AXES, axis=1, tiled=True),
        lax.all_gather(norm_shifts, AXES, axis=1, tiled=True),
        lax.all_gather(final_shift, AXES, axis=0, tiled=True),
    )
    (
        kernels,
        point_weight,
        stem_weight,
        ffn_inner,
        ffn_outer,
        qkv_weight,
        out_weight,
        conv_inner,
        conv_taps,
        conv_outer,
        norm_rows,
        shift_rows,
        final_row,
    ) = gathered
    kernels_wide = kernels.astype(jnp.float32)
    gains_wide = norm_rows.astype(jnp.float32)
    shifts_wide = shift_rows.astype(jnp.float32)
    final_wide = final_row.astype(jnp.float32)
    masked = mel.astype(jnp.float32) * feature_mask
    level_two, front_pullback = jax.vjp(
        lambda masked_input, first_taps, second_taps: stem_front(
            masked_input, first_taps, second_taps, segments
        ),
        masked,
        kernels_wide[0],
        kernels_wide[1],
    )
    channels = level_two.shape[2]
    level_two_low = level_two.reshape(-1, channels).astype(jnp.bfloat16)
    point_two = matmul(level_two_low, point_weight[0])
    level_three, middle_pullback = jax.vjp(
        lambda point_input, third_taps: stem_middle(point_input, third_taps, segments),
        point_two,
        kernels_wide[2],
    )
    level_three_low = level_three.reshape(-1, channels).astype(jnp.bfloat16)
    point_three = matmul(level_three_low, point_weight[1])
    stem_hidden = jax.nn.silu(point_three).reshape(frames, -1).astype(jnp.bfloat16)
    after_stem = matmul(stem_hidden, stem_weight)
    ffn_result_one, ffn_kept_one = ffn_forward(
        after_stem, gains_wide[0], shifts_wide[0], ffn_inner[0], ffn_outer[0]
    )
    after_ffn = after_stem + 0.5 * ffn_result_one
    attn_normed = layer_norm(after_ffn, gains_wide[1], shifts_wide[1]).astype(jnp.bfloat16)
    joined = matmul(attn_normed, qkv_weight).astype(jnp.bfloat16)
    mixed_heads, log_totals = attend_forward(joined, segments, contexts)
    mixed_low = mixed_heads.reshape(frames, -1).astype(jnp.bfloat16)
    after_attn = after_ffn + matmul(mixed_low, out_weight)
    conv_normed = layer_norm(after_attn, gains_wide[2], shifts_wide[2]).astype(jnp.bfloat16)
    gated_rows = matmul(conv_normed, conv_inner)
    taps_wide = conv_taps.astype(jnp.float32)
    depthwise, depth_pullback = jax.vjp(
        lambda gate_input, taps_input: depth_glu(gate_input, taps_input, segments),
        gated_rows,
        taps_wide,
    )
    first_sum, second_sum = lax.psum(
        (jnp.sum(depthwise * present, axis=0), jnp.sum(depthwise * depthwise * present, axis=0)),
        AXES,
    )
    average = first_sum / counted
    spread = second_sum / counted - average * average
    inv_spread = lax.rsqrt(spread + EPSILON)
    standard = (depthwise - average) * inv_spread
    batch_normed = standard * gains_wide[3] + shifts_wide[3]
    conv_active = jax.nn.silu(batch_normed).astype(jnp.bfloat16)
    after_conv = after_attn + matmul(conv_active, conv_outer)
    ffn_result_two, ffn_kept_two = ffn_forward(
        after_conv, gains_wide[4], shifts_wide[4], ffn_inner[1], ffn_outer[1]
    )
    after_second = after_conv + 0.5 * ffn_result_two
    activations = (layer_norm(after_second, gains_wide[5], final_wide) * present).astype(
        jnp.bfloat16
    )
    weights_back = (
        lax.all_gather(stem_kernels, AXES, axis=2, tiled=True),
        lax.all_gather(stem_point, AXES, axis=1, tiled=True),
        lax.all_gather(stem_out, AXES, axis=0, tiled=True),
        lax.all_gather(ffn_in, AXES, axis=1, tiled=True),
        lax.all_gather(ffn_out, AXES, axis=1, tiled=True),
        lax.all_gather(qkv, AXES, axis=0, tiled=True),
        lax.all_gather(attn_out, AXES, axis=0, tiled=True),
        lax.all_gather(conv_in, AXES, axis=0, tiled=True),
        lax.all_gather(conv_depth, AXES, axis=1, tiled=True),
        lax.all_gather(conv_out, AXES, axis=0, tiled=True),
        lax.all_gather(norm_gains, AXES, axis=1, tiled=True),
        lax.all_gather(norm_shifts, AXES, axis=1, tiled=True),
        lax.all_gather(final_shift, AXES, axis=0, tiled=True),
    )
    (
        back_kernels,
        back_point,
        back_stem,
        back_inner,
        back_outer,
        back_qkv,
        back_attn,
        back_conv_in,
        back_taps,
        back_conv_out,
        back_gains,
        back_shifts,
        back_final,
    ) = weights_back
    back_gains_wide = back_gains.astype(jnp.float32)
    back_shifts_wide = back_shifts.astype(jnp.float32)
    back_final_wide = back_final.astype(jnp.float32)
    grad_final = cotangent.astype(jnp.float32) * present
    pullback = jax.vjp(layer_norm, after_second, back_gains_wide[5], back_final_wide)[1]
    grad_stream, grad_gain_final, grad_shift_final = pullback(grad_final)
    ffn_two = ffn_backward(
        after_conv,
        back_gains_wide[4],
        back_shifts_wide[4],
        back_inner[1],
        back_outer[1],
        ffn_kept_two,
        (0.5 * grad_stream).astype(jnp.bfloat16),
    )
    grad_stream = grad_stream + ffn_two[0]
    grad_conv_low = grad_stream.astype(jnp.bfloat16)
    grad_conv_out = over_rows(conv_active, grad_conv_low)
    grad_active = against(grad_conv_low, back_conv_out)
    grad_batch = jax.vjp(jax.nn.silu, batch_normed)[1](grad_active)[0]
    beta_sum, gamma_sum = lax.psum(
        (jnp.sum(grad_batch * present, axis=0), jnp.sum(grad_batch * standard * present, axis=0)),
        AXES,
    )
    bn_gain = back_gains_wide[3]
    grad_first = (
        inv_spread * inv_spread * bn_gain * gamma_sum * average - inv_spread * bn_gain * beta_sum
    ) / counted
    grad_second = -0.5 * inv_spread * inv_spread * bn_gain * gamma_sum / counted
    grad_depth = bn_gain * inv_spread * grad_batch + present * (
        grad_first + 2.0 * depthwise * grad_second
    )
    grad_gated, grad_taps = depth_pullback(grad_depth)
    grad_gated_low = grad_gated.astype(jnp.bfloat16)
    grad_conv_in = over_rows(conv_normed, grad_gated_low)
    pullback = jax.vjp(layer_norm, after_attn, back_gains_wide[2], back_shifts_wide[2])[1]
    conv_norm_grads = pullback(against(grad_gated_low, back_conv_in))
    grad_stream = grad_stream + conv_norm_grads[0]
    grad_attn_low = grad_stream.astype(jnp.bfloat16)
    grad_attn_out = over_rows(mixed_low, grad_attn_low)
    grad_mixed = against(grad_attn_low, back_attn).astype(jnp.bfloat16).reshape(mixed_heads.shape)
    grad_joined = attend_backward(joined, segments, contexts, log_totals, grad_mixed).astype(
        jnp.bfloat16
    )
    grad_qkv = over_rows(attn_normed, grad_joined)
    pullback = jax.vjp(layer_norm, after_ffn, back_gains_wide[1], back_shifts_wide[1])[1]
    attn_norm_grads = pullback(against(grad_joined, back_qkv))
    grad_stream = grad_stream + attn_norm_grads[0]
    ffn_one = ffn_backward(
        after_stem,
        back_gains_wide[0],
        back_shifts_wide[0],
        back_inner[0],
        back_outer[0],
        ffn_kept_one,
        (0.5 * grad_stream).astype(jnp.bfloat16),
    )
    grad_stream = grad_stream + ffn_one[0]
    grad_stem_low = grad_stream.astype(jnp.bfloat16)
    grad_stem_out = over_rows(stem_hidden, grad_stem_low)
    grad_hidden = against(grad_stem_low, back_stem).reshape(point_three.shape)
    grad_point_three = jax.vjp(jax.nn.silu, point_three)[1](grad_hidden)[0].astype(jnp.bfloat16)
    grad_third_point = over_rows(level_three_low, grad_point_three)
    grad_level_three = against(grad_point_three, back_point[1]).reshape(level_three.shape)
    grad_point_two, grad_third_kernel = middle_pullback(grad_level_three)
    grad_point_two_low = grad_point_two.astype(jnp.bfloat16)
    grad_second_point = over_rows(level_two_low, grad_point_two_low)
    grad_level_two = against(grad_point_two_low, back_point[0]).reshape(level_two.shape)
    grad_masked, grad_first_kernel, grad_second_kernel = front_pullback(grad_level_two)
    mel_grad = grad_masked * feature_mask
    zero_row = jnp.zeros_like(grad_gain_final)
    grad_gains = jnp.stack(
        [ffn_one[1], attn_norm_grads[1], conv_norm_grads[1], zero_row, ffn_two[1], grad_gain_final]
    )
    grad_shifts = jnp.stack(
        [ffn_one[2], attn_norm_grads[2], conv_norm_grads[2], zero_row, ffn_two[2]]
    )
    grad_kernels = jnp.stack([grad_first_kernel, grad_second_kernel, grad_third_kernel])
    grad_points = jnp.stack([grad_second_point, grad_third_point])
    grad_inner = jnp.stack([ffn_one[3], ffn_two[3]])
    grad_outer = jnp.stack([ffn_one[4], ffn_two[4]])
    owned_grads = (
        lax.psum_scatter(grad_kernels, AXES, scatter_dimension=2, tiled=True),
        lax.psum_scatter(grad_points, AXES, scatter_dimension=1, tiled=True),
        lax.psum_scatter(grad_stem_out, AXES, scatter_dimension=0, tiled=True),
        lax.psum_scatter(grad_inner, AXES, scatter_dimension=1, tiled=True),
        lax.psum_scatter(grad_outer, AXES, scatter_dimension=1, tiled=True),
        lax.psum_scatter(grad_qkv, AXES, scatter_dimension=0, tiled=True),
        lax.psum_scatter(grad_attn_out, AXES, scatter_dimension=0, tiled=True),
        lax.psum_scatter(grad_conv_in, AXES, scatter_dimension=0, tiled=True),
        lax.psum_scatter(grad_taps, AXES, scatter_dimension=1, tiled=True),
        lax.psum_scatter(grad_conv_out, AXES, scatter_dimension=0, tiled=True),
        lax.psum_scatter(grad_gains, AXES, scatter_dimension=1, tiled=True),
        lax.psum_scatter(grad_shifts, AXES, scatter_dimension=1, tiled=True),
        lax.psum_scatter(grad_shift_final, AXES, scatter_dimension=0, tiled=True),
    )
    share_width = gamma_sum.shape[0] // (lax.axis_size(AXES[0]) * lax.axis_size(AXES[1]))
    own_gamma = lax.dynamic_slice_in_dim(gamma_sum, device * share_width, share_width)
    own_beta = lax.dynamic_slice_in_dim(beta_sum, device * share_width, share_width)
    owned_gains = owned_grads[10].at[3].add(own_gamma)
    owned_shifts = owned_grads[11].at[3].add(own_beta)
    return (
        activations,
        mel_grad,
        owned_grads[0],
        owned_grads[1],
        owned_grads[2],
        owned_grads[3],
        owned_grads[4],
        owned_grads[5],
        owned_grads[6],
        owned_grads[7],
        owned_grads[8],
        owned_grads[9],
        owned_gains,
        owned_shifts,
        owned_grads[12],
    )


def gather_sources(v):
    return [
        v.small,
        v.point,
        v.stem_out,
        v.ffn_in.at[0],
        v.ffn_out.at[0],
        v.qkv,
        v.attn_out,
        v.conv_in,
        v.conv_out,
        v.ffn_in.at[1],
        v.ffn_out.at[1],
    ]


def packed_small(stem_kernels, conv_depth, norm_gains, norm_shifts, final_shift):
    wide = jnp.concatenate([conv_depth, norm_gains, norm_shifts, final_shift[None]], axis=0)
    taps = stem_kernels.reshape(-1, stem_kernels.shape[2])
    wide = jnp.pad(wide, ((0, 32 - wide.shape[0]), (0, LANES - wide.shape[1])))
    taps = jnp.pad(taps, ((0, 32 - taps.shape[0]), (0, LANES - taps.shape[1])))
    return jnp.concatenate([wide, taps], axis=0)


def local(
    mel,
    cotangent,
    lengths,
    assignment,
    time_spans,
    freq_spans,
    contexts,
    stem_kernels,
    stem_point,
    stem_out,
    ffn_in,
    ffn_out,
    qkv,
    attn_out,
    conv_in,
    conv_depth,
    conv_out,
    norm_gains,
    norm_shifts,
    final_shift,
):
    arguments = (mel, cotangent, lengths, assignment, time_spans, freq_spans, contexts)
    arguments += (stem_kernels, stem_point, stem_out, ffn_in, ffn_out, qkv, attn_out)
    arguments += (conv_in, conv_depth, conv_out, norm_gains, norm_shifts, final_shift)
    if qkv.shape[0] % TILE or stem_out.shape[0] % TILE:
        return local_plain(*arguments)
    sizes = grid_sizes()
    devices = sizes[0] * sizes[1] * sizes[2] * sizes[3]
    frames, width = cotangent.shape
    bins = mel.shape[1]
    channels = stem_point.shape[2]
    hidden = ffn_in.shape[2]
    heads = contexts.shape[0]
    bins_two, bins_three = 4 * GROUPS, 2 * GROUPS
    mel_phases = jnp.pad(
        mel.reshape(frames, 8, bins).swapaxes(0, 1), ((0, 0), (0, 0), (0, LANES - bins))
    )
    small = packed_small(stem_kernels, conv_depth, norm_gains, norm_shifts, final_shift)
    point = stem_point.astype(F32).swapaxes(0, 1).reshape(stem_point.shape[1], -1)
    inputs = dict(
        mel=(mel_phases, pltpu.VMEM),
        cotangent=(cotangent, pltpu.VMEM),
        lengths=(lengths.reshape(1, -1), pltpu.VMEM),
        assignment=(assignment.reshape(1, -1), pltpu.VMEM),
        time_spans=(time_spans.reshape(-1), pltpu.SMEM),
        freq_spans=(freq_spans.reshape(-1), pltpu.SMEM),
        contexts=(contexts, pltpu.SMEM),
        small=(small, pl.ANY),
        point=(point, pl.ANY),
        stem_out=(stem_out, pl.ANY),
        ffn_in=(ffn_in, pl.ANY),
        ffn_out=(ffn_out, pl.ANY),
        qkv=(qkv, pl.ANY),
        attn_out=(attn_out, pl.ANY),
        conv_in=(conv_in, pl.ANY),
        conv_out=(conv_out, pl.ANY),
    )
    shards = [
        small.shape,
        point.shape,
        stem_out.shape,
        ffn_in.shape[1:],
        ffn_out.shape[1:],
        qkv.shape,
        attn_out.shape,
        conv_in.shape,
        conv_out.shape,
        ffn_in.shape[1:],
        ffn_out.shape[1:],
    ]
    count = len(shards)
    dma = pltpu.SemaphoreType.DMA
    z_steps = max(1, sizes[2] - 1)
    wide = max(1, sizes[0] - 1, sizes[1] - 1)
    near = sizes[2] * CORES - 1
    far = max(1, sizes[0] * sizes[1] - 1)
    tokens = (frames, width)
    total_rows = (max(8, 2 * width // LANES), LANES)
    scratch = dict(
        held=[pltpu.VMEM(sizes + s, F32 if i == 1 else BF16) for i, s in enumerate(shards)],
        g_local=dma((count,)),
        g_z=dma((2, count, z_steps)),
        g_hop=dma((2, count, 2, 2, wide)),
        g_core=dma((2, count)),
        t_own=pltpu.VMEM((2,) + total_rows, F32),
        t_mid=pltpu.VMEM((2,) + total_rows, F32),
        t_near=pltpu.VMEM((2, near) + total_rows, F32),
        t_far=pltpu.VMEM((2, far) + total_rows, F32),
        t_sem=dma((2, 2, near + far)),
        feats=pltpu.VMEM((9, frames, LANES), F32),
        windows=pltpu.VMEM((GROUPS, 4 * frames, LANES), BF16),
        params=pltpu.VMEM((32, width), F32),
        kernels=pltpu.VMEM((32, channels), F32),
        band_wide=pltpu.VMEM((LANES, channels), F32),
        banded=pltpu.VMEM((8, LANES, channels), BF16),
        points=pltpu.VMEM((2, channels, channels), BF16),
        one_even=pltpu.VMEM((4 * frames, channels), F32),
        one_odd=pltpu.VMEM((2, 4 * frames, channels), F32),
        two_even=pltpu.VMEM((2 * frames, channels), F32),
        two_odd=pltpu.VMEM((2, 2 * frames, channels), F32),
        level_two=pltpu.VMEM((bins_two, 2 * frames, channels), BF16),
        point_two=pltpu.VMEM((bins_two, 2 * frames, channels), BF16),
        level_three=pltpu.VMEM((bins_three, frames, channels), BF16),
        point_three=pltpu.VMEM((bins_three, frames, channels), BF16),
        weights=pltpu.VMEM((heads, frames, frames), F32),
        joined=pltpu.VMEM((frames, 3 * width), BF16),
        gated=pltpu.VMEM((frames, 2 * width), F32),
        hidden0=pltpu.VMEM((frames, hidden), BF16),
        hidden1=pltpu.VMEM((frames, hidden), BF16),
        active0=pltpu.VMEM((frames, hidden), BF16),
        active1=pltpu.VMEM((frames, hidden), BF16),
        after_stem=pltpu.VMEM(tokens, F32),
        after_ffn=pltpu.VMEM(tokens, F32),
        after_attn=pltpu.VMEM(tokens, F32),
        after_conv=pltpu.VMEM(tokens, F32),
        after_second=pltpu.VMEM(tokens, F32),
        merged=pltpu.VMEM(tokens, F32),
        depthwise=pltpu.VMEM(tokens, F32),
        standard=pltpu.VMEM(tokens, F32),
        batch_normed=pltpu.VMEM(tokens, F32),
        normed0=pltpu.VMEM(tokens, BF16),
        normed1=pltpu.VMEM(tokens, BF16),
        normed2=pltpu.VMEM(tokens, BF16),
        normed4=pltpu.VMEM(tokens, BF16),
        mixed=pltpu.VMEM(tokens, BF16),
        conv_active=pltpu.VMEM(tokens, BF16),
    )
    outputs = dict(
        activations=(tokens, BF16),
        mel_grad=((8, frames, LANES), F32),
        grad_kernels=((27, channels // devices), F32),
        grad_point=((2 * channels // devices, channels), F32),
        grad_stem=(stem_out.shape, F32),
        grad_inner=(ffn_in.shape, F32),
        grad_outer=(ffn_out.shape, F32),
        grad_qkv=(qkv.shape, F32),
        grad_attn=(attn_out.shape, F32),
        grad_conv_in=(conv_in.shape, F32),
        grad_depth=(conv_depth.shape, F32),
        grad_conv_out=(conv_out.shape, F32),
        grad_gains=(norm_gains.shape, F32),
        grad_shifts=(norm_shifts.shape, F32),
        grad_final=((1, width // devices), F32),
    )
    grads = [
        types.SimpleNamespace(weight=weight, product=weight > 0, block=block)
        for weight, block in [(weight, shards[weight]) for weight in range(10, 1, -1)]
        + [(0, (2 * channels // devices, channels)), (0, (32, LANES)), (0, (32, LANES))]
    ]
    lead = sizes[:3]
    columns, mates, right, parts, kept, landed, landed_z = {}, {}, {}, {}, {}, {}, {}
    for i, spec in enumerate(grads):
        rows, breadth = spec.block
        if spec.product:
            columns[i] = pltpu.VMEM(sizes + (rows, frames), BF16)
            mates[i] = pltpu.VMEM(lead + (rows, frames), BF16)
            right[i] = pltpu.VMEM((2 * frames, breadth), BF16)
        else:
            parts[i] = pltpu.VMEM(sizes + spec.block, BF16)
            kept[i] = pltpu.VMEM(lead + spec.block, BF16)
            mates[i] = pltpu.VMEM(lead + spec.block, BF16)
        split = 2 if breadth // 2 % LANES == 0 else 1
        part = (rows, breadth // split)
        landed[i] = []
        for order in range(split):
            one, two = (1, 0) if order == 0 else (0, 1)
            steps = (max(1, sizes[one] - 1), max(1, sizes[two] - 1))
            landed[i].append(
                [
                    pltpu.VMEM((steps[0], sizes[two], sizes[2]) + part, BF16),
                    pltpu.VMEM((steps[1], sizes[2]) + part, BF16),
                ]
            )
        landed_z[i] = pltpu.VMEM((z_steps,) + spec.block, BF16)
    scratch |= dict(
        columns=columns,
        mates=mates,
        right=right,
        parts=parts,
        kept=kept,
        landed=landed,
        landed_z=landed_z,
        s_core=dma((2, len(grads), 2)),
        s_hop=dma((2, len(grads), 2, 2, wide)),
        s_z=dma((2, len(grads), z_steps)),
        stem_hidden=pltpu.VMEM((frames, bins_three * channels), BF16),
        d_params=pltpu.VMEM((32, width), F32),
        d_taps=pltpu.VMEM((32, channels), F32),
        stream=pltpu.VMEM(tokens, F32),
        grad_batch=pltpu.VMEM(tokens, F32),
        g_mixed=pltpu.VMEM(tokens, BF16),
        g_three=pltpu.VMEM((frames, bins_three * channels), BF16),
        g_two=pltpu.VMEM((2, 2 * frames, channels), BF16),
        g_one=pltpu.VMEM((2, 4 * frames, channels), BF16),
        d_three=pltpu.VMEM((2, 2 * frames, channels), F32),
        d_two_even=pltpu.VMEM((2, 3 * frames, channels), F32),
        d_two_odd=pltpu.VMEM((3 * frames, channels), F32),
        d_kernels=pltpu.VMEM((27, 8, channels), F32),
        d_points=pltpu.VMEM((2, channels, channels), F32),
        d_windows=pltpu.VMEM((GROUPS, 4 * frames, LANES), F32),
        d_banded=pltpu.VMEM((8, LANES, channels), F32),
        window_turned=pltpu.VMEM((LANES, 4 * frames), BF16),
    )
    plan = types.SimpleNamespace(
        sizes=sizes,
        frames=frames,
        bins=bins,
        count=count,
        width=width,
        channels=channels,
        heads=heads,
        radius=conv_depth.shape[0] // 2,
        time_masks=time_spans.shape[1],
        freq_masks=freq_spans.shape[1],
        sources=gather_sources,
        grads=grads,
    )
    kinds = ({name: 0 for name in inputs}, {name: 0 for name in outputs}, scratch)
    plan.trees = [jax.tree.structure(kind) for kind in kinds]
    results = pl.pallas_call(
        functools.partial(layer_kernel, plan),
        out_shape=[jax.ShapeDtypeStruct(*spec) for _, spec in sorted(outputs.items())],
        in_specs=[pl.BlockSpec(memory_space=space) for _, (_, space) in sorted(inputs.items())],
        out_specs=[pl.BlockSpec(memory_space=pltpu.VMEM)] * len(outputs),
        scratch_shapes=jax.tree.leaves(scratch),
        compiler_params=pltpu.CompilerParams(
            collective_id=0, has_side_effects=True, vmem_limit_bytes=62 * 2**20
        ),
        name="layer",
    )(*[value for _, (value, _) in sorted(inputs.items())])
    made = types.SimpleNamespace(**dict(zip(sorted(outputs), results)))
    mel_grad = made.mel_grad[:, :, :bins].swapaxes(0, 1).reshape(mel.shape)
    return (
        made.activations,
        mel_grad,
        made.grad_kernels.reshape(stem_kernels.shape),
        made.grad_point.reshape(stem_point.shape),
        made.grad_stem,
        made.grad_inner,
        made.grad_outer,
        made.grad_qkv,
        made.grad_attn,
        made.grad_conv_in,
        made.grad_depth,
        made.grad_conv_out,
        made.grad_gains,
        made.grad_shifts,
        made.grad_final.reshape(final_shift.shape),
    )


def solution(mesh):
    return jax.shard_map(
        local,
        mesh=mesh,
        in_specs=(
            P(AXES, None),
            P(AXES, None),
            P(),
            P(),
            P(AXES, None, None),
            P(AXES, None, None),
            P(),
            P(None, None, AXES),
            P(None, AXES, None),
            P(AXES, None),
            P(None, AXES, None),
            P(None, AXES, None),
            P(AXES, None),
            P(AXES, None),
            P(AXES, None),
            P(None, AXES),
            P(AXES, None),
            P(None, AXES),
            P(None, AXES),
            P(AXES),
        ),
        out_specs=(
            P(AXES, None),
            P(AXES, None),
            P(None, None, AXES),
            P(None, AXES, None),
            P(AXES, None),
            P(None, AXES, None),
            P(None, AXES, None),
            P(AXES, None),
            P(AXES, None),
            P(AXES, None),
            P(None, AXES),
            P(AXES, None),
            P(None, AXES),
            P(None, AXES),
            P(AXES),
        ),
        check_vma=False,
    )
```

```python
import functools
import types

import jax
import jax.numpy as jnp
from jax import lax
from jax.experimental import pallas as pl
from jax.experimental.pallas import tpu as pltpu
from jax.sharding import PartitionSpec as P

CTX = 128


EPSILON = 1e-05
MASKED_LOGIT = -1e30
MESH = pl.DeviceIdType.MESH
CORES = 2
AXES = ("dp", "fsdp")
LANES = 128
BINS = 24
GROUPS = 5
TILE = 16
PART = 32
F32 = jnp.float32
BF16 = jnp.bfloat16


def grid_sizes():
    dp, fsdp = lax.axis_size(AXES[0]), lax.axis_size(AXES[1])
    high = 2 if dp % 2 == 0 else 1
    return (high, dp // high, fsdp // CORES, CORES)


def own_place(sizes):
    dp, fsdp = lax.axis_index(AXES[0]), lax.axis_index(AXES[1])
    return (dp // sizes[1], dp % sizes[1], fsdp // CORES, fsdp % CORES)


def peer_on(place, sizes, digit, step):
    other = list(place)
    other[digit] = (place[digit] + step) % sizes[digit]
    return tuple(other)


def device_of(place, sizes):
    return (place[0] * sizes[1] + place[1], place[2] * CORES + place[3])


def send(src, dst, device, send_sem, recv_sem):
    copy = pltpu.make_async_remote_copy(
        src_ref=src,
        dst_ref=dst,
        send_sem=send_sem,
        recv_sem=recv_sem,
        device_id=device,
        device_id_type=MESH,
    )
    copy.start()
    return copy


def group_peers(sizes):
    dp, fsdp = lax.axis_index(AXES[0]), lax.axis_index(AXES[1])
    dp_size, fsdp_size = sizes[0] * sizes[1], sizes[2] * CORES
    near = [(dp, (fsdp + step) % fsdp_size) for step in range(1, fsdp_size)]
    far = [((dp + step) % dp_size, fsdp) for step in range(1, dp_size)]
    return near, far


def greet(sizes):
    near, far = group_peers(sizes)
    for device in near + far:
        pl.semaphore_signal(
            pltpu.get_barrier_semaphore(), inc=1, device_id=device, device_id_type=MESH
        )


def await_greetings(sizes):
    near, far = group_peers(sizes)
    pl.semaphore_wait(pltpu.get_barrier_semaphore(), len(near) + len(far))


def iota(shape, axis):
    return lax.broadcasted_iota(jnp.int32, shape, axis)


def flags(condition):
    return jnp.where(condition, 1.0, 0.0)


def mm(left, right):
    return jnp.dot(left, right, preferred_element_type=F32)


def mm_t(left, right):
    return lax.dot_general(left, right, (((1,), (1,)), ((), ())), preferred_element_type=F32)


def rows_of(value):
    return value.reshape(-1, value.shape[-1])


def sigmoid(value):
    return 0.5 + 0.5 * jnp.tanh(0.5 * value)


def silu(value):
    half = 0.5 * value
    return half + half * jnp.tanh(half)


def silu_and_slope(value):
    gate = sigmoid(value)
    out = value * gate
    return out, gate + out * (1.0 - gate)


def normalized(value):
    centred = value - jnp.mean(value, axis=-1, keepdims=True)
    scale = lax.rsqrt(jnp.mean(centred * centred, axis=-1, keepdims=True) + EPSILON)
    return centred * scale, scale


def layer_norm(value, gain, shift):
    return normalized(value)[0] * gain + shift


def layer_norm_back(value, gain, grad):
    unit, scale = normalized(value)
    inner = grad * gain
    centre = jnp.mean(inner, axis=-1, keepdims=True)
    along = jnp.mean(inner * unit, axis=-1, keepdims=True)
    grad_value = scale * (inner - centre - unit * along)
    return grad_value, column_sum(grad * unit), column_sum(grad)


def column_sum(value):
    return jnp.sum(value, axis=0, keepdims=True)


def shift_rows(value, step):
    rows = value.shape[0]
    step = step % rows
    return value if step == 0 else pltpu.roll(value, step, 0)


TAP_ROW, GAIN_ROW, SHIFT_ROW, FINAL_ROW = 0, 9, 15, 20


def layer_kernel(plan, *refs):
    fields, at = {}, 0
    for tree in plan.trees:
        fields |= tree.unflatten(refs[at : at + tree.num_leaves])
        at += tree.num_leaves
    v = types.SimpleNamespace(**fields)
    sizes, frames, bins = plan.sizes, plan.frames, plan.bins
    place = own_place(sizes)
    a, b, z, c = place
    mate = device_of(peer_on(place, sizes, 3, 1), sizes)
    device = lax.axis_index(AXES[0]) * (sizes[2] * CORES) + lax.axis_index(AXES[1])
    count = plan.count
    pending = []

    def arrive(copies):
        for copy in copies:
            copy.wait_recv()
        pending.extend(copies)


    sources = plan.sources(v)
    held = v.held
    opened, first, second, third = {}, {}, {}, {}

    def halves(start, width):
        half = width // 2
        if half % LANES:
            return (pl.ds(start, width),)
        return (pl.ds(start, half), pl.ds(start + half, half))

    def open_piece(p):
        item, start, width = plan.pieces[p]
        lanes = pl.ds(start, width)
        source, own = sources[item].at[:, lanes], held[item].at[a, b, z, c, :, lanes]
        keep = pltpu.make_async_copy(source, own, v.g_local.at[p])
        keep.start()
        opened[p] = (
            keep,
            [
                send(
                    source,
                    own,
                    device_of(peer_on(place, sizes, 2, step), sizes),
                    v.g_z.at[0, p, step - 1],
                    v.g_z.at[1, p, step - 1],
                )
                for step in range(1, sizes[2])
            ],
        )

    def hop_piece(p, hop):
        item, start, width = plan.pieces[p]
        copies = []
        for order, lanes in enumerate(halves(start, width)):
            digit = 1 - order if hop == 0 else order
            if hop == 0:
                part = held[item].at[a, b, :, c, :, lanes]
            elif order == 0:
                part = held[item].at[a, :, :, c, :, lanes]
            else:
                part = held[item].at[:, b, :, c, :, lanes]
            for step in range(1, sizes[digit]):
                copies.append(
                    send(
                        part,
                        part,
                        device_of(peer_on(place, sizes, digit, step), sizes),
                        v.g_hop.at[0, p, hop, order, step - 1],
                        v.g_hop.at[1, p, hop, order, step - 1],
                    )
                )
        return copies

    state = types.SimpleNamespace(turn=0)
    turns = plan.turns

    def pieces_at(at):
        return turns[at] if 0 <= at < len(turns) else ()

    def turn():
        at = state.turn
        state.turn += 1
        for p in pieces_at(at + 2):
            open_piece(p)
        for p in pieces_at(at):
            opened[p][0].wait()
            arrive(opened[p][1])
            first[p] = hop_piece(p, 0)
        for p in pieces_at(at - 1):
            arrive(first[p])
            second[p] = hop_piece(p, 1)
        for p in pieces_at(at - 2):
            arrive(second[p])
            item, start, width = plan.pieces[p]
            part = held[item].at[:, :, :, c, :, pl.ds(start, width)]
            third[p] = [send(part, part, mate, v.g_core.at[0, p], v.g_core.at[1, p])]
        for p in pieces_at(at - 3):
            arrive(third[p])

    def need(item):
        last = max(
            at for at, ps in enumerate(turns) for p in ps if plan.pieces[p][0] == item
        )
        while state.turn < last + 4:
            turn()

    greet(sizes)
    v.packed[...] = jnp.zeros(v.packed.shape, F32)
    for row, piece in (
        (TAP_ROW, v.conv_depth),
        (GAIN_ROW, v.norm_gains),
        (SHIFT_ROW, v.norm_shifts),
        (FINAL_ROW, v.final_shift),
    ):
        v.packed[row : row + piece.shape[0], : piece.shape[1]] = piece[...].astype(F32)
    for layer in range(3):
        row = 32 + 9 * layer
        v.packed[row : row + 9, : v.stem_kernels.shape[1]] = v.stem_kernels[layer].astype(F32).T
    v.small[...] = v.packed[...].astype(BF16)
    for layer in range(2):
        at = layer * plan.channels
        v.point[:, at : at + plan.channels] = v.stem_point[layer].astype(F32)
    await_greetings(sizes)
    for at in range(2):
        for p in pieces_at(at):
            open_piece(p)


    own_len = jnp.where(v.assignment[...] == device, v.lengths[...], 0)
    utterances = own_len.shape[1]
    upto = flags(
        iota((utterances, utterances), 0) <= iota((utterances, utterances), 1)
    ).astype(BF16)
    own_low = jnp.broadcast_to(own_len.astype(F32), (TILE, utterances)).astype(BF16)
    finish = mm(own_low, upto)[:1]
    begin = finish - own_len.astype(F32)
    at_frame = iota((frames, utterances), 0).astype(F32)
    inside = flags((at_frame >= begin) & (at_frame < finish))
    same = mm_t(inside.astype(BF16), inside.astype(BF16))
    present = jnp.sum(inside, axis=1, keepdims=True)
    ahead = iota((frames, frames), 1) - iota((frames, frames), 0)

    def same_at(step):
        return jnp.sum(jnp.where(ahead == step, same, 0.0), axis=1, keepdims=True)

    joint = same_at(-1)
    counted = jnp.sum(v.lengths[...].astype(F32), axis=1, keepdims=True)


    bin_at = iota((1, LANES), 1)
    bin_keep = bin_at < bins
    for mask in range(plan.freq_masks):
        start, width = v.freq_spans[0, mask, 0], v.freq_spans[0, mask, 1]
        bin_keep = bin_keep & jnp.logical_not((bin_at >= start) & (bin_at < start + width))
    bin_keep = flags(bin_keep)

    def keep_of(phase):
        at = iota((frames, 1), 0) * 8 + phase
        keep = present
        for mask in range(plan.time_masks):
            start, width = v.time_spans[0, mask, 0], v.time_spans[0, mask, 1]
            keep = jnp.where((at >= start) & (at < start + width), 0.0, keep)
        return keep * bin_keep

    for phase in range(8):
        at = pl.ds(phase * frames, frames)
        v.frames_wide[at, :bins] = v.mel[:, at].astype(F32).T
    for phase in range(8):
        masked = jnp.where(
            keep_of(phase) > 0.5, v.frames_wide[pl.ds(phase, frames, stride=8), :], 0.0
        )
        v.feats[phase + 1] = masked
        if phase == 7:
            v.feats[0] = shift_rows(masked, 1) * joint
    lane = iota((1, LANES), 1)

    def band(tap):
        return (lane >= BINS * tap) & (lane < BINS * tap + 17)

    for group in range(GROUPS):
        for phase in range(4):
            total = jnp.zeros((frames, LANES), F32)
            for tap in range(3):
                moved = pltpu.roll(
                    v.feats[2 * phase + tap], (BINS * tap - 16 * group + 1) % LANES, 1
                )
                total = jnp.where(band(tap), moved, total)
            v.windows[group, pl.ds(phase * frames, frames)] = total.astype(BF16)


    need(0)
    devices = sizes[0] * sizes[1] * sizes[2] * CORES

    def spread(rows, width, target):
        each = width // devices
        per_tile = LANES // each
        for tile in range(width // LANES):
            total = jnp.zeros((32, LANES), F32)
            for k in range(per_tile):
                d = tile * per_tile + k
                index = (
                    d // (sizes[1] * sizes[2] * CORES),
                    d // (sizes[2] * CORES) % sizes[1],
                    d // CORES % sizes[2],
                    d % CORES,
                )
                piece = held[0][index][rows : rows + 32].astype(F32)
                total = total + (pltpu.roll(piece, each * k, 1) if k else piece)
            target[:, tile * LANES : (tile + 1) * LANES] = total

    width = plan.width
    channels = plan.channels
    spread(0, width, v.params)
    spread(32, channels, v.kernels)

    def param(row):
        return v.params[row : row + 1]

    def kernel_row(layer, tap, lanes):
        return v.kernels[9 * layer + tap : 9 * layer + tap + 1, lanes]

    every = pl.ds(0, channels)
    for f in range(8):
        v.band_wide[...] = jnp.zeros((LANES, channels), F32)
        for tap in range(9):
            row = BINS * (tap // 3) + 2 * f + tap % 3
            v.band_wide[row : row + 1] = kernel_row(0, tap, every)
        v.banded[:, f * channels : (f + 1) * channels] = v.band_wide[...].astype(BF16)

    need(1)
    point = held[1][...]
    point = point.reshape(-1, point.shape[-1])
    v.points[0] = point[:, :channels].astype(BF16)
    v.points[1] = point[:, channels:].astype(BF16)

    def wide_chunks(extent):
        step = min(extent, 4 * LANES)
        return [slice(start, start + step) for start in range(0, extent, step)]


    grads = plan.grads
    left_sent = {}
    OUTER1, INNER1, CONV_OUT, CONV_IN, ATTN, QKV, OUTER0, INNER0, STEM, POINT, WIDE, TAPS = range(12)

    def transposed(value):
        return jnp.transpose(value.astype(F32)).astype(BF16)

    def start_left(i, left):
        columns = v.columns[i]
        per_part = left.shape[1] // (sizes[0] * sizes[1])
        for high in range(sizes[0]):
            for low in range(sizes[1]):
                start = (high * sizes[1] + low) * per_part
                part = transposed(left[:, start : start + per_part])
                columns[high, low] = part.reshape(columns.shape[2:])
        left_sent[i] = [
            send(
                columns.at[:, :, :, 1 - c],
                v.mates[i],
                mate,
                v.s_core.at[0, i, 0],
                v.s_core.at[1, i, 0],
            )
        ]


    def phase_rows(ref, phase, lanes):
        return ref[pl.ds(phase * frames, frames), lanes]

    chunks = [pl.ds(LANES * k, LANES) for k in range(channels // LANES)]
    v.ones_wide[2] = jnp.zeros(v.ones_wide.shape[1:], F32)
    v.two_odd[1] = jnp.zeros(v.two_odd.shape[1:], F32)

    def stem_step(group, half):
        three = 2 * group + half
        for side in range(2):
            two = 2 * three + side
            low = 4 * half + 2 * side
            window = v.windows[group]
            for f, slot in ((0, 0), (1, 1 + side)):
                at = pl.multiple_of((low + f) * channels, channels)
                value = silu(mm(window, v.banded[:, pl.ds(at, channels)]))
                v.ones_wide[slot] = value
            pieces = (v.ones_wide.at[2 - side], v.ones_wide.at[0], v.ones_wide.at[1 + side])
            for lanes in chunks:
                late = early = odd = None
                for column, piece in enumerate(pieces):
                    w0, w1, w2 = (kernel_row(1, 3 * row + column, lanes) for row in range(3))
                    p0, p1, p2, p3 = (phase_rows(piece, phase, lanes) for phase in range(4))
                    carried = w0 * p3
                    even = w1 * p0 + w2 * p1
                    after = w0 * p1 + w1 * p2 + w2 * p3
                    late = carried if late is None else late + carried
                    early = even if early is None else early + even
                    odd = after if odd is None else odd + after
                early = early + shift_rows(late, 1) * joint
                v.level_now[pl.ds(0, frames), lanes] = early.astype(BF16)
                v.level_now[pl.ds(frames, frames), lanes] = odd.astype(BF16)
            v.level_two[two] = transposed(v.level_now[...])
            point_two = mm(v.level_now[...], v.points[0])
            v.point_two[two] = point_two.astype(BF16)
            hidden = silu(point_two)
            if side == 0:
                v.two_even[...] = hidden
            else:
                v.two_odd[half] = hidden
        pieces = (v.two_odd.at[1 - half], v.two_even, v.two_odd.at[half])
        for lanes in chunks:
            late = total = None
            for column, piece in enumerate(pieces):
                w0, w1, w2 = (kernel_row(2, 3 * row + column, lanes) for row in range(3))
                p0, p1 = (phase_rows(piece, phase, lanes) for phase in range(2))
                carried = w0 * p1
                now = w1 * p0 + w2 * p1
                late = carried if late is None else late + carried
                total = now if total is None else total + now
            total = total + shift_rows(late, 1) * joint
            v.level_now[pl.ds(0, frames), lanes] = total.astype(BF16)
        level_three = v.level_now[pl.ds(0, frames)]
        v.level_three[three] = transposed(level_three)
        point_three = mm(level_three, v.points[1])
        v.point_three[three] = point_three.astype(BF16)
        at = pl.multiple_of(three * channels, channels)
        v.stem_hidden[:, pl.ds(at, channels)] = silu(point_three).astype(BF16)

    for group in range(GROUPS):
        lax.fori_loop(0, 2, lambda half, carry: (stem_step(group, half), carry)[1], 0)
        turn()

    bins_three = 2 * GROUPS


    start_left(STEM, v.stem_hidden)
    need(2)
    v.after_stem[...] = mm(v.stem_hidden[...], rows_of(held[2][...]))

    def ffn(stream, row, inner, outer, normed_ref, hidden_ref, active_ref, items):
        normed_ref[...] = layer_norm(stream, param(GAIN_ROW + row), param(SHIFT_ROW + row)).astype(BF16)
        start_left(items[0], normed_ref)
        need(inner)
        for lanes in wide_chunks(hidden_ref.shape[1]):
            hidden = mm(normed_ref[...], rows_of(held[inner][:, :, :, :, :, lanes]))
            hidden_ref[:, lanes] = hidden.astype(BF16)
            active_ref[:, lanes] = silu(hidden).astype(BF16)
        start_left(items[1], active_ref)
        need(outer)
        return mm(active_ref[...], rows_of(held[outer][...]))

    v.after_ffn[...] = v.after_stem[...] + 0.5 * ffn(
        v.after_stem[...], 0, 3, 4, v.normed0, v.hidden0, v.active0, (INNER0, OUTER0)
    )
    v.normed1[...] = layer_norm(
        v.after_ffn[...], param(GAIN_ROW + 1), param(SHIFT_ROW + 1)
    ).astype(BF16)
    start_left(QKV, v.normed1)
    need(5)
    for lanes in wide_chunks(3 * width):
        v.joined[:, lanes] = mm(v.normed1[...], rows_of(held[5][:, :, :, :, :, lanes])).astype(BF16)
    heads = plan.heads
    per_tile = LANES * heads // width
    head_width = width // heads
    apart = jnp.abs(ahead)

    def head_lanes(head):
        inner = head % per_tile
        return (lane >= inner * head_width) & (lane < (inner + 1) * head_width)

    def tile_of(ref, part, head):
        start = part * width + head // per_tile * LANES
        return ref[:, start : start + LANES]

    def only(value, head):
        return jnp.where(head_lanes(head), value.astype(F32), 0.0).astype(BF16)

    for tile in range(width // LANES):
        mixed = jnp.zeros((frames, LANES), F32)
        for head in range(tile * per_tile, (tile + 1) * per_tile):
            scores = mm_t(only(tile_of(v.joined, 0, head), head), tile_of(v.joined, 1, head))
            allowed = (same > 0.5) & (apart <= v.contexts[head])
            logits = jnp.where(allowed, scores * head_width ** (-0.5), MASKED_LOGIT)
            exponent = jnp.exp(logits - jnp.max(logits, axis=-1, keepdims=True))
            weights = exponent / jnp.sum(exponent, axis=-1, keepdims=True)
            v.weights[head] = weights
            out = mm(weights.astype(BF16), tile_of(v.joined, 2, head))
            mixed = jnp.where(head_lanes(head), out, mixed)
        v.mixed[:, tile * LANES : (tile + 1) * LANES] = mixed.astype(BF16)
    start_left(ATTN, v.mixed)
    need(6)
    v.after_attn[...] = v.after_ffn[...] + mm(v.mixed[...], rows_of(held[6][...]))
    v.normed2[...] = layer_norm(
        v.after_attn[...], param(GAIN_ROW + 2), param(SHIFT_ROW + 2)
    ).astype(BF16)
    start_left(CONV_IN, v.normed2)
    need(7)
    for lanes in wide_chunks(2 * width):
        v.gated[:, lanes] = mm(v.normed2[...], rows_of(held[7][:, :, :, :, :, lanes]))
    radius = plan.radius
    merged = v.gated[:, :width] * sigmoid(v.gated[:, width:])
    v.merged[...] = merged
    depthwise = jnp.zeros((frames, width), F32)
    for tap in range(2 * radius + 1):
        step = tap - radius
        depthwise = depthwise + shift_rows(merged, -step) * same_at(step) * param(TAP_ROW + tap)
    v.depthwise[...] = depthwise

    near, far = group_peers(sizes)
    blocks = width // LANES

    def open_total(which, rows):
        for row, value in enumerate(rows):
            for k in range(blocks):
                at = row * blocks + k
                v.t_own[which, at : at + 1] = value[:, k * LANES : (k + 1) * LANES]
        return [
            send(
                v.t_own.at[which],
                v.t_near.at[which, k],
                peer,
                v.t_sem.at[0, which, k],
                v.t_sem.at[1, which, k],
            )
            for k, peer in enumerate(near)
        ]

    def close_total(which, copies):
        arrive(copies)
        total = v.t_own[which]
        for k in range(len(near)):
            total = total + v.t_near[which, k]
        v.t_mid[which] = total
        copies = [
            send(
                v.t_mid.at[which],
                v.t_far.at[which, k],
                peer,
                v.t_sem.at[0, which, len(near) + k],
                v.t_sem.at[1, which, len(near) + k],
            )
            for k, peer in enumerate(far)
        ]
        arrive(copies)
        for k in range(len(far)):
            total = total + v.t_far[which, k]
        return [
            jnp.concatenate(
                [total[row * blocks + k : row * blocks + k + 1] for k in range(blocks)], axis=1
            )
            for row in range(2)
        ]

    counts = open_total(
        0, [column_sum(depthwise * present), column_sum(depthwise * depthwise * present)]
    )
    turn()
    first_sum, second_sum = close_total(0, counts)
    average = first_sum / counted
    spread_out = second_sum / counted - average * average
    inv_spread = lax.rsqrt(spread_out + EPSILON)
    v.standard[...] = (v.depthwise[...] - average) * inv_spread
    v.batch_normed[...] = v.standard[...] * param(GAIN_ROW + 3) + param(SHIFT_ROW + 3)
    v.conv_active[...] = silu(v.batch_normed[...]).astype(BF16)
    start_left(CONV_OUT, v.conv_active)
    need(8)
    v.after_conv[...] = v.after_attn[...] + mm(v.conv_active[...], rows_of(held[8][...]))
    v.after_second[...] = v.after_conv[...] + 0.5 * ffn(
        v.after_conv[...], 4, 9, 10, v.normed4, v.hidden1, v.active1, (INNER1, OUTER1)
    )
    gain_last, shift_last = param(GAIN_ROW + 5), param(FINAL_ROW)
    v.activations[...] = (
        layer_norm(v.after_second[...], gain_last, shift_last) * present
    ).astype(BF16)


    need(count - 1)
    for copy in pending:
        copy.wait_send()
    pending.clear()
    core_sent, hop_one, hop_two, z_sent = {}, {}, {}, {}
    sums = plan.sums

    def block_of(i):
        spec = grads[i]
        return held[spec.weight].at[:, :, :, 0] if spec.weight else v.kept[i]

    def right_of(i):
        return v.right[i].at[pl.ds(0, frames)]

    def start_product(i):
        core_sent[i] = left_sent[i] + [
            send(
                right_of(i),
                v.right[i].at[pl.ds(frames, frames)],
                mate,
                v.s_core.at[0, i, 1],
                v.s_core.at[1, i, 1],
            ),
        ]

    def start_sum(i):
        core_sent[i] = [
            send(
                v.parts[i].at[:, :, :, 1 - c],
                v.mates[i],
                mate,
                v.s_core.at[0, i, 0],
                v.s_core.at[1, i, 0],
            )
        ]

    def take_product(i):
        spec = grads[i]
        arrive(core_sent[i])
        block = block_of(i)
        if spec.product:
            own, mates, right = v.columns[i], v.mates[i], v.right[i]
            split = spec.block[0] > 2 * TILE
            columns = 2 * LANES
            steps = spec.block[1] // columns
            parts = sizes[0] * (sizes[1] if split else 1)

            def multiply(at, carry):
                part = at // steps
                lanes = pl.ds(pl.multiple_of(at % steps * columns, columns), columns)
                index = (part // sizes[1], part % sizes[1]) if split else (part,)
                middle = (slice(None),) * (3 - len(index))
                left = jnp.concatenate(
                    [rows_of(own[index + middle + (c,)]), rows_of(mates[index])], axis=1
                )
                product = mm(left, right[:, lanes]).astype(BF16)
                target = block.at[index + middle + (slice(None), lanes)]
                target[...] = product.reshape(target.shape)
                return carry

            lax.fori_loop(0, parts * steps, multiply, 0)
        else:
            own = v.parts[i][:, :, :, c].astype(F32)
            block[...] = (own + v.mates[i][...].astype(F32)).astype(BF16)

    def send_hop(p, hop):
        i, start, width = sums[p]
        block = block_of(i)
        copies = []
        for order, lanes in enumerate(halves(start, width)):
            digit = 1 - order if hop == 0 else order
            for step in range(1, sizes[digit]):
                other = peer_on(place, sizes, digit, step)
                if hop == 0:
                    part = block.at[:, other[1]] if order == 0 else block.at[other[0]]
                    part = part.at[:, :, :, lanes]
                else:
                    part = block.at[other[0], b] if order == 0 else block.at[a, other[1]]
                    part = part.at[:, :, lanes]
                copies.append(
                    send(
                        part,
                        v.landed[p][order][hop].at[step - 1],
                        device_of(other, sizes),
                        v.s_hop.at[0, p, hop, order, step - 1],
                        v.s_hop.at[1, p, hop, order, step - 1],
                    )
                )
        return copies

    def add_hop(p, hop):
        i, start, width = sums[p]
        block = block_of(i)
        for order, lanes in enumerate(halves(start, width)):
            digit = 1 - order if hop == 0 else order
            landed = v.landed[p][order][hop]
            if hop == 0:
                mine = block.at[:, b] if order == 0 else block.at[a]
                mine = mine.at[:, :, :, lanes]
            else:
                mine = block.at[a, b].at[:, :, lanes]
            lead = mine.shape[:-2]

            def add(at, carry):
                index = (at,) if len(lead) == 1 else (at // lead[1], at % lead[1])
                total = mine[index].astype(F32)
                for step in range(1, sizes[digit]):
                    total = total + landed[(step - 1,) + index].astype(F32)
                mine[index] = total.astype(BF16)
                return carry

            lax.fori_loop(0, lead[0] * (lead[1] if len(lead) > 1 else 1), add, 0)

    taken = set()

    def first_hop(p):
        if sums[p][0] not in taken:
            taken.add(sums[p][0])
            take_product(sums[p][0])
        hop_one[p] = send_hop(p, 0)

    def second_hop(p):
        arrive(hop_one[p])
        add_hop(p, 0)
        hop_two[p] = send_hop(p, 1)

    def third_hop(p):
        arrive(hop_two[p])
        add_hop(p, 1)
        i, start, width = sums[p]
        block = block_of(i)
        z_sent[p] = []
        for step in range(1, sizes[2]):
            other = peer_on(place, sizes, 2, step)
            z_sent[p].append(
                send(
                    block.at[a, b, other[2], :, pl.ds(start, width)],
                    v.landed_z[p].at[step - 1],
                    device_of(other, sizes),
                    v.s_z.at[0, p, step - 1],
                    v.s_z.at[1, p, step - 1],
                )
            )

    owned = (
        v.grad_outer.at[1],
        v.grad_inner.at[1],
        v.grad_conv_out,
        v.grad_conv_in,
        v.grad_attn,
        v.grad_qkv,
        v.grad_outer.at[0],
        v.grad_inner.at[0],
        v.grad_stem,
        v.grad_point,
        v.sum_wide,
        v.sum_taps,
    )

    def finish_sum(p):
        arrive(z_sent[p])
        i, start, width = sums[p]
        lanes = pl.ds(start, width)
        total = block_of(i)[a, b, z, :, lanes].astype(F32)
        for step in range(1, sizes[2]):
            total = total + v.landed_z[p][step - 1].astype(F32)
        owned[i][:, lanes] = total

    stages = (first_hop, second_hop, third_hop, finish_sum)
    progress = types.SimpleNamespace(at=0)

    def advance(moment):
        while progress.at < len(plan.steps) and plan.steps[progress.at][0] <= moment:
            _, stage, p = plan.steps[progress.at]
            stages[stage](p)
            progress.at += 1

    def add_param(row, value):
        v.d_params[row : row + 1] = value

    v.d_params[...] = jnp.zeros(v.d_params.shape, F32)

    grad = v.cotangent[...].astype(F32) * present
    grad_stream, gain_part, shift_part = layer_norm_back(v.after_second[...], gain_last, grad)
    add_param(GAIN_ROW + 5, gain_part)
    add_param(FINAL_ROW, shift_part)
    v.stream[...] = grad_stream

    def norm_back(row, value_ref, grad_normed):
        grad_value, gain_part, shift_part = layer_norm_back(
            value_ref[...], param(GAIN_ROW + row), grad_normed
        )
        add_param(GAIN_ROW + row, gain_part)
        add_param(SHIFT_ROW + row, shift_part)
        v.stream[...] = v.stream[...] + grad_value

    def ffn_back(row, stream_ref, inner, outer, hidden, items):
        out_grad, hidden_grad = right_of(items[0]), right_of(items[1])
        out_grad[...] = (0.5 * v.stream[...]).astype(BF16)
        start_product(items[0])
        start = 0
        for high in range(sizes[0]):
            for low in range(sizes[1]):
                rows = rows_of(held[outer][high, low])
                lanes = slice(start, start + rows.shape[0])
                start += rows.shape[0]
                slope = silu_and_slope(hidden[:, lanes].astype(F32))[1]
                hidden_grad[:, lanes] = (mm_t(out_grad[...], rows) * slope).astype(BF16)
        start_product(items[1])
        norm_back(row, stream_ref, mm_t(hidden_grad[...], rows_of(held[inner][...])))

    ffn_back(
        4,
        v.after_conv,
        9,
        10,
        v.hidden1,
        (OUTER1, INNER1),
    )
    right_of(CONV_OUT)[...] = v.stream[...].astype(BF16)
    start_product(CONV_OUT)
    grad_active = mm_t(right_of(CONV_OUT)[...], rows_of(held[8][...]))
    grad_batch = grad_active * silu_and_slope(v.batch_normed[...])[1] * present
    v.grad_batch[...] = grad_batch
    beta_own = column_sum(grad_batch)
    gamma_own = column_sum(grad_batch * v.standard[...])
    add_param(GAIN_ROW + 3, gamma_own)
    add_param(SHIFT_ROW + 3, beta_own)
    totals = open_total(1, [beta_own, gamma_own])
    advance(1)
    beta_sum, gamma_sum = close_total(1, totals)
    bn_gain = param(GAIN_ROW + 3)
    grad_first = (
        inv_spread * inv_spread * bn_gain * gamma_sum * average - inv_spread * bn_gain * beta_sum
    ) / counted
    grad_second = -0.5 * inv_spread * inv_spread * bn_gain * gamma_sum / counted
    grad_depth = bn_gain * inv_spread * v.grad_batch[...] + present * (
        grad_first + 2.0 * v.depthwise[...] * grad_second
    )
    grad_merged = jnp.zeros((frames, width), F32)
    for tap in range(2 * radius + 1):
        step = tap - radius
        part = grad_depth * same_at(step)
        add_param(TAP_ROW + tap, column_sum(part * shift_rows(v.merged[...], -step)))
        grad_merged = grad_merged + shift_rows(part, step) * param(TAP_ROW + tap)
    gate = sigmoid(v.gated[:, width:])
    right_of(CONV_IN)[:, :width] = (grad_merged * gate).astype(BF16)
    right_of(CONV_IN)[:, width:] = (grad_merged * v.merged[...] * (1.0 - gate)).astype(BF16)
    start_product(CONV_IN)
    norm_back(2, v.after_attn, mm_t(right_of(CONV_IN)[...], rows_of(held[7][...])))

    right_of(ATTN)[...] = v.stream[...].astype(BF16)
    start_product(ATTN)
    v.g_mixed[...] = mm_t(right_of(ATTN)[...], rows_of(held[6][...])).astype(BF16)
    for tile in range(width // LANES):
        advance(10 + tile)
        parts = [jnp.zeros((frames, LANES), F32) for _ in range(3)]
        mixed_grad = v.g_mixed[:, tile * LANES : (tile + 1) * LANES]
        for head in range(tile * per_tile, (tile + 1) * per_tile):
            weights = v.weights[head]
            grad_weights = mm_t(only(mixed_grad, head), tile_of(v.joined, 2, head))
            row_dot = jnp.sum(weights * grad_weights, axis=-1, keepdims=True)
            grad_scores = weights * (grad_weights - row_dot) * head_width ** (-0.5)
            pieces = (
                mm(grad_scores.astype(BF16), tile_of(v.joined, 1, head)),
                mm(transposed(grad_scores), tile_of(v.joined, 0, head)),
                mm(transposed(weights), mixed_grad),
            )
            parts = [
                jnp.where(head_lanes(head), piece, part) for piece, part in zip(pieces, parts)
            ]
        for k, part in enumerate(parts):
            start = k * width + tile * LANES
            right_of(QKV)[:, start : start + LANES] = part.astype(BF16)
    start_product(QKV)
    norm_back(1, v.after_ffn, mm_t(right_of(QKV)[...], rows_of(held[5][...])))
    ffn_back(
        0,
        v.after_stem,
        3,
        4,
        v.hidden0,
        (OUTER0, INNER0),
    )
    advance(15)
    right_of(STEM)[...] = v.stream[...].astype(BF16)
    start_product(STEM)
    start = 0
    for high in range(sizes[0]):
        for low in range(sizes[1]):
            rows = rows_of(held[2][high, low])
            lanes = slice(start, start + rows.shape[0])
            start += rows.shape[0]
            v.g_three[:, lanes] = mm_t(right_of(STEM)[...], rows).astype(BF16)
    def gather_columns(i, source, width):
        each = width // devices
        for d in range(devices):
            index = (
                d // (sizes[1] * sizes[2] * CORES),
                d // (sizes[2] * CORES) % sizes[1],
                d // CORES % sizes[2],
                d % CORES,
            )
            tile, k = d * each // LANES, d * each % LANES
            piece = source[:, tile * LANES : (tile + 1) * LANES]
            piece = pltpu.roll(piece, LANES - k, 1) if k else piece
            v.parts[i][index] = jnp.where(lane < each, piece, 0.0).astype(BF16)

    gather_columns(WIDE, v.d_params, width)
    start_sum(WIDE)
    advance(STEM_MOMENT)


    v.d_kernels[...] = jnp.zeros(v.d_kernels.shape, F32)
    v.d_points[...] = jnp.zeros(v.d_points.shape, F32)
    v.d_windows[...] = jnp.zeros(v.d_windows.shape, F32)
    v.d_banded[...] = jnp.zeros(v.d_banded.shape, F32)
    v.d_three[0] = jnp.zeros(v.d_three.shape[1:], F32)
    v.d_two_even[0] = jnp.zeros(v.d_two_even.shape[1:], BF16)

    def add_kernel(layer, tap, lanes, value):
        folded = jnp.sum(value.reshape(-1, 8, LANES), axis=0)
        v.d_kernels[9 * layer + tap, :, lanes] += folded

    def stem_back(group, half, moment):
        three = 2 * group + half
        at = pl.multiple_of(three * channels, channels)
        slope = silu_and_slope(v.point_three[three].astype(F32))[1]
        grad_point = (v.g_three[:, pl.ds(at, channels)].astype(F32) * slope).astype(BF16)
        v.d_points[1] += mm(v.level_three[three], grad_point)
        level_grad = mm_t(grad_point, v.points[1])
        v.d_three[half, pl.ds(0, frames)] = level_grad
        v.d_three[half, pl.ds(frames, frames)] = shift_rows(level_grad * joint, -1)
        here, above = v.d_three.at[half], v.d_three.at[1 - half]
        for lanes in chunks:
            k = [kernel_row(2, tap, lanes) for tap in range(9)]
            d, ds = (phase_rows(here, phase, lanes) for phase in range(2))
            n, ns = (phase_rows(above, phase, lanes) for phase in range(2))
            two = 2 * three
            h0, s0 = silu_and_slope(v.point_two[two, pl.ds(0, frames), lanes].astype(F32))
            h1, s1 = silu_and_slope(v.point_two[two, pl.ds(frames, frames), lanes].astype(F32))
            v.g_two[0, pl.ds(0, frames), lanes] = (k[4] * d * s0).astype(BF16)
            v.g_two[0, pl.ds(frames, frames), lanes] = ((k[7] * d + k[1] * ds) * s1).astype(BF16)
            add_kernel(2, 1, lanes, ds * h1)
            add_kernel(2, 4, lanes, d * h0)
            add_kernel(2, 7, lanes, d * h1)
            two = 2 * three + 1
            h0, s0 = silu_and_slope(v.point_two[two, pl.ds(0, frames), lanes].astype(F32))
            h1, s1 = silu_and_slope(v.point_two[two, pl.ds(frames, frames), lanes].astype(F32))
            v.g_two[1, pl.ds(0, frames), lanes] = ((k[5] * d + k[3] * n) * s0).astype(BF16)
            v.g_two[1, pl.ds(frames, frames), lanes] = (
                (k[8] * d + k[2] * ds + k[6] * n + k[0] * ns) * s1
            ).astype(BF16)
            add_kernel(2, 2, lanes, ds * h1)
            add_kernel(2, 5, lanes, d * h0)
            add_kernel(2, 8, lanes, d * h1)
            add_kernel(2, 0, lanes, ns * h1)
            add_kernel(2, 3, lanes, n * h0)
            add_kernel(2, 6, lanes, n * h1)
        for side in range(2):
            low_grad = v.g_two[side]
            v.d_points[0] += mm(v.level_two[2 * three + side], low_grad)
            level_grad = mm_t(low_grad, v.points[0])
            target = v.d_two_odd if side else v.d_two_even.at[half]
            target[pl.ds(0, 2 * frames)] = level_grad.astype(BF16)
            carried = shift_rows(level_grad[:frames] * joint, -1)
            target[pl.ds(2 * frames, frames)] = carried.astype(BF16)
        advance(moment + STEM_STEP / 3)
        low = 4 * half
        for f in range(4):
            at = (low + f) * channels
            v.ones[f] = mm(v.windows[group], v.banded[:, at : at + channels]).astype(BF16)
        for side in (1, 0):
            here = v.d_two_odd if side else v.d_two_even.at[half]
            above = v.d_two_even.at[1 - half] if side else v.d_two_odd
            for lanes in chunks:
                k = [
                    jnp.broadcast_to(kernel_row(1, tap, lanes), (PART, LANES)).astype(BF16)
                    for tap in range(9)
                ]

                def convolve_back(part, carry, k=k, lanes=lanes, side=side, here=here, above=above):
                    def rows_at(phase):
                        return pl.ds(pl.multiple_of(phase * frames + part * PART, PART), PART)

                    def level_one(f, phase):
                        half_value = v.ones[2 * side + f, rows_at(phase), lanes] * 0.5
                        bend = jnp.tanh(half_value)
                        gate = 0.5 + 0.5 * bend
                        out = half_value + half_value * bend
                        return out, gate + out * (1.0 - gate)

                    def put(f, phase, value):
                        at = pl.multiple_of((2 * side + f) * channels, channels)
                        at = pl.ds(at + lanes.start, LANES)
                        v.g_one[rows_at(phase), at] = value

                    def add(tap, value):
                        value = value.astype(F32).reshape(-1, 8, LANES)
                        v.d_kernels[9 + tap, :, lanes] += jnp.sum(value, axis=0)

                    d0, d1, ds = (here[rows_at(phase), lanes] for phase in range(3))
                    n0, n1, ns = (above[rows_at(phase), lanes] for phase in range(3))
                    h, s = level_one(0, 0)
                    put(0, 0, k[4] * d0 * s)
                    middle = d0 * h
                    h, s = level_one(0, 1)
                    put(0, 1, (k[7] * d0 + k[1] * d1) * s)
                    before, behind = d1 * h, d0 * h
                    h, s = level_one(0, 2)
                    put(0, 2, k[4] * d1 * s)
                    middle = middle + d1 * h
                    h, s = level_one(0, 3)
                    put(0, 3, (k[7] * d1 + k[1] * ds) * s)
                    add(1, before + ds * h)
                    add(4, middle)
                    add(7, behind + d1 * h)
                    h, s = level_one(1, 0)
                    put(1, 0, (k[5] * d0 + k[3] * n0) * s)
                    middle, middle_n = d0 * h, n0 * h
                    h, s = level_one(1, 1)
                    put(1, 1, (k[8] * d0 + k[2] * d1 + k[6] * n0 + k[0] * n1) * s)
                    before, behind = d1 * h, d0 * h
                    before_n, behind_n = n1 * h, n0 * h
                    h, s = level_one(1, 2)
                    put(1, 2, (k[5] * d1 + k[3] * n1) * s)
                    middle, middle_n = middle + d1 * h, middle_n + n1 * h
                    h, s = level_one(1, 3)
                    put(1, 3, (k[8] * d1 + k[2] * ds + k[6] * n1 + k[0] * ns) * s)
                    add(2, before + ds * h)
                    add(5, middle)
                    add(8, behind + d1 * h)
                    add(0, before_n + ns * h)
                    add(3, middle_n)
                    add(6, behind_n + n1 * h)
                    return carry

                lax.fori_loop(0, frames // PART, convolve_back, 0)
            advance(moment + STEM_STEP * (3 - side) / 3)
        at = pl.ds(low * channels, 4 * channels)
        v.d_windows[group] += mm_t(v.g_one[...], v.banded[:, at])
        v.d_banded[:, at] += mm(v.window_turned[...], v.g_one[...])

    for number in range(bins_three):
        three = bins_three - 1 - number
        if three % 2:
            v.window_turned[...] = transposed(v.windows[three // 2])
        stem_back(three // 2, three % 2, STEM_MOMENT + STEM_STEP * number)


    for layer in range(1, 3):
        for tap in range(9):
            row = 9 * layer + tap
            v.d_taps[row : row + 1] = column_sum(v.d_kernels[row])
    for tap in range(9):
        total = None
        for f in range(8):
            row = BINS * (tap // 3) + 2 * f + tap % 3
            piece = v.d_banded[row : row + 1, f * channels : (f + 1) * channels]
            total = piece if total is None else total + piece
        v.d_taps[tap : tap + 1] = total
    v.d_taps[27:32] = jnp.zeros((5, channels), F32)

    gather_columns(TAPS, v.d_taps, channels)
    shape = sizes + (channels // devices, channels)
    v.parts[POINT][...] = jnp.concatenate(
        [v.d_points[0].reshape(shape), v.d_points[1].reshape(shape)], axis=4
    ).astype(BF16)
    for i in (POINT, TAPS):
        start_sum(i)
    advance(plan.small_moment)


    for phase in range(9):
        v.feats[phase] = jnp.zeros((frames, LANES), F32)
    for group in range(GROUPS):
        for phase in range(4):
            rows = v.d_windows[group, pl.ds(phase * frames, frames)]
            for tap in range(3):
                piece = jnp.where(band(tap), rows, 0.0)
                back = (16 * group - 1 - BINS * tap) % LANES
                v.feats[2 * phase + tap] += pltpu.roll(piece, back, 1)
    for phase in range(8):
        total = v.feats[phase + 1]
        if phase == 7:
            total = total + shift_rows(v.feats[0] * joint, -1)
        v.frames_wide[pl.ds(phase, frames, stride=8), :] = total * keep_of(phase)

    for phase in range(8):
        at = pl.ds(phase * frames, frames)
        v.mel_grad[:, at] = v.frames_wide[at, :].T[:bins]

    advance(float("inf"))
    wide = v.sum_wide[...]
    each = width // devices
    v.grad_depth[...] = wide[TAP_ROW:GAIN_ROW, :each]
    v.grad_gains[...] = wide[GAIN_ROW:SHIFT_ROW, :each]
    v.grad_shifts[...] = wide[SHIFT_ROW:FINAL_ROW, :each]
    v.grad_final[...] = wide[FINAL_ROW : FINAL_ROW + 1, :each]
    taps = v.sum_taps[...].T
    for layer in range(3):
        v.grad_kernels[layer] = taps[: channels // devices, 9 * layer : 9 * layer + 9]
    for copy in pending:
        copy.wait_send()


def frame_segments(lengths, assignment, device, frames):
    belongs = assignment == device
    own_sizes = jnp.where(belongs, lengths, 0)
    finishes = jnp.cumsum(own_sizes, dtype=jnp.int32)
    beginnings = finishes - own_sizes
    position = jnp.arange(frames, dtype=jnp.int32)[:, None]
    inside = belongs[None, :] & (position >= beginnings[None, :]) & (position < finishes[None, :])
    number = jnp.arange(lengths.shape[0], dtype=jnp.int32)[None, :] + 1
    return jnp.sum(jnp.where(inside, number, 0), axis=1, dtype=jnp.int32) - 1


def feature_keep(segments, time_spans, freq_spans, mel_bins):
    frames = segments.shape[0] * 8
    position = jnp.arange(frames, dtype=jnp.int32)[:, None]
    covered = (position >= time_spans[None, :, 0]) & (
        position < time_spans[None, :, 0] + time_spans[None, :, 1]
    )
    time_keep = jnp.repeat(segments >= 0, 8) & jnp.logical_not(jnp.any(covered, axis=1))
    channel = jnp.arange(mel_bins, dtype=jnp.int32)[:, None]
    banned = (channel >= freq_spans[None, :, 0]) & (
        channel < freq_spans[None, :, 0] + freq_spans[None, :, 1]
    )
    freq_keep = jnp.logical_not(jnp.any(banned, axis=1))
    return (time_keep[:, None] & freq_keep[None, :]).astype(jnp.float32)


def time_taps(values, seg_in, seg_out):
    out_len = seg_out.shape[0]
    paired = values.reshape((out_len, 2) + values.shape[1:])
    even_part = paired[:, 0]
    odd_part = paired[:, 1]
    prior_part = jnp.concatenate([jnp.zeros_like(odd_part[:1]), odd_part[:-1]], axis=0)
    seg_pairs = seg_in.reshape(out_len, 2)
    prior_segs = jnp.concatenate([jnp.full((1,), -2, jnp.int32), seg_pairs[:-1, 1]])
    opening = ((prior_segs == seg_out) & (seg_out >= 0)).astype(values.dtype)
    opening = opening.reshape((out_len,) + (1,) * (values.ndim - 1))
    return (prior_part * opening, even_part, odd_part)


def freq_taps(values):
    frames, bins_in = (values.shape[0], values.shape[1])
    paired = values.reshape((frames, bins_in // 2, 2) + values.shape[2:])
    even_part = paired[:, :, 0]
    odd_part = paired[:, :, 1]
    prior_part = jnp.concatenate([jnp.zeros_like(odd_part[:, :1]), odd_part[:, :-1]], axis=1)
    return (prior_part, even_part, odd_part)


def strided_conv(values, kernel, seg_in, seg_out):
    summed = None
    for tap_row, tap_rows in enumerate(time_taps(values, seg_in, seg_out)):
        for tap_col, tap_piece in enumerate(freq_taps(tap_rows)):
            if tap_piece.ndim == 2:
                tap_piece = tap_piece[:, :, None]
            addend = tap_piece * kernel[3 * tap_row + tap_col]
            summed = addend if summed is None else summed + addend
    present = (seg_out >= 0).astype(summed.dtype)
    return summed * present[:, None, None]


def depth_glu(gated_rows, kernel, segments):
    model_width = gated_rows.shape[1] // 2
    merged = gated_rows[:, :model_width] * jax.nn.sigmoid(gated_rows[:, model_width:])
    radius = kernel.shape[0] // 2
    frames = gated_rows.shape[0]
    padded = jnp.pad(merged, ((radius, radius), (0, 0)))
    padded_segs = jnp.pad(segments, (radius, radius), constant_values=-2)
    summed = jnp.zeros_like(merged)
    for tap_index in range(kernel.shape[0]):
        same_segment = (padded_segs[tap_index : tap_index + frames] == segments).astype(
            merged.dtype
        )
        summed = (
            summed
            + padded[tap_index : tap_index + frames] * same_segment[:, None] * kernel[tap_index]
        )
    return summed


def stem_front(masked, first_kernel, second_kernel, segments):
    seg_zero = jnp.repeat(segments, 8)
    seg_one = jnp.repeat(segments, 4)
    seg_two = jnp.repeat(segments, 2)
    level_one = jax.nn.silu(strided_conv(masked, first_kernel, seg_zero, seg_one))
    return strided_conv(level_one, second_kernel, seg_one, seg_two)


def stem_middle(point_two, third_kernel, segments):
    frames = segments.shape[0]
    channels = point_two.shape[1]
    hidden = jax.nn.silu(point_two).reshape(frames * 2, -1, channels)
    return strided_conv(hidden, third_kernel, jnp.repeat(segments, 2), segments)


def matmul(operand, matrix):
    return jnp.dot(operand, matrix, preferred_element_type=jnp.float32)


def over_rows(operand, matrix):
    return lax.dot_general(
        operand, matrix, (((0,), (0,)), ((), ())), preferred_element_type=jnp.float32
    )


def against(operand, matrix):
    return lax.dot_general(
        operand, matrix, (((1,), (1,)), ((), ())), preferred_element_type=jnp.float32
    )


def ffn_forward(stream, norm_gain, norm_shift, inner_weight, outer_weight):
    normed = layer_norm(stream, norm_gain, norm_shift).astype(jnp.bfloat16)
    hidden = matmul(normed, inner_weight)
    active = jax.nn.silu(hidden).astype(jnp.bfloat16)
    return (matmul(active, outer_weight), (normed, hidden, active))


def ffn_backward(stream, norm_gain, norm_shift, inner_weight, outer_weight, kept_values, grad_out):
    normed, hidden, active = kept_values
    grad_outer = over_rows(active, grad_out)
    grad_active = against(grad_out, outer_weight)
    grad_hidden = jax.vjp(jax.nn.silu, hidden)[1](grad_active)[0].astype(jnp.bfloat16)
    grad_inner = over_rows(normed, grad_hidden)
    grad_normed = against(grad_hidden, inner_weight)
    pullback = jax.vjp(layer_norm, stream, norm_gain, norm_shift)[1]
    grad_stream, grad_gain, grad_shift = pullback(grad_normed)
    return (grad_stream, grad_gain, grad_shift, grad_inner, grad_outer)


def split_heads(joined, head_count):
    frames = joined.shape[0]
    model_width = joined.shape[1] // 3
    shaped = joined.reshape(frames, 3, head_count, model_width // head_count)
    return (shaped[:, 0], shaped[:, 1], shaped[:, 2])


def block_logits(queries, key_rows, query_segs, key_segs, anchor, frames, contexts):
    scores = jnp.einsum("qhd,khd->hqk", queries, key_rows, preferred_element_type=jnp.float32)
    radius = (key_rows.shape[0] - queries.shape[0]) // 2
    query_pos = anchor + jnp.arange(queries.shape[0], dtype=jnp.int32)
    key_pos = anchor - radius + jnp.arange(key_rows.shape[0], dtype=jnp.int32)
    distance = jnp.abs(query_pos[:, None] - key_pos[None, :])
    allowed = (
        (query_segs[:, None] == key_segs[None, :])
        & (key_pos[None, :] >= 0)
        & (key_pos[None, :] < frames)
    )
    allowed = allowed[None] & (distance[None] <= contexts[:, None, None])
    return jnp.where(allowed, scores * queries.shape[2] ** (-0.5), MASKED_LOGIT)


def attend_forward(joined, segments, contexts):
    frames = joined.shape[0]
    queries, key_rows, value_rows = split_heads(joined, contexts.shape[0])
    padded_keys = jnp.pad(key_rows, ((CTX, CTX), (0, 0), (0, 0)))
    padded_values = jnp.pad(value_rows, ((CTX, CTX), (0, 0), (0, 0)))
    padded_segs = jnp.pad(segments, (CTX, CTX), constant_values=-2)
    logits = block_logits(queries, padded_keys, segments, padded_segs, 0, frames, contexts)
    highest = jnp.max(logits, axis=-1, keepdims=True)
    exponent = jnp.exp(logits - highest)
    summed = jnp.sum(exponent, axis=-1, keepdims=True)
    weights = (exponent / summed).astype(jnp.bfloat16)
    outputs = jnp.einsum("hqk,khd->qhd", weights, padded_values, preferred_element_type=jnp.float32)
    log_parts = highest[:, :, 0] + jnp.log(summed[:, :, 0])
    return (outputs, log_parts)


def attend_backward(joined, segments, contexts, log_totals, grad_mixed):
    frames = joined.shape[0]
    queries, key_rows, value_rows = split_heads(joined, contexts.shape[0])
    padded_keys = jnp.pad(key_rows, ((CTX, CTX), (0, 0), (0, 0)))
    padded_values = jnp.pad(value_rows, ((CTX, CTX), (0, 0), (0, 0)))
    padded_segs = jnp.pad(segments, (CTX, CTX), constant_values=-2)
    block_rows = min(frames, 512)
    grad_keys = jnp.zeros(padded_keys.shape, jnp.float32)
    grad_values = jnp.zeros(padded_values.shape, jnp.float32)
    query_span = slice(0, block_rows)
    key_span = slice(0, block_rows + 2 * CTX)
    logits = block_logits(queries, padded_keys, segments, padded_segs, 0, frames, contexts)
    weights = jnp.exp(logits - log_totals[:, query_span, None])
    grad_weights = jnp.einsum(
        "qhd,khd->hqk", grad_mixed, padded_values, preferred_element_type=jnp.float32
    )
    row_dot = jnp.sum(weights * grad_weights, axis=-1, keepdims=True)
    grad_scores = (weights * (grad_weights - row_dot) * queries.shape[2] ** (-0.5)).astype(
        jnp.bfloat16
    )
    grad_queries = jnp.einsum(
        "hqk,khd->qhd", grad_scores, padded_keys, preferred_element_type=jnp.float32
    )
    grad_keys = grad_keys.at[key_span].add(
        jnp.einsum("hqk,qhd->khd", grad_scores, queries, preferred_element_type=jnp.float32)
    )
    grad_values = grad_values.at[key_span].add(
        jnp.einsum(
            "hqk,qhd->khd",
            weights.astype(jnp.bfloat16),
            grad_mixed,
            preferred_element_type=jnp.float32,
        )
    )
    stacked = jnp.stack(
        [grad_queries, grad_keys[CTX : CTX + frames], grad_values[CTX : CTX + frames]], axis=1
    )
    return stacked.reshape(frames, -1)


def local_plain(
    mel,
    cotangent,
    lengths,
    assignment,
    time_spans,
    freq_spans,
    contexts,
    stem_kernels,
    stem_point,
    stem_out,
    ffn_in,
    ffn_out,
    qkv,
    attn_out,
    conv_in,
    conv_depth,
    conv_out,
    norm_gains,
    norm_shifts,
    final_shift,
):
    device = lax.axis_index(AXES[0]) * lax.axis_size(AXES[1]) + lax.axis_index(AXES[1])
    frames = cotangent.shape[0]
    segments = frame_segments(lengths, assignment, device, frames)
    feature_mask = feature_keep(segments, time_spans[0], freq_spans[0], mel.shape[1])
    present = (segments >= 0).astype(jnp.float32)[:, None]
    counted = jnp.sum(lengths).astype(jnp.float32)
    gathered = (
        lax.all_gather(stem_kernels, AXES, axis=2, tiled=True),
        lax.all_gather(stem_point, AXES, axis=1, tiled=True),
        lax.all_gather(stem_out, AXES, axis=0, tiled=True),
        lax.all_gather(ffn_in, AXES, axis=1, tiled=True),
        lax.all_gather(ffn_out, AXES, axis=1, tiled=True),
        lax.all_gather(qkv, AXES, axis=0, tiled=True),
        lax.all_gather(attn_out, AXES, axis=0, tiled=True),
        lax.all_gather(conv_in, AXES, axis=0, tiled=True),
        lax.all_gather(conv_depth, AXES, axis=1, tiled=True),
        lax.all_gather(conv_out, AXES, axis=0, tiled=True),
        lax.all_gather(norm_gains, AXES, axis=1, tiled=True),
        lax.all_gather(norm_shifts, AXES, axis=1, tiled=True),
        lax.all_gather(final_shift, AXES, axis=0, tiled=True),
    )
    (
        kernels,
        point_weight,
        stem_weight,
        ffn_inner,
        ffn_outer,
        qkv_weight,
        out_weight,
        conv_inner,
        conv_taps,
        conv_outer,
        norm_rows,
        shift_rows,
        final_row,
    ) = gathered
    kernels_wide = kernels.astype(jnp.float32)
    gains_wide = norm_rows.astype(jnp.float32)
    shifts_wide = shift_rows.astype(jnp.float32)
    final_wide = final_row.astype(jnp.float32)
    masked = mel.astype(jnp.float32) * feature_mask
    level_two, front_pullback = jax.vjp(
        lambda masked_input, first_taps, second_taps: stem_front(
            masked_input, first_taps, second_taps, segments
        ),
        masked,
        kernels_wide[0],
        kernels_wide[1],
    )
    channels = level_two.shape[2]
    level_two_low = level_two.reshape(-1, channels).astype(jnp.bfloat16)
    point_two = matmul(level_two_low, point_weight[0])
    level_three, middle_pullback = jax.vjp(
        lambda point_input, third_taps: stem_middle(point_input, third_taps, segments),
        point_two,
        kernels_wide[2],
    )
    level_three_low = level_three.reshape(-1, channels).astype(jnp.bfloat16)
    point_three = matmul(level_three_low, point_weight[1])
    stem_hidden = jax.nn.silu(point_three).reshape(frames, -1).astype(jnp.bfloat16)
    after_stem = matmul(stem_hidden, stem_weight)
    ffn_result_one, ffn_kept_one = ffn_forward(
        after_stem, gains_wide[0], shifts_wide[0], ffn_inner[0], ffn_outer[0]
    )
    after_ffn = after_stem + 0.5 * ffn_result_one
    attn_normed = layer_norm(after_ffn, gains_wide[1], shifts_wide[1]).astype(jnp.bfloat16)
    joined = matmul(attn_normed, qkv_weight).astype(jnp.bfloat16)
    mixed_heads, log_totals = attend_forward(joined, segments, contexts)
    mixed_low = mixed_heads.reshape(frames, -1).astype(jnp.bfloat16)
    after_attn = after_ffn + matmul(mixed_low, out_weight)
    conv_normed = layer_norm(after_attn, gains_wide[2], shifts_wide[2]).astype(jnp.bfloat16)
    gated_rows = matmul(conv_normed, conv_inner)
    taps_wide = conv_taps.astype(jnp.float32)
    depthwise, depth_pullback = jax.vjp(
        lambda gate_input, taps_input: depth_glu(gate_input, taps_input, segments),
        gated_rows,
        taps_wide,
    )
    first_sum, second_sum = lax.psum(
        (jnp.sum(depthwise * present, axis=0), jnp.sum(depthwise * depthwise * present, axis=0)),
        AXES,
    )
    average = first_sum / counted
    spread = second_sum / counted - average * average
    inv_spread = lax.rsqrt(spread + EPSILON)
    standard = (depthwise - average) * inv_spread
    batch_normed = standard * gains_wide[3] + shifts_wide[3]
    conv_active = jax.nn.silu(batch_normed).astype(jnp.bfloat16)
    after_conv = after_attn + matmul(conv_active, conv_outer)
    ffn_result_two, ffn_kept_two = ffn_forward(
        after_conv, gains_wide[4], shifts_wide[4], ffn_inner[1], ffn_outer[1]
    )
    after_second = after_conv + 0.5 * ffn_result_two
    activations = (layer_norm(after_second, gains_wide[5], final_wide) * present).astype(
        jnp.bfloat16
    )
    weights_back = (
        lax.all_gather(stem_kernels, AXES, axis=2, tiled=True),
        lax.all_gather(stem_point, AXES, axis=1, tiled=True),
        lax.all_gather(stem_out, AXES, axis=0, tiled=True),
        lax.all_gather(ffn_in, AXES, axis=1, tiled=True),
        lax.all_gather(ffn_out, AXES, axis=1, tiled=True),
        lax.all_gather(qkv, AXES, axis=0, tiled=True),
        lax.all_gather(attn_out, AXES, axis=0, tiled=True),
        lax.all_gather(conv_in, AXES, axis=0, tiled=True),
        lax.all_gather(conv_depth, AXES, axis=1, tiled=True),
        lax.all_gather(conv_out, AXES, axis=0, tiled=True),
        lax.all_gather(norm_gains, AXES, axis=1, tiled=True),
        lax.all_gather(norm_shifts, AXES, axis=1, tiled=True),
        lax.all_gather(final_shift, AXES, axis=0, tiled=True),
    )
    (
        back_kernels,
        back_point,
        back_stem,
        back_inner,
        back_outer,
        back_qkv,
        back_attn,
        back_conv_in,
        back_taps,
        back_conv_out,
        back_gains,
        back_shifts,
        back_final,
    ) = weights_back
    back_gains_wide = back_gains.astype(jnp.float32)
    back_shifts_wide = back_shifts.astype(jnp.float32)
    back_final_wide = back_final.astype(jnp.float32)
    grad_final = cotangent.astype(jnp.float32) * present
    pullback = jax.vjp(layer_norm, after_second, back_gains_wide[5], back_final_wide)[1]
    grad_stream, grad_gain_final, grad_shift_final = pullback(grad_final)
    ffn_two = ffn_backward(
        after_conv,
        back_gains_wide[4],
        back_shifts_wide[4],
        back_inner[1],
        back_outer[1],
        ffn_kept_two,
        (0.5 * grad_stream).astype(jnp.bfloat16),
    )
    grad_stream = grad_stream + ffn_two[0]
    grad_conv_low = grad_stream.astype(jnp.bfloat16)
    grad_conv_out = over_rows(conv_active, grad_conv_low)
    grad_active = against(grad_conv_low, back_conv_out)
    grad_batch = jax.vjp(jax.nn.silu, batch_normed)[1](grad_active)[0]
    beta_sum, gamma_sum = lax.psum(
        (jnp.sum(grad_batch * present, axis=0), jnp.sum(grad_batch * standard * present, axis=0)),
        AXES,
    )
    bn_gain = back_gains_wide[3]
    grad_first = (
        inv_spread * inv_spread * bn_gain * gamma_sum * average - inv_spread * bn_gain * beta_sum
    ) / counted
    grad_second = -0.5 * inv_spread * inv_spread * bn_gain * gamma_sum / counted
    grad_depth = bn_gain * inv_spread * grad_batch + present * (
        grad_first + 2.0 * depthwise * grad_second
    )
    grad_gated, grad_taps = depth_pullback(grad_depth)
    grad_gated_low = grad_gated.astype(jnp.bfloat16)
    grad_conv_in = over_rows(conv_normed, grad_gated_low)
    pullback = jax.vjp(layer_norm, after_attn, back_gains_wide[2], back_shifts_wide[2])[1]
    conv_norm_grads = pullback(against(grad_gated_low, back_conv_in))
    grad_stream = grad_stream + conv_norm_grads[0]
    grad_attn_low = grad_stream.astype(jnp.bfloat16)
    grad_attn_out = over_rows(mixed_low, grad_attn_low)
    grad_mixed = against(grad_attn_low, back_attn).astype(jnp.bfloat16).reshape(mixed_heads.shape)
    grad_joined = attend_backward(joined, segments, contexts, log_totals, grad_mixed).astype(
        jnp.bfloat16
    )
    grad_qkv = over_rows(attn_normed, grad_joined)
    pullback = jax.vjp(layer_norm, after_ffn, back_gains_wide[1], back_shifts_wide[1])[1]
    attn_norm_grads = pullback(against(grad_joined, back_qkv))
    grad_stream = grad_stream + attn_norm_grads[0]
    ffn_one = ffn_backward(
        after_stem,
        back_gains_wide[0],
        back_shifts_wide[0],
        back_inner[0],
        back_outer[0],
        ffn_kept_one,
        (0.5 * grad_stream).astype(jnp.bfloat16),
    )
    grad_stream = grad_stream + ffn_one[0]
    grad_stem_low = grad_stream.astype(jnp.bfloat16)
    grad_stem_out = over_rows(stem_hidden, grad_stem_low)
    grad_hidden = against(grad_stem_low, back_stem).reshape(point_three.shape)
    grad_point_three = jax.vjp(jax.nn.silu, point_three)[1](grad_hidden)[0].astype(jnp.bfloat16)
    grad_third_point = over_rows(level_three_low, grad_point_three)
    grad_level_three = against(grad_point_three, back_point[1]).reshape(level_three.shape)
    grad_point_two, grad_third_kernel = middle_pullback(grad_level_three)
    grad_point_two_low = grad_point_two.astype(jnp.bfloat16)
    grad_second_point = over_rows(level_two_low, grad_point_two_low)
    grad_level_two = against(grad_point_two_low, back_point[0]).reshape(level_two.shape)
    grad_masked, grad_first_kernel, grad_second_kernel = front_pullback(grad_level_two)
    mel_grad = grad_masked * feature_mask
    zero_row = jnp.zeros_like(grad_gain_final)
    grad_gains = jnp.stack(
        [ffn_one[1], attn_norm_grads[1], conv_norm_grads[1], zero_row, ffn_two[1], grad_gain_final]
    )
    grad_shifts = jnp.stack(
        [ffn_one[2], attn_norm_grads[2], conv_norm_grads[2], zero_row, ffn_two[2]]
    )
    grad_kernels = jnp.stack([grad_first_kernel, grad_second_kernel, grad_third_kernel])
    grad_points = jnp.stack([grad_second_point, grad_third_point])
    grad_inner = jnp.stack([ffn_one[3], ffn_two[3]])
    grad_outer = jnp.stack([ffn_one[4], ffn_two[4]])
    owned_grads = (
        lax.psum_scatter(grad_kernels, AXES, scatter_dimension=2, tiled=True),
        lax.psum_scatter(grad_points, AXES, scatter_dimension=1, tiled=True),
        lax.psum_scatter(grad_stem_out, AXES, scatter_dimension=0, tiled=True),
        lax.psum_scatter(grad_inner, AXES, scatter_dimension=1, tiled=True),
        lax.psum_scatter(grad_outer, AXES, scatter_dimension=1, tiled=True),
        lax.psum_scatter(grad_qkv, AXES, scatter_dimension=0, tiled=True),
        lax.psum_scatter(grad_attn_out, AXES, scatter_dimension=0, tiled=True),
        lax.psum_scatter(grad_conv_in, AXES, scatter_dimension=0, tiled=True),
        lax.psum_scatter(grad_taps, AXES, scatter_dimension=1, tiled=True),
        lax.psum_scatter(grad_conv_out, AXES, scatter_dimension=0, tiled=True),
        lax.psum_scatter(grad_gains, AXES, scatter_dimension=1, tiled=True),
        lax.psum_scatter(grad_shifts, AXES, scatter_dimension=1, tiled=True),
        lax.psum_scatter(grad_shift_final, AXES, scatter_dimension=0, tiled=True),
    )
    share_width = gamma_sum.shape[0] // (lax.axis_size(AXES[0]) * lax.axis_size(AXES[1]))
    own_gamma = lax.dynamic_slice_in_dim(gamma_sum, device * share_width, share_width)
    own_beta = lax.dynamic_slice_in_dim(beta_sum, device * share_width, share_width)
    owned_gains = owned_grads[10].at[3].add(own_gamma)
    owned_shifts = owned_grads[11].at[3].add(own_beta)
    return (
        activations,
        mel_grad,
        owned_grads[0],
        owned_grads[1],
        owned_grads[2],
        owned_grads[3],
        owned_grads[4],
        owned_grads[5],
        owned_grads[6],
        owned_grads[7],
        owned_grads[8],
        owned_grads[9],
        owned_gains,
        owned_shifts,
        owned_grads[12],
    )


def gather_sources(v):
    return [
        v.small,
        v.point,
        v.stem_out,
        v.ffn_in.at[0],
        v.ffn_out.at[0],
        v.qkv,
        v.attn_out,
        v.conv_in,
        v.conv_out,
        v.ffn_in.at[1],
        v.ffn_out.at[1],
    ]


STEM_MOMENT = 17
STEM_STEP = 5.0
SMALL_MOMENT = 68
MOMENTS = (0, 0, 0, 10, 10, 13, 15, 15, 17, SMALL_MOMENT, 17, SMALL_MOMENT)
LINK_BYTES = 1e4
LATENCY = 8.0
AHEAD = 8.0


def order_of_steps(sums, grads):
    size = [grads[i].block[0] * width * 2 / LINK_BYTES for i, _, width in sums]
    waiting = list(range(len(sums)))
    hopped, steps = [], []
    now, z_free = 0.0, 0.0
    while waiting or hopped:
        ready = [entry for entry in hopped if entry[0] <= now]
        fresh = [p for p in waiting if MOMENTS[sums[p][0]] <= now]
        if ready:
            entry = ready[0]
            hopped.remove(entry)
            arrived, p = entry
            steps.append((max(arrived, now - AHEAD), 1, p))
            now += size[p] / 2
            landed = now + LATENCY
            steps.append((landed, 2, p))
            z_free = max(z_free, landed) + size[p]
            steps.append((z_free + 2 * LATENCY, 3, p))
        elif fresh:
            p = fresh[0]
            waiting.remove(p)
            steps.append((max(MOMENTS[sums[p][0]], now - AHEAD), 0, p))
            now += size[p]
            hopped.append((now + LATENCY, p))
        else:
            now = min([entry[0] for entry in hopped] + [MOMENTS[sums[p][0]] for p in waiting])
    return sorted(steps)


def finish_kernel(count, *refs):
    for i in range(count):
        refs[count + i][...] = refs[i][...]


def local(
    mel,
    cotangent,
    lengths,
    assignment,
    time_spans,
    freq_spans,
    contexts,
    stem_kernels,
    stem_point,
    stem_out,
    ffn_in,
    ffn_out,
    qkv,
    attn_out,
    conv_in,
    conv_depth,
    conv_out,
    norm_gains,
    norm_shifts,
    final_shift,
):
    arguments = (mel, cotangent, lengths, assignment, time_spans, freq_spans, contexts)
    arguments += (stem_kernels, stem_point, stem_out, ffn_in, ffn_out, qkv, attn_out)
    arguments += (conv_in, conv_depth, conv_out, norm_gains, norm_shifts, final_shift)
    if qkv.shape[0] % TILE or stem_out.shape[0] % TILE:
        return local_plain(*arguments)
    sizes = grid_sizes()
    devices = sizes[0] * sizes[1] * sizes[2] * sizes[3]
    frames, width = cotangent.shape
    bins = mel.shape[1]
    channels = stem_point.shape[2]
    hidden = ffn_in.shape[2]
    heads = contexts.shape[0]
    bins_two, bins_three = 4 * GROUPS, 2 * GROUPS
    inputs = dict(
        mel=(mel.T, pltpu.VMEM),
        stem_kernels=(stem_kernels.swapaxes(1, 2), pltpu.VMEM),
        stem_point=(stem_point, pltpu.VMEM),
        conv_depth=(conv_depth, pltpu.VMEM),
        norm_gains=(norm_gains, pltpu.VMEM),
        norm_shifts=(norm_shifts, pltpu.VMEM),
        final_shift=(final_shift.reshape(1, -1), pltpu.VMEM),
        cotangent=(cotangent, pltpu.VMEM),
        lengths=(lengths.reshape(1, -1), pltpu.VMEM),
        assignment=(assignment.reshape(1, -1), pltpu.VMEM),
        time_spans=(time_spans, pltpu.SMEM),
        freq_spans=(freq_spans, pltpu.SMEM),
        contexts=(contexts, pltpu.SMEM),
        stem_out=(stem_out, pl.ANY),
        ffn_in=(ffn_in, pl.ANY),
        ffn_out=(ffn_out, pl.ANY),
        qkv=(qkv, pl.ANY),
        attn_out=(attn_out, pl.ANY),
        conv_in=(conv_in, pl.ANY),
        conv_out=(conv_out, pl.ANY),
    )
    shards = [
        (64, LANES),
        (stem_point.shape[1], 2 * channels),
        stem_out.shape,
        ffn_in.shape[1:],
        ffn_out.shape[1:],
        qkv.shape,
        attn_out.shape,
        conv_in.shape,
        conv_out.shape,
        ffn_in.shape[1:],
        ffn_out.shape[1:],
    ]
    count = len(shards)

    def cut(item, width, pieces=2):
        return [(item, width // pieces * k, width // pieces) for k in range(pieces)]

    def whole(item):
        return cut(item, shards[item][1], 1)

    def halved(item):
        return cut(item, shards[item][1])

    groups = [whole(0) + whole(1) + whole(6), whole(8)]
    groups += [[piece] for item in (2, 3, 4, 5) for piece in halved(item)]
    groups += [whole(7)] + [[piece] for item in (9, 10) for piece in halved(item)]
    pieces = [piece for group in groups for piece in group]
    turns = [[pieces.index(piece) for piece in group] for group in groups]
    dma = pltpu.SemaphoreType.DMA
    z_steps = max(1, sizes[2] - 1)
    wide = max(1, sizes[0] - 1, sizes[1] - 1)
    near = sizes[2] * CORES - 1
    far = max(1, sizes[0] * sizes[1] - 1)
    tokens = (frames, width)
    total_rows = (max(8, 2 * width // LANES), LANES)
    scratch = dict(
        held=[pltpu.VMEM(sizes + s, F32 if i == 1 else BF16) for i, s in enumerate(shards)],
        g_local=dma((len(pieces),)),
        g_z=dma((2, len(pieces), z_steps)),
        g_hop=dma((2, len(pieces), 2, 2, wide)),
        g_core=dma((2, len(pieces))),
        t_own=pltpu.VMEM((2,) + total_rows, F32),
        t_mid=pltpu.VMEM((2,) + total_rows, F32),
        t_near=pltpu.VMEM((2, near) + total_rows, F32),
        t_far=pltpu.VMEM((2, far) + total_rows, F32),
        t_sem=dma((2, 2, near + far)),
        packed=pltpu.VMEM((64, LANES), F32),
        small=pltpu.VMEM((64, LANES), BF16),
        point=pltpu.VMEM((stem_point.shape[1], 2 * channels), F32),
        frames_wide=pltpu.VMEM((8 * frames, LANES), F32),
        feats=pltpu.VMEM((9, frames, LANES), F32),
        windows=pltpu.VMEM((GROUPS, 4 * frames, LANES), BF16),
        params=pltpu.VMEM((32, width), F32),
        kernels=pltpu.VMEM((32, channels), F32),
        band_wide=pltpu.VMEM((LANES, channels), F32),
        banded=pltpu.VMEM((LANES, 8 * channels), BF16),
        points=pltpu.VMEM((2, channels, channels), BF16),
        ones_wide=pltpu.VMEM((3, 4 * frames, channels), F32),
        ones=pltpu.VMEM((4, 4 * frames, channels), BF16),
        two_even=pltpu.VMEM((2 * frames, channels), F32),
        two_odd=pltpu.VMEM((2, 2 * frames, channels), F32),
        level_now=pltpu.VMEM((2 * frames, channels), BF16),
        level_two=pltpu.VMEM((bins_two, channels, 2 * frames), BF16),
        point_two=pltpu.VMEM((bins_two, 2 * frames, channels), BF16),
        level_three=pltpu.VMEM((bins_three, channels, frames), BF16),
        point_three=pltpu.VMEM((bins_three, frames, channels), BF16),
        weights=pltpu.VMEM((heads, frames, frames), F32),
        joined=pltpu.VMEM((frames, 3 * width), BF16),
        gated=pltpu.VMEM((frames, 2 * width), F32),
        hidden0=pltpu.VMEM((frames, hidden), BF16),
        hidden1=pltpu.VMEM((frames, hidden), BF16),
        active0=pltpu.VMEM((frames, hidden), BF16),
        active1=pltpu.VMEM((frames, hidden), BF16),
        after_stem=pltpu.VMEM(tokens, F32),
        after_ffn=pltpu.VMEM(tokens, F32),
        after_attn=pltpu.VMEM(tokens, F32),
        after_conv=pltpu.VMEM(tokens, F32),
        after_second=pltpu.VMEM(tokens, F32),
        merged=pltpu.VMEM(tokens, F32),
        depthwise=pltpu.VMEM(tokens, F32),
        standard=pltpu.VMEM(tokens, F32),
        batch_normed=pltpu.VMEM(tokens, F32),
        normed0=pltpu.VMEM(tokens, BF16),
        normed1=pltpu.VMEM(tokens, BF16),
        normed2=pltpu.VMEM(tokens, BF16),
        normed4=pltpu.VMEM(tokens, BF16),
        mixed=pltpu.VMEM(tokens, BF16),
        conv_active=pltpu.VMEM(tokens, BF16),
    )
    outputs = dict(
        activations=(tokens, BF16),
        mel_grad=((bins, 8 * frames), F32),
        grad_kernels=((3, channels // devices, 9), F32),
        grad_point=((2 * channels // devices, channels), F32),
        grad_stem=(stem_out.shape, F32),
        grad_inner=(ffn_in.shape, F32),
        grad_outer=(ffn_out.shape, F32),
        grad_qkv=(qkv.shape, F32),
        grad_attn=(attn_out.shape, F32),
        grad_conv_in=(conv_in.shape, F32),
        grad_depth=(conv_depth.shape, F32),
        grad_conv_out=(conv_out.shape, F32),
        grad_gains=(norm_gains.shape, F32),
        grad_shifts=(norm_shifts.shape, F32),
        grad_final=((1, width // devices), F32),
    )
    grads = [
        types.SimpleNamespace(weight=weight, product=weight > 0, block=block)
        for weight, block in [(weight, shards[weight]) for weight in range(10, 1, -1)]
        + [(0, (2 * channels // devices, channels)), (0, (32, LANES)), (0, (32, LANES))]
    ]
    lead = sizes[:3]
    columns, mates, right, parts, kept, landed, landed_z = {}, {}, {}, {}, {}, {}, {}
    for i, spec in enumerate(grads):
        rows, breadth = spec.block
        if spec.product:
            columns[i] = pltpu.VMEM(sizes + (rows, frames), BF16)
            mates[i] = pltpu.VMEM(lead + (rows, frames), BF16)
            right[i] = pltpu.VMEM((2 * frames, breadth), BF16)
        else:
            parts[i] = pltpu.VMEM(sizes + spec.block, BF16)
            kept[i] = pltpu.VMEM(lead + spec.block, BF16)
            mates[i] = pltpu.VMEM(lead + spec.block, BF16)
    sums = []
    for i, spec in enumerate(grads):
        large = spec.block[0] * spec.block[1] >= 2**14 + 2**12 and spec.block[1] % (4 * LANES) == 0
        sums += cut(i, spec.block[1], 2 if large else 1)
    for p, (i, _, breadth) in enumerate(sums):
        rows = grads[i].block[0]
        split = 2 if breadth // 2 % LANES == 0 else 1
        part = (rows, breadth // split)
        landed[p] = []
        for order in range(split):
            one, two = (1, 0) if order == 0 else (0, 1)
            steps = (max(1, sizes[one] - 1), max(1, sizes[two] - 1))
            landed[p].append(
                [
                    pltpu.VMEM((steps[0], sizes[two], sizes[2]) + part, BF16),
                    pltpu.VMEM((steps[1], sizes[2]) + part, BF16),
                ]
            )
        landed_z[p] = pltpu.VMEM((z_steps, rows, breadth), BF16)
    scratch |= dict(
        columns=columns,
        mates=mates,
        right=right,
        parts=parts,
        kept=kept,
        landed=landed,
        landed_z=landed_z,
        s_core=dma((2, len(grads), 2)),
        s_hop=dma((2, len(sums), 2, 2, wide)),
        s_z=dma((2, len(sums), z_steps)),
        stem_hidden=pltpu.VMEM((frames, bins_three * channels), BF16),
        sum_wide=pltpu.VMEM((32, LANES), F32),
        sum_taps=pltpu.VMEM((32, LANES), F32),
        d_params=pltpu.VMEM((32, width), F32),
        d_taps=pltpu.VMEM((32, channels), F32),
        stream=pltpu.VMEM(tokens, F32),
        grad_batch=pltpu.VMEM(tokens, F32),
        g_mixed=pltpu.VMEM(tokens, BF16),
        g_three=pltpu.VMEM((frames, bins_three * channels), BF16),
        g_two=pltpu.VMEM((2, 2 * frames, channels), BF16),
        g_one=pltpu.VMEM((4 * frames, 4 * channels), BF16),
        d_three=pltpu.VMEM((2, 2 * frames, channels), F32),
        d_two_even=pltpu.VMEM((2, 3 * frames, channels), BF16),
        d_two_odd=pltpu.VMEM((3 * frames, channels), BF16),
        d_kernels=pltpu.VMEM((27, 8, channels), F32),
        d_points=pltpu.VMEM((2, channels, channels), F32),
        d_windows=pltpu.VMEM((GROUPS, 4 * frames, LANES), F32),
        d_banded=pltpu.VMEM((LANES, 8 * channels), F32),
        window_turned=pltpu.VMEM((LANES, 4 * frames), BF16),
    )
    plan = types.SimpleNamespace(
        sizes=sizes,
        frames=frames,
        bins=bins,
        count=count,
        width=width,
        channels=channels,
        heads=heads,
        radius=conv_depth.shape[0] // 2,
        time_masks=time_spans.shape[1],
        freq_masks=freq_spans.shape[1],
        sources=gather_sources,
        grads=grads,
        pieces=pieces,
        turns=turns,
        sums=sums,
        steps=order_of_steps(sums, grads),
        small_moment=SMALL_MOMENT,
    )
    kinds = ({name: 0 for name in inputs}, {name: 0 for name in outputs}, scratch)
    plan.trees = [jax.tree.structure(kind) for kind in kinds]
    results = pl.pallas_call(
        functools.partial(layer_kernel, plan),
        out_shape=[jax.ShapeDtypeStruct(*spec) for _, spec in sorted(outputs.items())],
        in_specs=[pl.BlockSpec(memory_space=space) for _, (_, space) in sorted(inputs.items())],
        out_specs=[pl.BlockSpec(memory_space=pltpu.VMEM)] * len(outputs),
        scratch_shapes=jax.tree.leaves(scratch),
        compiler_params=pltpu.CompilerParams(
            collective_id=0, has_side_effects=True, vmem_limit_bytes=63 * 2**20
        ),
        name="layer",
    )(*[value for _, (value, _) in sorted(inputs.items())])
    made = types.SimpleNamespace(**dict(zip(sorted(outputs), results)))
    finals = [
        (made.mel_grad, made.mel_grad.shape),
        (made.activations, tokens),
        (made.grad_kernels, made.grad_kernels.shape),
        (made.grad_point, made.grad_point.shape),
        (made.grad_stem, stem_out.shape),
        (made.grad_inner, ffn_in.shape),
        (made.grad_outer, ffn_out.shape),
        (made.grad_qkv, qkv.shape),
        (made.grad_attn, attn_out.shape),
        (made.grad_conv_in, conv_in.shape),
        (made.grad_depth, conv_depth.shape),
        (made.grad_conv_out, conv_out.shape),
        (made.grad_gains, norm_gains.shape),
        (made.grad_shifts, norm_shifts.shape),
        (made.grad_final, made.grad_final.shape),
    ]
    done = pl.pallas_call(
        functools.partial(finish_kernel, len(finals)),
        out_shape=[jax.ShapeDtypeStruct(shape, value.dtype) for value, shape in finals],
        in_specs=[pl.BlockSpec(memory_space=pltpu.VMEM)] * len(finals),
        out_specs=[pl.BlockSpec(memory_space=pltpu.VMEM)] * len(finals),
        name="finish",
    )(*[value for value, _ in finals])
    return (
        done[1],
        done[0].T,
        done[2].swapaxes(1, 2),
        done[3].reshape(stem_point.shape),
        *done[4:14],
        done[14].reshape(final_shift.shape),
    )


def solution(mesh):
    return jax.shard_map(
        local,
        mesh=mesh,
        in_specs=(
            P(AXES, None),
            P(AXES, None),
            P(),
            P(),
            P(AXES, None, None),
            P(AXES, None, None),
            P(),
            P(None, None, AXES),
            P(None, AXES, None),
            P(AXES, None),
            P(None, AXES, None),
            P(None, AXES, None),
            P(AXES, None),
            P(AXES, None),
            P(AXES, None),
            P(None, AXES),
            P(AXES, None),
            P(None, AXES),
            P(None, AXES),
            P(AXES),
        ),
        out_specs=(
            P(AXES, None),
            P(AXES, None),
            P(None, None, AXES),
            P(None, AXES, None),
            P(AXES, None),
            P(None, AXES, None),
            P(None, AXES, None),
            P(AXES, None),
            P(AXES, None),
            P(AXES, None),
            P(None, AXES),
            P(AXES, None),
            P(None, AXES),
            P(None, AXES),
            P(AXES),
        ),
        check_vma=False,
    )
```

```python
import functools
import types

import jax
import jax.numpy as jnp
from jax import lax
from jax.experimental import pallas as pl
from jax.experimental.pallas import tpu as pltpu
from jax.sharding import PartitionSpec as P

CTX = 128


EPSILON = 1e-05
MASKED_LOGIT = -1e30
MESH = pl.DeviceIdType.MESH
CORES = 2
AXES = ("dp", "fsdp")
LANES = 128
BINS = 24
GROUPS = 5
TILE = 16
PART = 32
F32 = jnp.float32
BF16 = jnp.bfloat16


def grid_sizes():
    dp, fsdp = lax.axis_size(AXES[0]), lax.axis_size(AXES[1])
    high = 2 if dp % 2 == 0 else 1
    return (high, dp // high, fsdp // CORES, CORES)


def own_place(sizes):
    dp, fsdp = lax.axis_index(AXES[0]), lax.axis_index(AXES[1])
    return (dp // sizes[1], dp % sizes[1], fsdp // CORES, fsdp % CORES)


def peer_on(place, sizes, digit, step):
    other = list(place)
    other[digit] = (place[digit] + step) % sizes[digit]
    return tuple(other)


def device_of(place, sizes):
    return (place[0] * sizes[1] + place[1], place[2] * CORES + place[3])


def send(src, dst, device, send_sem, recv_sem):
    copy = pltpu.make_async_remote_copy(
        src_ref=src,
        dst_ref=dst,
        send_sem=send_sem,
        recv_sem=recv_sem,
        device_id=device,
        device_id_type=MESH,
    )
    copy.start()
    return copy


def group_peers(sizes):
    dp, fsdp = lax.axis_index(AXES[0]), lax.axis_index(AXES[1])
    dp_size, fsdp_size = sizes[0] * sizes[1], sizes[2] * CORES
    near = [(dp, (fsdp + step) % fsdp_size) for step in range(1, fsdp_size)]
    far = [((dp + step) % dp_size, fsdp) for step in range(1, dp_size)]
    return near, far


def greet(sizes):
    near, far = group_peers(sizes)
    for device in near + far:
        pl.semaphore_signal(
            pltpu.get_barrier_semaphore(), inc=1, device_id=device, device_id_type=MESH
        )


def await_greetings(sizes):
    near, far = group_peers(sizes)
    pl.semaphore_wait(pltpu.get_barrier_semaphore(), len(near) + len(far))


def iota(shape, axis):
    return lax.broadcasted_iota(jnp.int32, shape, axis)


def flags(condition):
    return jnp.where(condition, 1.0, 0.0)


def mm(left, right):
    return jnp.dot(left, right, preferred_element_type=F32)


def mm_t(left, right):
    return lax.dot_general(left, right, (((1,), (1,)), ((), ())), preferred_element_type=F32)


def rows_of(value):
    return value.reshape(-1, value.shape[-1])


def sigmoid(value):
    return 0.5 + 0.5 * jnp.tanh(0.5 * value)


def silu(value):
    half = 0.5 * value
    return half + half * jnp.tanh(half)


def silu_and_slope(value):
    gate = sigmoid(value)
    out = value * gate
    return out, gate + out * (1.0 - gate)


def normalized(value):
    centred = value - jnp.mean(value, axis=-1, keepdims=True)
    scale = lax.rsqrt(jnp.mean(centred * centred, axis=-1, keepdims=True) + EPSILON)
    return centred * scale, scale


def layer_norm(value, gain, shift):
    return normalized(value)[0] * gain + shift


def layer_norm_back(value, gain, grad):
    unit, scale = normalized(value)
    inner = grad * gain
    centre = jnp.mean(inner, axis=-1, keepdims=True)
    along = jnp.mean(inner * unit, axis=-1, keepdims=True)
    grad_value = scale * (inner - centre - unit * along)
    return grad_value, column_sum(grad * unit), column_sum(grad)


def column_sum(value):
    return jnp.sum(value, axis=0, keepdims=True)


def shift_rows(value, step):
    rows = value.shape[0]
    step = step % rows
    return value if step == 0 else pltpu.roll(value, step, 0)


TAP_ROW, GAIN_ROW, SHIFT_ROW, FINAL_ROW = 0, 9, 15, 20


def layer_kernel(plan, *refs):
    fields, at = {}, 0
    for tree in plan.trees:
        fields |= tree.unflatten(refs[at : at + tree.num_leaves])
        at += tree.num_leaves
    v = types.SimpleNamespace(**fields)
    sizes, frames, bins = plan.sizes, plan.frames, plan.bins
    place = own_place(sizes)
    a, b, z, c = place
    mate = device_of(peer_on(place, sizes, 3, 1), sizes)
    device = lax.axis_index(AXES[0]) * (sizes[2] * CORES) + lax.axis_index(AXES[1])
    count = plan.count
    pending = []

    def arrive(copies):
        for copy in copies:
            copy.wait_recv()
        pending.extend(copies)


    sources = plan.sources(v)
    held = v.held
    opened, first, second, third = {}, {}, {}, {}

    def halves(start, width):
        half = width // 2
        if half % LANES:
            return (pl.ds(start, width),)
        return (pl.ds(start, half), pl.ds(start + half, half))

    def open_piece(p):
        item, start, width = plan.pieces[p]
        lanes = pl.ds(start, width)
        source, own = sources[item].at[:, lanes], held[item].at[a, b, z, c, :, lanes]
        keep = pltpu.make_async_copy(source, own, v.g_local.at[p])
        keep.start()
        opened[p] = (
            keep,
            [
                send(
                    source,
                    own,
                    device_of(peer_on(place, sizes, 2, step), sizes),
                    v.g_z.at[0, p, step - 1],
                    v.g_z.at[1, p, step - 1],
                )
                for step in range(1, sizes[2])
            ],
        )

    def hop_piece(p, hop):
        item, start, width = plan.pieces[p]
        copies = []
        for order, lanes in enumerate(halves(start, width)):
            digit = 1 - order if hop == 0 else order
            if hop == 0:
                part = held[item].at[a, b, :, c, :, lanes]
            elif order == 0:
                part = held[item].at[a, :, :, c, :, lanes]
            else:
                part = held[item].at[:, b, :, c, :, lanes]
            for step in range(1, sizes[digit]):
                copies.append(
                    send(
                        part,
                        part,
                        device_of(peer_on(place, sizes, digit, step), sizes),
                        v.g_hop.at[0, p, hop, order, step - 1],
                        v.g_hop.at[1, p, hop, order, step - 1],
                    )
                )
        return copies

    state = types.SimpleNamespace(turn=0)
    turns = plan.turns

    def pieces_at(at):
        return turns[at] if 0 <= at < len(turns) else ()

    def turn():
        at = state.turn
        state.turn += 1
        for p in pieces_at(at + 2):
            open_piece(p)
        for p in pieces_at(at):
            opened[p][0].wait()
            arrive(opened[p][1])
            first[p] = hop_piece(p, 0)
        for p in pieces_at(at - 1):
            arrive(first[p])
            second[p] = hop_piece(p, 1)
        for p in pieces_at(at - 2):
            arrive(second[p])
            item, start, width = plan.pieces[p]
            part = held[item].at[:, :, :, c, :, pl.ds(start, width)]
            third[p] = [send(part, part, mate, v.g_core.at[0, p], v.g_core.at[1, p])]
        for p in pieces_at(at - 3):
            arrive(third[p])

    def need(item):
        last = max(
            at for at, ps in enumerate(turns) for p in ps if plan.pieces[p][0] == item
        )
        while state.turn < last + 4:
            turn()

    greet(sizes)
    v.packed[...] = jnp.zeros(v.packed.shape, F32)
    for row, piece in (
        (TAP_ROW, v.conv_depth),
        (GAIN_ROW, v.norm_gains),
        (SHIFT_ROW, v.norm_shifts),
        (FINAL_ROW, v.final_shift),
    ):
        v.packed[row : row + piece.shape[0], : piece.shape[1]] = piece[...].astype(F32)
    for layer in range(3):
        row = 32 + 9 * layer
        v.packed[row : row + 9, : v.stem_kernels.shape[1]] = v.stem_kernels[layer].astype(F32).T
    v.small[...] = v.packed[...].astype(BF16)
    for layer in range(2):
        at = layer * plan.channels
        v.point[:, at : at + plan.channels] = v.stem_point[layer].astype(F32)
    await_greetings(sizes)
    for at in range(2):
        for p in pieces_at(at):
            open_piece(p)


    own_len = jnp.where(v.assignment[...] == device, v.lengths[...], 0)
    utterances = own_len.shape[1]
    upto = flags(
        iota((utterances, utterances), 0) <= iota((utterances, utterances), 1)
    ).astype(BF16)
    own_low = jnp.broadcast_to(own_len.astype(F32), (TILE, utterances)).astype(BF16)
    finish = mm(own_low, upto)[:1]
    begin = finish - own_len.astype(F32)
    at_frame = iota((frames, utterances), 0).astype(F32)
    inside = flags((at_frame >= begin) & (at_frame < finish))
    same = mm_t(inside.astype(BF16), inside.astype(BF16))
    present = jnp.sum(inside, axis=1, keepdims=True)
    ahead = iota((frames, frames), 1) - iota((frames, frames), 0)

    def same_at(step):
        return jnp.sum(jnp.where(ahead == step, same, 0.0), axis=1, keepdims=True)

    joint = same_at(-1)
    counted = jnp.sum(v.lengths[...].astype(F32), axis=1, keepdims=True)


    bin_at = iota((1, LANES), 1)
    bin_keep = bin_at < bins
    for mask in range(plan.freq_masks):
        start, width = v.freq_spans[0, mask, 0], v.freq_spans[0, mask, 1]
        bin_keep = bin_keep & jnp.logical_not((bin_at >= start) & (bin_at < start + width))
    bin_keep = flags(bin_keep)

    def keep_of(phase):
        at = iota((frames, 1), 0) * 8 + phase
        keep = present
        for mask in range(plan.time_masks):
            start, width = v.time_spans[0, mask, 0], v.time_spans[0, mask, 1]
            keep = jnp.where((at >= start) & (at < start + width), 0.0, keep)
        return keep * bin_keep

    for phase in range(8):
        at = pl.ds(phase * frames, frames)
        v.frames_wide[at, :bins] = v.mel[:, at].astype(F32).T
    for phase in range(8):
        masked = jnp.where(
            keep_of(phase) > 0.5, v.frames_wide[pl.ds(phase, frames, stride=8), :], 0.0
        )
        v.feats[phase + 1] = masked
        if phase == 7:
            v.feats[0] = shift_rows(masked, 1) * joint
    lane = iota((1, LANES), 1)

    def band(tap):
        return (lane >= BINS * tap) & (lane < BINS * tap + 17)

    for group in range(GROUPS):
        if group % 2 == 0:
            turn()
        for phase in range(4):
            total = jnp.zeros((frames, LANES), F32)
            for tap in range(3):
                moved = pltpu.roll(
                    v.feats[2 * phase + tap], (BINS * tap - 16 * group + 1) % LANES, 1
                )
                total = jnp.where(band(tap), moved, total)
            v.windows[group, pl.ds(phase * frames, frames)] = total.astype(BF16)


    need(0)
    devices = sizes[0] * sizes[1] * sizes[2] * CORES

    def spread(rows, width, target):
        each = width // devices
        per_tile = LANES // each
        for tile in range(width // LANES):
            total = jnp.zeros((32, LANES), F32)
            for k in range(per_tile):
                d = tile * per_tile + k
                index = (
                    d // (sizes[1] * sizes[2] * CORES),
                    d // (sizes[2] * CORES) % sizes[1],
                    d // CORES % sizes[2],
                    d % CORES,
                )
                piece = held[0][index][rows : rows + 32].astype(F32)
                total = total + (pltpu.roll(piece, each * k, 1) if k else piece)
            target[:, tile * LANES : (tile + 1) * LANES] = total

    width = plan.width
    channels = plan.channels
    spread(0, width, v.params)
    spread(32, channels, v.kernels)

    def param(row):
        return v.params[row : row + 1]

    def kernel_row(layer, tap, lanes):
        return v.kernels[9 * layer + tap : 9 * layer + tap + 1, lanes]

    every = pl.ds(0, channels)
    for f in range(8):
        v.band_wide[...] = jnp.zeros((LANES, channels), F32)
        for tap in range(9):
            row = BINS * (tap // 3) + 2 * f + tap % 3
            v.band_wide[row : row + 1] = kernel_row(0, tap, every)
        v.banded[:, f * channels : (f + 1) * channels] = v.band_wide[...].astype(BF16)

    need(1)
    point = held[1][...]
    point = point.reshape(-1, point.shape[-1])
    v.points[0] = point[:, :channels].astype(BF16)
    v.points[1] = point[:, channels:].astype(BF16)

    def wide_chunks(extent):
        step = min(extent, 4 * LANES)
        return [slice(start, start + step) for start in range(0, extent, step)]


    grads = plan.grads
    left_sent = {}
    OUTER1, INNER1, CONV_OUT, CONV_IN, ATTN, QKV, OUTER0, INNER0, STEM, POINT, WIDE, TAPS = range(12)

    def transposed(value):
        return jnp.transpose(value.astype(F32)).astype(BF16)

    def start_left(i, left):
        columns = v.columns[i]
        per_part = left.shape[1] // (sizes[0] * sizes[1])
        for high in range(sizes[0]):
            for low in range(sizes[1]):
                start = (high * sizes[1] + low) * per_part
                part = transposed(left[:, start : start + per_part])
                columns[high, low] = part.reshape(columns.shape[2:])
        left_sent[i] = [
            send(
                columns.at[:, :, :, 1 - c],
                v.mates[i],
                mate,
                v.s_core.at[0, i, 0],
                v.s_core.at[1, i, 0],
            )
        ]


    def phase_rows(ref, phase, lanes):
        return ref[pl.ds(phase * frames, frames), lanes]

    chunks = [pl.ds(LANES * k, LANES) for k in range(channels // LANES)]
    v.ones_wide[2] = jnp.zeros(v.ones_wide.shape[1:], F32)
    v.two_odd[1] = jnp.zeros(v.two_odd.shape[1:], F32)

    def stem_step(group, half):
        three = 2 * group + half
        for side in range(2):
            two = 2 * three + side
            low = 4 * half + 2 * side
            window = v.windows[group]
            for f, slot in ((0, 0), (1, 1 + side)):
                at = pl.multiple_of((low + f) * channels, channels)
                value = silu(mm(window, v.banded[:, pl.ds(at, channels)]))
                v.ones_wide[slot] = value
            pieces = (v.ones_wide.at[2 - side], v.ones_wide.at[0], v.ones_wide.at[1 + side])
            for lanes in chunks:
                late = early = odd = None
                for column, piece in enumerate(pieces):
                    w0, w1, w2 = (kernel_row(1, 3 * row + column, lanes) for row in range(3))
                    p0, p1, p2, p3 = (phase_rows(piece, phase, lanes) for phase in range(4))
                    carried = w0 * p3
                    even = w1 * p0 + w2 * p1
                    after = w0 * p1 + w1 * p2 + w2 * p3
                    late = carried if late is None else late + carried
                    early = even if early is None else early + even
                    odd = after if odd is None else odd + after
                early = early + shift_rows(late, 1) * joint
                v.level_now[pl.ds(0, frames), lanes] = early.astype(BF16)
                v.level_now[pl.ds(frames, frames), lanes] = odd.astype(BF16)
            v.level_two[two] = transposed(v.level_now[...])
            point_two = mm(v.level_now[...], v.points[0])
            v.point_two[two] = point_two.astype(BF16)
            hidden = silu(point_two)
            if side == 0:
                v.two_even[...] = hidden
            else:
                v.two_odd[half] = hidden
        pieces = (v.two_odd.at[1 - half], v.two_even, v.two_odd.at[half])
        for lanes in chunks:
            late = total = None
            for column, piece in enumerate(pieces):
                w0, w1, w2 = (kernel_row(2, 3 * row + column, lanes) for row in range(3))
                p0, p1 = (phase_rows(piece, phase, lanes) for phase in range(2))
                carried = w0 * p1
                now = w1 * p0 + w2 * p1
                late = carried if late is None else late + carried
                total = now if total is None else total + now
            total = total + shift_rows(late, 1) * joint
            v.level_now[pl.ds(0, frames), lanes] = total.astype(BF16)
        level_three = v.level_now[pl.ds(0, frames)]
        v.level_three[three] = transposed(level_three)
        point_three = mm(level_three, v.points[1])
        v.point_three[three] = point_three.astype(BF16)
        at = pl.multiple_of(three * channels, channels)
        v.stem_hidden[:, pl.ds(at, channels)] = silu(point_three).astype(BF16)

    for group in range(GROUPS):
        lax.fori_loop(0, 2, lambda half, carry: (stem_step(group, half), carry)[1], 0)
        turn()

    bins_three = 2 * GROUPS


    start_left(STEM, v.stem_hidden)
    need(2)
    v.after_stem[...] = mm(v.stem_hidden[...], rows_of(held[2][...]))

    def ffn(stream, row, inner, outer, normed_ref, hidden_ref, active_ref, items):
        normed_ref[...] = layer_norm(stream, param(GAIN_ROW + row), param(SHIFT_ROW + row)).astype(BF16)
        start_left(items[0], normed_ref)
        need(inner)
        for lanes in wide_chunks(hidden_ref.shape[1]):
            hidden = mm(normed_ref[...], rows_of(held[inner][:, :, :, :, :, lanes]))
            hidden_ref[:, lanes] = hidden.astype(BF16)
            active_ref[:, lanes] = silu(hidden).astype(BF16)
        start_left(items[1], active_ref)
        need(outer)
        return mm(active_ref[...], rows_of(held[outer][...]))

    v.after_ffn[...] = v.after_stem[...] + 0.5 * ffn(
        v.after_stem[...], 0, 3, 4, v.normed0, v.hidden0, v.active0, (INNER0, OUTER0)
    )
    v.normed1[...] = layer_norm(
        v.after_ffn[...], param(GAIN_ROW + 1), param(SHIFT_ROW + 1)
    ).astype(BF16)
    start_left(QKV, v.normed1)
    need(5)
    for lanes in wide_chunks(3 * width):
        v.joined[:, lanes] = mm(v.normed1[...], rows_of(held[5][:, :, :, :, :, lanes])).astype(BF16)
    heads = plan.heads
    per_tile = LANES * heads // width
    head_width = width // heads
    apart = jnp.abs(ahead)

    def head_lanes(head):
        inner = head % per_tile
        return (lane >= inner * head_width) & (lane < (inner + 1) * head_width)

    def tile_of(ref, part, head):
        start = part * width + head // per_tile * LANES
        return ref[:, start : start + LANES]

    def only(value, head):
        return jnp.where(head_lanes(head), value.astype(F32), 0.0).astype(BF16)

    for tile in range(width // LANES):
        mixed = jnp.zeros((frames, LANES), F32)
        for head in range(tile * per_tile, (tile + 1) * per_tile):
            scores = mm_t(only(tile_of(v.joined, 0, head), head), tile_of(v.joined, 1, head))
            allowed = (same > 0.5) & (apart <= v.contexts[head])
            logits = jnp.where(allowed, scores * head_width ** (-0.5), MASKED_LOGIT)
            exponent = jnp.exp(logits - jnp.max(logits, axis=-1, keepdims=True))
            weights = exponent / jnp.sum(exponent, axis=-1, keepdims=True)
            v.weights[head] = weights
            out = mm(weights.astype(BF16), tile_of(v.joined, 2, head))
            mixed = jnp.where(head_lanes(head), out, mixed)
        v.mixed[:, tile * LANES : (tile + 1) * LANES] = mixed.astype(BF16)
    start_left(ATTN, v.mixed)
    need(6)
    v.after_attn[...] = v.after_ffn[...] + mm(v.mixed[...], rows_of(held[6][...]))
    v.normed2[...] = layer_norm(
        v.after_attn[...], param(GAIN_ROW + 2), param(SHIFT_ROW + 2)
    ).astype(BF16)
    start_left(CONV_IN, v.normed2)
    need(7)
    for lanes in wide_chunks(2 * width):
        v.gated[:, lanes] = mm(v.normed2[...], rows_of(held[7][:, :, :, :, :, lanes]))
    radius = plan.radius
    merged = v.gated[:, :width] * sigmoid(v.gated[:, width:])
    v.merged[...] = merged
    depthwise = jnp.zeros((frames, width), F32)
    for tap in range(2 * radius + 1):
        step = tap - radius
        depthwise = depthwise + shift_rows(merged, -step) * same_at(step) * param(TAP_ROW + tap)
    v.depthwise[...] = depthwise

    near, far = group_peers(sizes)
    blocks = width // LANES

    def open_total(which, rows):
        for row, value in enumerate(rows):
            for k in range(blocks):
                at = row * blocks + k
                v.t_own[which, at : at + 1] = value[:, k * LANES : (k + 1) * LANES]
        return [
            send(
                v.t_own.at[which],
                v.t_near.at[which, k],
                peer,
                v.t_sem.at[0, which, k],
                v.t_sem.at[1, which, k],
            )
            for k, peer in enumerate(near)
        ]

    def close_total(which, copies):
        arrive(copies)
        total = v.t_own[which]
        for k in range(len(near)):
            total = total + v.t_near[which, k]
        v.t_mid[which] = total
        copies = [
            send(
                v.t_mid.at[which],
                v.t_far.at[which, k],
                peer,
                v.t_sem.at[0, which, len(near) + k],
                v.t_sem.at[1, which, len(near) + k],
            )
            for k, peer in enumerate(far)
        ]
        arrive(copies)
        for k in range(len(far)):
            total = total + v.t_far[which, k]
        return [
            jnp.concatenate(
                [total[row * blocks + k : row * blocks + k + 1] for k in range(blocks)], axis=1
            )
            for row in range(2)
        ]

    counts = open_total(
        0, [column_sum(depthwise * present), column_sum(depthwise * depthwise * present)]
    )
    turn()
    first_sum, second_sum = close_total(0, counts)
    average = first_sum / counted
    spread_out = second_sum / counted - average * average
    inv_spread = lax.rsqrt(spread_out + EPSILON)
    v.standard[...] = (v.depthwise[...] - average) * inv_spread
    v.batch_normed[...] = v.standard[...] * param(GAIN_ROW + 3) + param(SHIFT_ROW + 3)
    v.conv_active[...] = silu(v.batch_normed[...]).astype(BF16)
    start_left(CONV_OUT, v.conv_active)
    need(8)
    v.after_conv[...] = v.after_attn[...] + mm(v.conv_active[...], rows_of(held[8][...]))
    v.after_second[...] = v.after_conv[...] + 0.5 * ffn(
        v.after_conv[...], 4, 9, 10, v.normed4, v.hidden1, v.active1, (INNER1, OUTER1)
    )
    gain_last, shift_last = param(GAIN_ROW + 5), param(FINAL_ROW)
    v.activations[...] = (
        layer_norm(v.after_second[...], gain_last, shift_last) * present
    ).astype(BF16)


    need(count - 1)
    for copy in pending:
        copy.wait_send()
    pending.clear()
    core_sent, hop_one, hop_two, z_sent = {}, {}, {}, {}
    sums = plan.sums

    def block_of(i):
        spec = grads[i]
        return held[spec.weight].at[:, :, :, 0] if spec.weight else v.kept[i]

    def right_of(i):
        return v.right[i].at[pl.ds(0, frames)]

    def start_product(i):
        core_sent[i] = left_sent[i] + [
            send(
                right_of(i),
                v.right[i].at[pl.ds(frames, frames)],
                mate,
                v.s_core.at[0, i, 1],
                v.s_core.at[1, i, 1],
            ),
        ]

    def start_sum(i):
        core_sent[i] = [
            send(
                v.parts[i].at[:, :, :, 1 - c],
                v.mates[i],
                mate,
                v.s_core.at[0, i, 0],
                v.s_core.at[1, i, 0],
            )
        ]

    def take_product(i):
        spec = grads[i]
        arrive(core_sent[i])
        block = block_of(i)
        if spec.product:
            own, mates, right = v.columns[i], v.mates[i], v.right[i]
            split = spec.block[0] > 2 * TILE
            columns = 2 * LANES
            steps = spec.block[1] // columns
            parts = sizes[0] * (sizes[1] if split else 1)

            def multiply(at, carry):
                part = at // steps
                lanes = pl.ds(pl.multiple_of(at % steps * columns, columns), columns)
                index = (part // sizes[1], part % sizes[1]) if split else (part,)
                middle = (slice(None),) * (3 - len(index))
                left = jnp.concatenate(
                    [rows_of(own[index + middle + (c,)]), rows_of(mates[index])], axis=1
                )
                product = mm(left, right[:, lanes]).astype(BF16)
                target = block.at[index + middle + (slice(None), lanes)]
                target[...] = product.reshape(target.shape)
                return carry

            lax.fori_loop(0, parts * steps, multiply, 0, unroll=2)
        else:
            own = v.parts[i][:, :, :, c].astype(F32)
            block[...] = (own + v.mates[i][...].astype(F32)).astype(BF16)

    def send_hop(p, hop):
        i, start, width = sums[p]
        block = block_of(i)
        copies = []
        for order, lanes in enumerate(halves(start, width)):
            digit = 1 - order if hop == 0 else order
            for step in range(1, sizes[digit]):
                other = peer_on(place, sizes, digit, step)
                if hop == 0:
                    part = block.at[:, other[1]] if order == 0 else block.at[other[0]]
                    part = part.at[:, :, :, lanes]
                else:
                    part = block.at[other[0], b] if order == 0 else block.at[a, other[1]]
                    part = part.at[:, :, lanes]
                copies.append(
                    send(
                        part,
                        v.landed[p][order][hop].at[step - 1],
                        device_of(other, sizes),
                        v.s_hop.at[0, p, hop, order, step - 1],
                        v.s_hop.at[1, p, hop, order, step - 1],
                    )
                )
        return copies

    def add_hop(p, hop):
        i, start, width = sums[p]
        block = block_of(i)
        for order, lanes in enumerate(halves(start, width)):
            digit = 1 - order if hop == 0 else order
            landed = v.landed[p][order][hop]
            if hop == 0:
                mine = block.at[:, b] if order == 0 else block.at[a]
                mine = mine.at[:, :, :, lanes]
            else:
                mine = block.at[a, b].at[:, :, lanes]
            lead = mine.shape[:-2]

            def add(at, carry):
                index = (at,) if len(lead) == 1 else (at // lead[1], at % lead[1])
                total = mine[index].astype(F32)
                for step in range(1, sizes[digit]):
                    total = total + landed[(step - 1,) + index].astype(F32)
                mine[index] = total.astype(BF16)
                return carry

            lax.fori_loop(
                0, lead[0] * (lead[1] if len(lead) > 1 else 1), add, 0, unroll=True
            )

    taken = set()

    def first_hop(p):
        if sums[p][0] not in taken:
            taken.add(sums[p][0])
            take_product(sums[p][0])
        hop_one[p] = send_hop(p, 0)

    def second_hop(p):
        arrive(hop_one[p])
        add_hop(p, 0)
        hop_two[p] = send_hop(p, 1)

    def third_hop(p):
        arrive(hop_two[p])
        add_hop(p, 1)
        i, start, width = sums[p]
        block = block_of(i)
        z_sent[p] = []
        for step in range(1, sizes[2]):
            other = peer_on(place, sizes, 2, step)
            z_sent[p].append(
                send(
                    block.at[a, b, other[2], :, pl.ds(start, width)],
                    v.landed_z[p].at[step - 1],
                    device_of(other, sizes),
                    v.s_z.at[0, p, step - 1],
                    v.s_z.at[1, p, step - 1],
                )
            )

    owned = (
        v.grad_outer.at[1],
        v.grad_inner.at[1],
        v.grad_conv_out,
        v.grad_conv_in,
        v.grad_attn,
        v.grad_qkv,
        v.grad_outer.at[0],
        v.grad_inner.at[0],
        v.grad_stem,
        v.grad_point,
        v.sum_wide,
        v.sum_taps,
    )

    def finish_sum(p):
        arrive(z_sent[p])
        i, start, width = sums[p]
        lanes = pl.ds(start, width)
        total = block_of(i)[a, b, z, :, lanes].astype(F32)
        for step in range(1, sizes[2]):
            total = total + v.landed_z[p][step - 1].astype(F32)
        owned[i][:, lanes] = total

    stages = (first_hop, second_hop, third_hop, finish_sum)
    progress = types.SimpleNamespace(at=0)

    def advance(moment):
        while progress.at < len(plan.steps) and plan.steps[progress.at][0] <= moment:
            _, stage, p = plan.steps[progress.at]
            stages[stage](p)
            progress.at += 1

    def add_param(row, value):
        v.d_params[row : row + 1] = value

    v.d_params[...] = jnp.zeros(v.d_params.shape, F32)

    grad = v.cotangent[...].astype(F32) * present
    grad_stream, gain_part, shift_part = layer_norm_back(v.after_second[...], gain_last, grad)
    add_param(GAIN_ROW + 5, gain_part)
    add_param(FINAL_ROW, shift_part)
    v.stream[...] = grad_stream

    def norm_back(row, value_ref, grad_normed):
        grad_value, gain_part, shift_part = layer_norm_back(
            value_ref[...], param(GAIN_ROW + row), grad_normed
        )
        add_param(GAIN_ROW + row, gain_part)
        add_param(SHIFT_ROW + row, shift_part)
        v.stream[...] = v.stream[...] + grad_value

    def ffn_back(row, stream_ref, inner, outer, hidden, items):
        out_grad, hidden_grad = right_of(items[0]), right_of(items[1])
        out_grad[...] = (0.5 * v.stream[...]).astype(BF16)
        start_product(items[0])
        start = 0
        for high in range(sizes[0]):
            for low in range(sizes[1]):
                rows = rows_of(held[outer][high, low])
                lanes = slice(start, start + rows.shape[0])
                start += rows.shape[0]
                slope = silu_and_slope(hidden[:, lanes].astype(F32))[1]
                hidden_grad[:, lanes] = (mm_t(out_grad[...], rows) * slope).astype(BF16)
        start_product(items[1])
        norm_back(row, stream_ref, mm_t(hidden_grad[...], rows_of(held[inner][...])))

    ffn_back(
        4,
        v.after_conv,
        9,
        10,
        v.hidden1,
        (OUTER1, INNER1),
    )
    right_of(CONV_OUT)[...] = v.stream[...].astype(BF16)
    start_product(CONV_OUT)
    grad_active = mm_t(right_of(CONV_OUT)[...], rows_of(held[8][...]))
    grad_batch = grad_active * silu_and_slope(v.batch_normed[...])[1] * present
    v.grad_batch[...] = grad_batch
    beta_own = column_sum(grad_batch)
    gamma_own = column_sum(grad_batch * v.standard[...])
    add_param(GAIN_ROW + 3, gamma_own)
    add_param(SHIFT_ROW + 3, beta_own)
    totals = open_total(1, [beta_own, gamma_own])
    advance(1)
    beta_sum, gamma_sum = close_total(1, totals)
    bn_gain = param(GAIN_ROW + 3)
    grad_first = (
        inv_spread * inv_spread * bn_gain * gamma_sum * average - inv_spread * bn_gain * beta_sum
    ) / counted
    grad_second = -0.5 * inv_spread * inv_spread * bn_gain * gamma_sum / counted
    grad_depth = bn_gain * inv_spread * v.grad_batch[...] + present * (
        grad_first + 2.0 * v.depthwise[...] * grad_second
    )
    grad_merged = jnp.zeros((frames, width), F32)
    for tap in range(2 * radius + 1):
        step = tap - radius
        part = grad_depth * same_at(step)
        add_param(TAP_ROW + tap, column_sum(part * shift_rows(v.merged[...], -step)))
        grad_merged = grad_merged + shift_rows(part, step) * param(TAP_ROW + tap)
    gate = sigmoid(v.gated[:, width:])
    right_of(CONV_IN)[:, :width] = (grad_merged * gate).astype(BF16)
    right_of(CONV_IN)[:, width:] = (grad_merged * v.merged[...] * (1.0 - gate)).astype(BF16)
    start_product(CONV_IN)
    norm_back(2, v.after_attn, mm_t(right_of(CONV_IN)[...], rows_of(held[7][...])))

    right_of(ATTN)[...] = v.stream[...].astype(BF16)
    start_product(ATTN)
    v.g_mixed[...] = mm_t(right_of(ATTN)[...], rows_of(held[6][...])).astype(BF16)
    for tile in range(width // LANES):
        advance(10 + tile)
        parts = [jnp.zeros((frames, LANES), F32) for _ in range(3)]
        mixed_grad = v.g_mixed[:, tile * LANES : (tile + 1) * LANES]
        for head in range(tile * per_tile, (tile + 1) * per_tile):
            weights = v.weights[head]
            grad_weights = mm_t(only(mixed_grad, head), tile_of(v.joined, 2, head))
            row_dot = jnp.sum(weights * grad_weights, axis=-1, keepdims=True)
            grad_scores = weights * (grad_weights - row_dot) * head_width ** (-0.5)
            pieces = (
                mm(grad_scores.astype(BF16), tile_of(v.joined, 1, head)),
                mm(transposed(grad_scores), tile_of(v.joined, 0, head)),
                mm(transposed(weights), mixed_grad),
            )
            parts = [
                jnp.where(head_lanes(head), piece, part) for piece, part in zip(pieces, parts)
            ]
        for k, part in enumerate(parts):
            start = k * width + tile * LANES
            right_of(QKV)[:, start : start + LANES] = part.astype(BF16)
    start_product(QKV)
    norm_back(1, v.after_ffn, mm_t(right_of(QKV)[...], rows_of(held[5][...])))
    ffn_back(
        0,
        v.after_stem,
        3,
        4,
        v.hidden0,
        (OUTER0, INNER0),
    )
    advance(15)
    right_of(STEM)[...] = v.stream[...].astype(BF16)
    start_product(STEM)
    start = 0
    for high in range(sizes[0]):
        for low in range(sizes[1]):
            rows = rows_of(held[2][high, low])
            lanes = slice(start, start + rows.shape[0])
            start += rows.shape[0]
            v.g_three[:, lanes] = mm_t(right_of(STEM)[...], rows).astype(BF16)
    def gather_columns(i, source, width):
        each = width // devices
        for d in range(devices):
            index = (
                d // (sizes[1] * sizes[2] * CORES),
                d // (sizes[2] * CORES) % sizes[1],
                d // CORES % sizes[2],
                d % CORES,
            )
            tile, k = d * each // LANES, d * each % LANES
            piece = source[:, tile * LANES : (tile + 1) * LANES]
            piece = pltpu.roll(piece, LANES - k, 1) if k else piece
            v.parts[i][index] = jnp.where(lane < each, piece, 0.0).astype(BF16)

    gather_columns(WIDE, v.d_params, width)
    start_sum(WIDE)
    advance(STEM_MOMENT)


    v.d_kernels[...] = jnp.zeros(v.d_kernels.shape, F32)
    v.d_points[...] = jnp.zeros(v.d_points.shape, F32)
    v.d_windows[...] = jnp.zeros(v.d_windows.shape, F32)
    v.d_banded[...] = jnp.zeros(v.d_banded.shape, F32)
    v.d_three[0] = jnp.zeros(v.d_three.shape[1:], F32)
    v.d_two_even[0] = jnp.zeros(v.d_two_even.shape[1:], BF16)

    def add_kernel(layer, tap, lanes, value):
        folded = jnp.sum(value.reshape(-1, 8, LANES), axis=0)
        v.d_kernels[9 * layer + tap, :, lanes] += folded

    def stem_back(group, half, moment):
        three = 2 * group + half
        at = pl.multiple_of(three * channels, channels)
        slope = silu_and_slope(v.point_three[three].astype(F32))[1]
        grad_point = (v.g_three[:, pl.ds(at, channels)].astype(F32) * slope).astype(BF16)
        v.d_points[1] += mm(v.level_three[three], grad_point)
        level_grad = mm_t(grad_point, v.points[1])
        v.d_three[half, pl.ds(0, frames)] = level_grad
        v.d_three[half, pl.ds(frames, frames)] = shift_rows(level_grad * joint, -1)
        here, above = v.d_three.at[half], v.d_three.at[1 - half]
        for lanes in chunks:
            k = [kernel_row(2, tap, lanes) for tap in range(9)]
            d, ds = (phase_rows(here, phase, lanes) for phase in range(2))
            n, ns = (phase_rows(above, phase, lanes) for phase in range(2))
            two = 2 * three
            h0, s0 = silu_and_slope(v.point_two[two, pl.ds(0, frames), lanes].astype(F32))
            h1, s1 = silu_and_slope(v.point_two[two, pl.ds(frames, frames), lanes].astype(F32))
            v.g_two[0, pl.ds(0, frames), lanes] = (k[4] * d * s0).astype(BF16)
            v.g_two[0, pl.ds(frames, frames), lanes] = ((k[7] * d + k[1] * ds) * s1).astype(BF16)
            add_kernel(2, 1, lanes, ds * h1)
            add_kernel(2, 4, lanes, d * h0)
            add_kernel(2, 7, lanes, d * h1)
            two = 2 * three + 1
            h0, s0 = silu_and_slope(v.point_two[two, pl.ds(0, frames), lanes].astype(F32))
            h1, s1 = silu_and_slope(v.point_two[two, pl.ds(frames, frames), lanes].astype(F32))
            v.g_two[1, pl.ds(0, frames), lanes] = ((k[5] * d + k[3] * n) * s0).astype(BF16)
            v.g_two[1, pl.ds(frames, frames), lanes] = (
                (k[8] * d + k[2] * ds + k[6] * n + k[0] * ns) * s1
            ).astype(BF16)
            add_kernel(2, 2, lanes, ds * h1)
            add_kernel(2, 5, lanes, d * h0)
            add_kernel(2, 8, lanes, d * h1)
            add_kernel(2, 0, lanes, ns * h1)
            add_kernel(2, 3, lanes, n * h0)
            add_kernel(2, 6, lanes, n * h1)
        for side in range(2):
            low_grad = v.g_two[side]
            v.d_points[0] += mm(v.level_two[2 * three + side], low_grad)
            level_grad = mm_t(low_grad, v.points[0])
            target = v.d_two_odd if side else v.d_two_even.at[half]
            target[pl.ds(0, 2 * frames)] = level_grad.astype(BF16)
            carried = shift_rows(level_grad[:frames] * joint, -1)
            target[pl.ds(2 * frames, frames)] = carried.astype(BF16)
        advance(moment + STEM_STEP / 3)
        low = 4 * half
        for f in range(4):
            at = (low + f) * channels
            v.ones[f] = mm(v.windows[group], v.banded[:, at : at + channels]).astype(BF16)
        for side in (1, 0):
            here = v.d_two_odd if side else v.d_two_even.at[half]
            above = v.d_two_even.at[1 - half] if side else v.d_two_odd
            for lanes in chunks:
                k = [
                    jnp.broadcast_to(kernel_row(1, tap, lanes), (PART, LANES)).astype(BF16)
                    for tap in range(9)
                ]

                def convolve_back(part, carry, k=k, lanes=lanes, side=side, here=here, above=above):
                    def rows_at(phase):
                        return pl.ds(pl.multiple_of(phase * frames + part * PART, PART), PART)

                    def level_one(f, phase):
                        half_value = v.ones[2 * side + f, rows_at(phase), lanes] * 0.5
                        bend = jnp.tanh(half_value)
                        gate = 0.5 + 0.5 * bend
                        out = half_value + half_value * bend
                        return out, gate + out * (1.0 - gate)

                    def put(f, phase, value):
                        at = pl.multiple_of((2 * side + f) * channels, channels)
                        at = pl.ds(at + lanes.start, LANES)
                        v.g_one[rows_at(phase), at] = value

                    def add(tap, value):
                        value = value.astype(F32).reshape(-1, 8, LANES)
                        v.d_kernels[9 + tap, :, lanes] += jnp.sum(value, axis=0)

                    d0, d1, ds = (here[rows_at(phase), lanes] for phase in range(3))
                    n0, n1, ns = (above[rows_at(phase), lanes] for phase in range(3))
                    h, s = level_one(0, 0)
                    put(0, 0, k[4] * d0 * s)
                    middle = d0 * h
                    h, s = level_one(0, 1)
                    put(0, 1, (k[7] * d0 + k[1] * d1) * s)
                    before, behind = d1 * h, d0 * h
                    h, s = level_one(0, 2)
                    put(0, 2, k[4] * d1 * s)
                    middle = middle + d1 * h
                    h, s = level_one(0, 3)
                    put(0, 3, (k[7] * d1 + k[1] * ds) * s)
                    add(1, before + ds * h)
                    add(4, middle)
                    add(7, behind + d1 * h)
                    h, s = level_one(1, 0)
                    put(1, 0, (k[5] * d0 + k[3] * n0) * s)
                    middle, middle_n = d0 * h, n0 * h
                    h, s = level_one(1, 1)
                    put(1, 1, (k[8] * d0 + k[2] * d1 + k[6] * n0 + k[0] * n1) * s)
                    before, behind = d1 * h, d0 * h
                    before_n, behind_n = n1 * h, n0 * h
                    h, s = level_one(1, 2)
                    put(1, 2, (k[5] * d1 + k[3] * n1) * s)
                    middle, middle_n = middle + d1 * h, middle_n + n1 * h
                    h, s = level_one(1, 3)
                    put(1, 3, (k[8] * d1 + k[2] * ds + k[6] * n1 + k[0] * ns) * s)
                    add(2, before + ds * h)
                    add(5, middle)
                    add(8, behind + d1 * h)
                    add(0, before_n + ns * h)
                    add(3, middle_n)
                    add(6, behind_n + n1 * h)
                    return carry

                lax.fori_loop(0, frames // PART, convolve_back, 0, unroll=True)
            advance(moment + STEM_STEP * (3 - side) / 3)
        at = pl.ds(low * channels, 4 * channels)
        v.d_windows[group] += mm_t(v.g_one[...], v.banded[:, at])
        v.d_banded[:, at] += mm(v.window_turned[...], v.g_one[...])

    for number in range(bins_three):
        three = bins_three - 1 - number
        if three % 2:
            v.window_turned[...] = transposed(v.windows[three // 2])
        stem_back(three // 2, three % 2, STEM_MOMENT + STEM_STEP * number)


    for layer in range(1, 3):
        for tap in range(9):
            row = 9 * layer + tap
            v.d_taps[row : row + 1] = column_sum(v.d_kernels[row])
    for tap in range(9):
        total = None
        for f in range(8):
            row = BINS * (tap // 3) + 2 * f + tap % 3
            piece = v.d_banded[row : row + 1, f * channels : (f + 1) * channels]
            total = piece if total is None else total + piece
        v.d_taps[tap : tap + 1] = total
    v.d_taps[27:32] = jnp.zeros((5, channels), F32)

    gather_columns(TAPS, v.d_taps, channels)
    shape = sizes + (channels // devices, channels)
    v.parts[POINT][...] = jnp.concatenate(
        [v.d_points[0].reshape(shape), v.d_points[1].reshape(shape)], axis=4
    ).astype(BF16)
    for i in (POINT, TAPS):
        start_sum(i)
    advance(plan.small_moment)


    for phase in range(9):
        v.feats[phase] = jnp.zeros((frames, LANES), F32)
    for group in range(GROUPS):
        for phase in range(4):
            rows = v.d_windows[group, pl.ds(phase * frames, frames)]
            for tap in range(3):
                piece = jnp.where(band(tap), rows, 0.0)
                back = (16 * group - 1 - BINS * tap) % LANES
                v.feats[2 * phase + tap] += pltpu.roll(piece, back, 1)
    for phase in range(8):
        total = v.feats[phase + 1]
        if phase == 7:
            total = total + shift_rows(v.feats[0] * joint, -1)
        v.frames_wide[pl.ds(phase, frames, stride=8), :] = total * keep_of(phase)

    for phase in range(8):
        at = pl.ds(phase * frames, frames)
        v.mel_grad[:, at] = v.frames_wide[at, :].T[:bins]

    advance(float("inf"))
    wide = v.sum_wide[...]
    each = width // devices
    v.grad_depth[...] = wide[TAP_ROW:GAIN_ROW, :each]
    v.grad_gains[...] = wide[GAIN_ROW:SHIFT_ROW, :each]
    v.grad_shifts[...] = wide[SHIFT_ROW:FINAL_ROW, :each]
    v.grad_final[...] = wide[FINAL_ROW : FINAL_ROW + 1, :each]
    taps = v.sum_taps[...].T
    for layer in range(3):
        v.grad_kernels[layer] = taps[: channels // devices, 9 * layer : 9 * layer + 9]
    for copy in pending:
        copy.wait_send()


def frame_segments(lengths, assignment, device, frames):
    belongs = assignment == device
    own_sizes = jnp.where(belongs, lengths, 0)
    finishes = jnp.cumsum(own_sizes, dtype=jnp.int32)
    beginnings = finishes - own_sizes
    position = jnp.arange(frames, dtype=jnp.int32)[:, None]
    inside = belongs[None, :] & (position >= beginnings[None, :]) & (position < finishes[None, :])
    number = jnp.arange(lengths.shape[0], dtype=jnp.int32)[None, :] + 1
    return jnp.sum(jnp.where(inside, number, 0), axis=1, dtype=jnp.int32) - 1


def feature_keep(segments, time_spans, freq_spans, mel_bins):
    frames = segments.shape[0] * 8
    position = jnp.arange(frames, dtype=jnp.int32)[:, None]
    covered = (position >= time_spans[None, :, 0]) & (
        position < time_spans[None, :, 0] + time_spans[None, :, 1]
    )
    time_keep = jnp.repeat(segments >= 0, 8) & jnp.logical_not(jnp.any(covered, axis=1))
    channel = jnp.arange(mel_bins, dtype=jnp.int32)[:, None]
    banned = (channel >= freq_spans[None, :, 0]) & (
        channel < freq_spans[None, :, 0] + freq_spans[None, :, 1]
    )
    freq_keep = jnp.logical_not(jnp.any(banned, axis=1))
    return (time_keep[:, None] & freq_keep[None, :]).astype(jnp.float32)


def time_taps(values, seg_in, seg_out):
    out_len = seg_out.shape[0]
    paired = values.reshape((out_len, 2) + values.shape[1:])
    even_part = paired[:, 0]
    odd_part = paired[:, 1]
    prior_part = jnp.concatenate([jnp.zeros_like(odd_part[:1]), odd_part[:-1]], axis=0)
    seg_pairs = seg_in.reshape(out_len, 2)
    prior_segs = jnp.concatenate([jnp.full((1,), -2, jnp.int32), seg_pairs[:-1, 1]])
    opening = ((prior_segs == seg_out) & (seg_out >= 0)).astype(values.dtype)
    opening = opening.reshape((out_len,) + (1,) * (values.ndim - 1))
    return (prior_part * opening, even_part, odd_part)


def freq_taps(values):
    frames, bins_in = (values.shape[0], values.shape[1])
    paired = values.reshape((frames, bins_in // 2, 2) + values.shape[2:])
    even_part = paired[:, :, 0]
    odd_part = paired[:, :, 1]
    prior_part = jnp.concatenate([jnp.zeros_like(odd_part[:, :1]), odd_part[:, :-1]], axis=1)
    return (prior_part, even_part, odd_part)


def strided_conv(values, kernel, seg_in, seg_out):
    summed = None
    for tap_row, tap_rows in enumerate(time_taps(values, seg_in, seg_out)):
        for tap_col, tap_piece in enumerate(freq_taps(tap_rows)):
            if tap_piece.ndim == 2:
                tap_piece = tap_piece[:, :, None]
            addend = tap_piece * kernel[3 * tap_row + tap_col]
            summed = addend if summed is None else summed + addend
    present = (seg_out >= 0).astype(summed.dtype)
    return summed * present[:, None, None]


def depth_glu(gated_rows, kernel, segments):
    model_width = gated_rows.shape[1] // 2
    merged = gated_rows[:, :model_width] * jax.nn.sigmoid(gated_rows[:, model_width:])
    radius = kernel.shape[0] // 2
    frames = gated_rows.shape[0]
    padded = jnp.pad(merged, ((radius, radius), (0, 0)))
    padded_segs = jnp.pad(segments, (radius, radius), constant_values=-2)
    summed = jnp.zeros_like(merged)
    for tap_index in range(kernel.shape[0]):
        same_segment = (padded_segs[tap_index : tap_index + frames] == segments).astype(
            merged.dtype
        )
        summed = (
            summed
            + padded[tap_index : tap_index + frames] * same_segment[:, None] * kernel[tap_index]
        )
    return summed


def stem_front(masked, first_kernel, second_kernel, segments):
    seg_zero = jnp.repeat(segments, 8)
    seg_one = jnp.repeat(segments, 4)
    seg_two = jnp.repeat(segments, 2)
    level_one = jax.nn.silu(strided_conv(masked, first_kernel, seg_zero, seg_one))
    return strided_conv(level_one, second_kernel, seg_one, seg_two)


def stem_middle(point_two, third_kernel, segments):
    frames = segments.shape[0]
    channels = point_two.shape[1]
    hidden = jax.nn.silu(point_two).reshape(frames * 2, -1, channels)
    return strided_conv(hidden, third_kernel, jnp.repeat(segments, 2), segments)


def matmul(operand, matrix):
    return jnp.dot(operand, matrix, preferred_element_type=jnp.float32)


def over_rows(operand, matrix):
    return lax.dot_general(
        operand, matrix, (((0,), (0,)), ((), ())), preferred_element_type=jnp.float32
    )


def against(operand, matrix):
    return lax.dot_general(
        operand, matrix, (((1,), (1,)), ((), ())), preferred_element_type=jnp.float32
    )


def ffn_forward(stream, norm_gain, norm_shift, inner_weight, outer_weight):
    normed = layer_norm(stream, norm_gain, norm_shift).astype(jnp.bfloat16)
    hidden = matmul(normed, inner_weight)
    active = jax.nn.silu(hidden).astype(jnp.bfloat16)
    return (matmul(active, outer_weight), (normed, hidden, active))


def ffn_backward(stream, norm_gain, norm_shift, inner_weight, outer_weight, kept_values, grad_out):
    normed, hidden, active = kept_values
    grad_outer = over_rows(active, grad_out)
    grad_active = against(grad_out, outer_weight)
    grad_hidden = jax.vjp(jax.nn.silu, hidden)[1](grad_active)[0].astype(jnp.bfloat16)
    grad_inner = over_rows(normed, grad_hidden)
    grad_normed = against(grad_hidden, inner_weight)
    pullback = jax.vjp(layer_norm, stream, norm_gain, norm_shift)[1]
    grad_stream, grad_gain, grad_shift = pullback(grad_normed)
    return (grad_stream, grad_gain, grad_shift, grad_inner, grad_outer)


def split_heads(joined, head_count):
    frames = joined.shape[0]
    model_width = joined.shape[1] // 3
    shaped = joined.reshape(frames, 3, head_count, model_width // head_count)
    return (shaped[:, 0], shaped[:, 1], shaped[:, 2])


def block_logits(queries, key_rows, query_segs, key_segs, anchor, frames, contexts):
    scores = jnp.einsum("qhd,khd->hqk", queries, key_rows, preferred_element_type=jnp.float32)
    radius = (key_rows.shape[0] - queries.shape[0]) // 2
    query_pos = anchor + jnp.arange(queries.shape[0], dtype=jnp.int32)
    key_pos = anchor - radius + jnp.arange(key_rows.shape[0], dtype=jnp.int32)
    distance = jnp.abs(query_pos[:, None] - key_pos[None, :])
    allowed = (
        (query_segs[:, None] == key_segs[None, :])
        & (key_pos[None, :] >= 0)
        & (key_pos[None, :] < frames)
    )
    allowed = allowed[None] & (distance[None] <= contexts[:, None, None])
    return jnp.where(allowed, scores * queries.shape[2] ** (-0.5), MASKED_LOGIT)


def attend_forward(joined, segments, contexts):
    frames = joined.shape[0]
    queries, key_rows, value_rows = split_heads(joined, contexts.shape[0])
    padded_keys = jnp.pad(key_rows, ((CTX, CTX), (0, 0), (0, 0)))
    padded_values = jnp.pad(value_rows, ((CTX, CTX), (0, 0), (0, 0)))
    padded_segs = jnp.pad(segments, (CTX, CTX), constant_values=-2)
    logits = block_logits(queries, padded_keys, segments, padded_segs, 0, frames, contexts)
    highest = jnp.max(logits, axis=-1, keepdims=True)
    exponent = jnp.exp(logits - highest)
    summed = jnp.sum(exponent, axis=-1, keepdims=True)
    weights = (exponent / summed).astype(jnp.bfloat16)
    outputs = jnp.einsum("hqk,khd->qhd", weights, padded_values, preferred_element_type=jnp.float32)
    log_parts = highest[:, :, 0] + jnp.log(summed[:, :, 0])
    return (outputs, log_parts)


def attend_backward(joined, segments, contexts, log_totals, grad_mixed):
    frames = joined.shape[0]
    queries, key_rows, value_rows = split_heads(joined, contexts.shape[0])
    padded_keys = jnp.pad(key_rows, ((CTX, CTX), (0, 0), (0, 0)))
    padded_values = jnp.pad(value_rows, ((CTX, CTX), (0, 0), (0, 0)))
    padded_segs = jnp.pad(segments, (CTX, CTX), constant_values=-2)
    block_rows = min(frames, 512)
    grad_keys = jnp.zeros(padded_keys.shape, jnp.float32)
    grad_values = jnp.zeros(padded_values.shape, jnp.float32)
    query_span = slice(0, block_rows)
    key_span = slice(0, block_rows + 2 * CTX)
    logits = block_logits(queries, padded_keys, segments, padded_segs, 0, frames, contexts)
    weights = jnp.exp(logits - log_totals[:, query_span, None])
    grad_weights = jnp.einsum(
        "qhd,khd->hqk", grad_mixed, padded_values, preferred_element_type=jnp.float32
    )
    row_dot = jnp.sum(weights * grad_weights, axis=-1, keepdims=True)
    grad_scores = (weights * (grad_weights - row_dot) * queries.shape[2] ** (-0.5)).astype(
        jnp.bfloat16
    )
    grad_queries = jnp.einsum(
        "hqk,khd->qhd", grad_scores, padded_keys, preferred_element_type=jnp.float32
    )
    grad_keys = grad_keys.at[key_span].add(
        jnp.einsum("hqk,qhd->khd", grad_scores, queries, preferred_element_type=jnp.float32)
    )
    grad_values = grad_values.at[key_span].add(
        jnp.einsum(
            "hqk,qhd->khd",
            weights.astype(jnp.bfloat16),
            grad_mixed,
            preferred_element_type=jnp.float32,
        )
    )
    stacked = jnp.stack(
        [grad_queries, grad_keys[CTX : CTX + frames], grad_values[CTX : CTX + frames]], axis=1
    )
    return stacked.reshape(frames, -1)


def local_plain(
    mel,
    cotangent,
    lengths,
    assignment,
    time_spans,
    freq_spans,
    contexts,
    stem_kernels,
    stem_point,
    stem_out,
    ffn_in,
    ffn_out,
    qkv,
    attn_out,
    conv_in,
    conv_depth,
    conv_out,
    norm_gains,
    norm_shifts,
    final_shift,
):
    device = lax.axis_index(AXES[0]) * lax.axis_size(AXES[1]) + lax.axis_index(AXES[1])
    frames = cotangent.shape[0]
    segments = frame_segments(lengths, assignment, device, frames)
    feature_mask = feature_keep(segments, time_spans[0], freq_spans[0], mel.shape[1])
    present = (segments >= 0).astype(jnp.float32)[:, None]
    counted = jnp.sum(lengths).astype(jnp.float32)
    gathered = (
        lax.all_gather(stem_kernels, AXES, axis=2, tiled=True),
        lax.all_gather(stem_point, AXES, axis=1, tiled=True),
        lax.all_gather(stem_out, AXES, axis=0, tiled=True),
        lax.all_gather(ffn_in, AXES, axis=1, tiled=True),
        lax.all_gather(ffn_out, AXES, axis=1, tiled=True),
        lax.all_gather(qkv, AXES, axis=0, tiled=True),
        lax.all_gather(attn_out, AXES, axis=0, tiled=True),
        lax.all_gather(conv_in, AXES, axis=0, tiled=True),
        lax.all_gather(conv_depth, AXES, axis=1, tiled=True),
        lax.all_gather(conv_out, AXES, axis=0, tiled=True),
        lax.all_gather(norm_gains, AXES, axis=1, tiled=True),
        lax.all_gather(norm_shifts, AXES, axis=1, tiled=True),
        lax.all_gather(final_shift, AXES, axis=0, tiled=True),
    )
    (
        kernels,
        point_weight,
        stem_weight,
        ffn_inner,
        ffn_outer,
        qkv_weight,
        out_weight,
        conv_inner,
        conv_taps,
        conv_outer,
        norm_rows,
        shift_rows,
        final_row,
    ) = gathered
    kernels_wide = kernels.astype(jnp.float32)
    gains_wide = norm_rows.astype(jnp.float32)
    shifts_wide = shift_rows.astype(jnp.float32)
    final_wide = final_row.astype(jnp.float32)
    masked = mel.astype(jnp.float32) * feature_mask
    level_two, front_pullback = jax.vjp(
        lambda masked_input, first_taps, second_taps: stem_front(
            masked_input, first_taps, second_taps, segments
        ),
        masked,
        kernels_wide[0],
        kernels_wide[1],
    )
    channels = level_two.shape[2]
    level_two_low = level_two.reshape(-1, channels).astype(jnp.bfloat16)
    point_two = matmul(level_two_low, point_weight[0])
    level_three, middle_pullback = jax.vjp(
        lambda point_input, third_taps: stem_middle(point_input, third_taps, segments),
        point_two,
        kernels_wide[2],
    )
    level_three_low = level_three.reshape(-1, channels).astype(jnp.bfloat16)
    point_three = matmul(level_three_low, point_weight[1])
    stem_hidden = jax.nn.silu(point_three).reshape(frames, -1).astype(jnp.bfloat16)
    after_stem = matmul(stem_hidden, stem_weight)
    ffn_result_one, ffn_kept_one = ffn_forward(
        after_stem, gains_wide[0], shifts_wide[0], ffn_inner[0], ffn_outer[0]
    )
    after_ffn = after_stem + 0.5 * ffn_result_one
    attn_normed = layer_norm(after_ffn, gains_wide[1], shifts_wide[1]).astype(jnp.bfloat16)
    joined = matmul(attn_normed, qkv_weight).astype(jnp.bfloat16)
    mixed_heads, log_totals = attend_forward(joined, segments, contexts)
    mixed_low = mixed_heads.reshape(frames, -1).astype(jnp.bfloat16)
    after_attn = after_ffn + matmul(mixed_low, out_weight)
    conv_normed = layer_norm(after_attn, gains_wide[2], shifts_wide[2]).astype(jnp.bfloat16)
    gated_rows = matmul(conv_normed, conv_inner)
    taps_wide = conv_taps.astype(jnp.float32)
    depthwise, depth_pullback = jax.vjp(
        lambda gate_input, taps_input: depth_glu(gate_input, taps_input, segments),
        gated_rows,
        taps_wide,
    )
    first_sum, second_sum = lax.psum(
        (jnp.sum(depthwise * present, axis=0), jnp.sum(depthwise * depthwise * present, axis=0)),
        AXES,
    )
    average = first_sum / counted
    spread = second_sum / counted - average * average
    inv_spread = lax.rsqrt(spread + EPSILON)
    standard = (depthwise - average) * inv_spread
    batch_normed = standard * gains_wide[3] + shifts_wide[3]
    conv_active = jax.nn.silu(batch_normed).astype(jnp.bfloat16)
    after_conv = after_attn + matmul(conv_active, conv_outer)
    ffn_result_two, ffn_kept_two = ffn_forward(
        after_conv, gains_wide[4], shifts_wide[4], ffn_inner[1], ffn_outer[1]
    )
    after_second = after_conv + 0.5 * ffn_result_two
    activations = (layer_norm(after_second, gains_wide[5], final_wide) * present).astype(
        jnp.bfloat16
    )
    weights_back = (
        lax.all_gather(stem_kernels, AXES, axis=2, tiled=True),
        lax.all_gather(stem_point, AXES, axis=1, tiled=True),
        lax.all_gather(stem_out, AXES, axis=0, tiled=True),
        lax.all_gather(ffn_in, AXES, axis=1, tiled=True),
        lax.all_gather(ffn_out, AXES, axis=1, tiled=True),
        lax.all_gather(qkv, AXES, axis=0, tiled=True),
        lax.all_gather(attn_out, AXES, axis=0, tiled=True),
        lax.all_gather(conv_in, AXES, axis=0, tiled=True),
        lax.all_gather(conv_depth, AXES, axis=1, tiled=True),
        lax.all_gather(conv_out, AXES, axis=0, tiled=True),
        lax.all_gather(norm_gains, AXES, axis=1, tiled=True),
        lax.all_gather(norm_shifts, AXES, axis=1, tiled=True),
        lax.all_gather(final_shift, AXES, axis=0, tiled=True),
    )
    (
        back_kernels,
        back_point,
        back_stem,
        back_inner,
        back_outer,
        back_qkv,
        back_attn,
        back_conv_in,
        back_taps,
        back_conv_out,
        back_gains,
        back_shifts,
        back_final,
    ) = weights_back
    back_gains_wide = back_gains.astype(jnp.float32)
    back_shifts_wide = back_shifts.astype(jnp.float32)
    back_final_wide = back_final.astype(jnp.float32)
    grad_final = cotangent.astype(jnp.float32) * present
    pullback = jax.vjp(layer_norm, after_second, back_gains_wide[5], back_final_wide)[1]
    grad_stream, grad_gain_final, grad_shift_final = pullback(grad_final)
    ffn_two = ffn_backward(
        after_conv,
        back_gains_wide[4],
        back_shifts_wide[4],
        back_inner[1],
        back_outer[1],
        ffn_kept_two,
        (0.5 * grad_stream).astype(jnp.bfloat16),
    )
    grad_stream = grad_stream + ffn_two[0]
    grad_conv_low = grad_stream.astype(jnp.bfloat16)
    grad_conv_out = over_rows(conv_active, grad_conv_low)
    grad_active = against(grad_conv_low, back_conv_out)
    grad_batch = jax.vjp(jax.nn.silu, batch_normed)[1](grad_active)[0]
    beta_sum, gamma_sum = lax.psum(
        (jnp.sum(grad_batch * present, axis=0), jnp.sum(grad_batch * standard * present, axis=0)),
        AXES,
    )
    bn_gain = back_gains_wide[3]
    grad_first = (
        inv_spread * inv_spread * bn_gain * gamma_sum * average - inv_spread * bn_gain * beta_sum
    ) / counted
    grad_second = -0.5 * inv_spread * inv_spread * bn_gain * gamma_sum / counted
    grad_depth = bn_gain * inv_spread * grad_batch + present * (
        grad_first + 2.0 * depthwise * grad_second
    )
    grad_gated, grad_taps = depth_pullback(grad_depth)
    grad_gated_low = grad_gated.astype(jnp.bfloat16)
    grad_conv_in = over_rows(conv_normed, grad_gated_low)
    pullback = jax.vjp(layer_norm, after_attn, back_gains_wide[2], back_shifts_wide[2])[1]
    conv_norm_grads = pullback(against(grad_gated_low, back_conv_in))
    grad_stream = grad_stream + conv_norm_grads[0]
    grad_attn_low = grad_stream.astype(jnp.bfloat16)
    grad_attn_out = over_rows(mixed_low, grad_attn_low)
    grad_mixed = against(grad_attn_low, back_attn).astype(jnp.bfloat16).reshape(mixed_heads.shape)
    grad_joined = attend_backward(joined, segments, contexts, log_totals, grad_mixed).astype(
        jnp.bfloat16
    )
    grad_qkv = over_rows(attn_normed, grad_joined)
    pullback = jax.vjp(layer_norm, after_ffn, back_gains_wide[1], back_shifts_wide[1])[1]
    attn_norm_grads = pullback(against(grad_joined, back_qkv))
    grad_stream = grad_stream + attn_norm_grads[0]
    ffn_one = ffn_backward(
        after_stem,
        back_gains_wide[0],
        back_shifts_wide[0],
        back_inner[0],
        back_outer[0],
        ffn_kept_one,
        (0.5 * grad_stream).astype(jnp.bfloat16),
    )
    grad_stream = grad_stream + ffn_one[0]
    grad_stem_low = grad_stream.astype(jnp.bfloat16)
    grad_stem_out = over_rows(stem_hidden, grad_stem_low)
    grad_hidden = against(grad_stem_low, back_stem).reshape(point_three.shape)
    grad_point_three = jax.vjp(jax.nn.silu, point_three)[1](grad_hidden)[0].astype(jnp.bfloat16)
    grad_third_point = over_rows(level_three_low, grad_point_three)
    grad_level_three = against(grad_point_three, back_point[1]).reshape(level_three.shape)
    grad_point_two, grad_third_kernel = middle_pullback(grad_level_three)
    grad_point_two_low = grad_point_two.astype(jnp.bfloat16)
    grad_second_point = over_rows(level_two_low, grad_point_two_low)
    grad_level_two = against(grad_point_two_low, back_point[0]).reshape(level_two.shape)
    grad_masked, grad_first_kernel, grad_second_kernel = front_pullback(grad_level_two)
    mel_grad = grad_masked * feature_mask
    zero_row = jnp.zeros_like(grad_gain_final)
    grad_gains = jnp.stack(
        [ffn_one[1], attn_norm_grads[1], conv_norm_grads[1], zero_row, ffn_two[1], grad_gain_final]
    )
    grad_shifts = jnp.stack(
        [ffn_one[2], attn_norm_grads[2], conv_norm_grads[2], zero_row, ffn_two[2]]
    )
    grad_kernels = jnp.stack([grad_first_kernel, grad_second_kernel, grad_third_kernel])
    grad_points = jnp.stack([grad_second_point, grad_third_point])
    grad_inner = jnp.stack([ffn_one[3], ffn_two[3]])
    grad_outer = jnp.stack([ffn_one[4], ffn_two[4]])
    owned_grads = (
        lax.psum_scatter(grad_kernels, AXES, scatter_dimension=2, tiled=True),
        lax.psum_scatter(grad_points, AXES, scatter_dimension=1, tiled=True),
        lax.psum_scatter(grad_stem_out, AXES, scatter_dimension=0, tiled=True),
        lax.psum_scatter(grad_inner, AXES, scatter_dimension=1, tiled=True),
        lax.psum_scatter(grad_outer, AXES, scatter_dimension=1, tiled=True),
        lax.psum_scatter(grad_qkv, AXES, scatter_dimension=0, tiled=True),
        lax.psum_scatter(grad_attn_out, AXES, scatter_dimension=0, tiled=True),
        lax.psum_scatter(grad_conv_in, AXES, scatter_dimension=0, tiled=True),
        lax.psum_scatter(grad_taps, AXES, scatter_dimension=1, tiled=True),
        lax.psum_scatter(grad_conv_out, AXES, scatter_dimension=0, tiled=True),
        lax.psum_scatter(grad_gains, AXES, scatter_dimension=1, tiled=True),
        lax.psum_scatter(grad_shifts, AXES, scatter_dimension=1, tiled=True),
        lax.psum_scatter(grad_shift_final, AXES, scatter_dimension=0, tiled=True),
    )
    share_width = gamma_sum.shape[0] // (lax.axis_size(AXES[0]) * lax.axis_size(AXES[1]))
    own_gamma = lax.dynamic_slice_in_dim(gamma_sum, device * share_width, share_width)
    own_beta = lax.dynamic_slice_in_dim(beta_sum, device * share_width, share_width)
    owned_gains = owned_grads[10].at[3].add(own_gamma)
    owned_shifts = owned_grads[11].at[3].add(own_beta)
    return (
        activations,
        mel_grad,
        owned_grads[0],
        owned_grads[1],
        owned_grads[2],
        owned_grads[3],
        owned_grads[4],
        owned_grads[5],
        owned_grads[6],
        owned_grads[7],
        owned_grads[8],
        owned_grads[9],
        owned_gains,
        owned_shifts,
        owned_grads[12],
    )


def gather_sources(v):
    return [
        v.small,
        v.point,
        v.stem_out,
        v.ffn_in.at[0],
        v.ffn_out.at[0],
        v.qkv,
        v.attn_out,
        v.conv_in,
        v.conv_out,
        v.ffn_in.at[1],
        v.ffn_out.at[1],
    ]


STEM_MOMENT = 17
STEM_STEP = 5.0
SMALL_MOMENT = 68
MOMENTS = (0, 0, 0, 10, 10, 14, 15, 15, 17, SMALL_MOMENT, 17, SMALL_MOMENT)
LINK_BYTES = 1e4
LATENCY = 8.0
AHEAD = 8.0


def order_of_steps(sums, grads):
    size = [grads[i].block[0] * width * 2 / LINK_BYTES for i, _, width in sums]
    waiting = list(range(len(sums)))
    hopped, steps = [], []
    now, z_free = 0.0, 0.0
    while waiting or hopped:
        ready = [entry for entry in hopped if entry[0] <= now]
        fresh = [p for p in waiting if MOMENTS[sums[p][0]] <= now]
        if ready:
            entry = ready[0]
            hopped.remove(entry)
            arrived, p = entry
            steps.append((max(arrived, now - AHEAD), 1, p))
            now += size[p] / 2
            landed = now + LATENCY
            steps.append((landed, 2, p))
            z_free = max(z_free, landed) + size[p]
            steps.append((z_free + 2 * LATENCY, 3, p))
        elif fresh:
            p = fresh[0]
            waiting.remove(p)
            steps.append((max(MOMENTS[sums[p][0]], now - AHEAD), 0, p))
            now += size[p]
            hopped.append((now + LATENCY, p))
        else:
            now = min([entry[0] for entry in hopped] + [MOMENTS[sums[p][0]] for p in waiting])
    return sorted(steps)


def finish_kernel(count, *refs):
    for i in range(count):
        refs[count + i][...] = refs[i][...]


def local(
    mel,
    cotangent,
    lengths,
    assignment,
    time_spans,
    freq_spans,
    contexts,
    stem_kernels,
    stem_point,
    stem_out,
    ffn_in,
    ffn_out,
    qkv,
    attn_out,
    conv_in,
    conv_depth,
    conv_out,
    norm_gains,
    norm_shifts,
    final_shift,
):
    arguments = (mel, cotangent, lengths, assignment, time_spans, freq_spans, contexts)
    arguments += (stem_kernels, stem_point, stem_out, ffn_in, ffn_out, qkv, attn_out)
    arguments += (conv_in, conv_depth, conv_out, norm_gains, norm_shifts, final_shift)
    if qkv.shape[0] % TILE or stem_out.shape[0] % TILE:
        return local_plain(*arguments)
    sizes = grid_sizes()
    devices = sizes[0] * sizes[1] * sizes[2] * sizes[3]
    frames, width = cotangent.shape
    bins = mel.shape[1]
    channels = stem_point.shape[2]
    hidden = ffn_in.shape[2]
    heads = contexts.shape[0]
    bins_two, bins_three = 4 * GROUPS, 2 * GROUPS
    inputs = dict(
        mel=(mel.T, pltpu.VMEM),
        stem_kernels=(stem_kernels.swapaxes(1, 2), pltpu.VMEM),
        stem_point=(stem_point, pltpu.VMEM),
        conv_depth=(conv_depth, pltpu.VMEM),
        norm_gains=(norm_gains, pltpu.VMEM),
        norm_shifts=(norm_shifts, pltpu.VMEM),
        final_shift=(final_shift.reshape(1, -1), pltpu.VMEM),
        cotangent=(cotangent, pltpu.VMEM),
        lengths=(lengths.reshape(1, -1), pltpu.VMEM),
        assignment=(assignment.reshape(1, -1), pltpu.VMEM),
        time_spans=(time_spans, pltpu.SMEM),
        freq_spans=(freq_spans, pltpu.SMEM),
        contexts=(contexts, pltpu.SMEM),
        stem_out=(stem_out, pl.ANY),
        ffn_in=(ffn_in, pl.ANY),
        ffn_out=(ffn_out, pl.ANY),
        qkv=(qkv, pl.ANY),
        attn_out=(attn_out, pl.ANY),
        conv_in=(conv_in, pl.ANY),
        conv_out=(conv_out, pl.ANY),
    )
    shards = [
        (64, LANES),
        (stem_point.shape[1], 2 * channels),
        stem_out.shape,
        ffn_in.shape[1:],
        ffn_out.shape[1:],
        qkv.shape,
        attn_out.shape,
        conv_in.shape,
        conv_out.shape,
        ffn_in.shape[1:],
        ffn_out.shape[1:],
    ]
    count = len(shards)

    def cut(item, width, pieces=2):
        return [(item, width // pieces * k, width // pieces) for k in range(pieces)]

    def whole(item):
        return cut(item, shards[item][1], 1)

    def halved(item):
        return cut(item, shards[item][1])

    groups = [whole(0) + whole(1) + whole(6), whole(8)]
    groups += [[piece] for item in (2, 3, 4, 5) for piece in halved(item)]
    groups += [whole(7)] + [[piece] for item in (9, 10) for piece in halved(item)]
    pieces = [piece for group in groups for piece in group]
    turns = [[pieces.index(piece) for piece in group] for group in groups]
    dma = pltpu.SemaphoreType.DMA
    z_steps = max(1, sizes[2] - 1)
    wide = max(1, sizes[0] - 1, sizes[1] - 1)
    near = sizes[2] * CORES - 1
    far = max(1, sizes[0] * sizes[1] - 1)
    tokens = (frames, width)
    total_rows = (max(8, 2 * width // LANES), LANES)
    scratch = dict(
        held=[pltpu.VMEM(sizes + s, F32 if i == 1 else BF16) for i, s in enumerate(shards)],
        g_local=dma((len(pieces),)),
        g_z=dma((2, len(pieces), z_steps)),
        g_hop=dma((2, len(pieces), 2, 2, wide)),
        g_core=dma((2, len(pieces))),
        t_own=pltpu.VMEM((2,) + total_rows, F32),
        t_mid=pltpu.VMEM((2,) + total_rows, F32),
        t_near=pltpu.VMEM((2, near) + total_rows, F32),
        t_far=pltpu.VMEM((2, far) + total_rows, F32),
        t_sem=dma((2, 2, near + far)),
        packed=pltpu.VMEM((64, LANES), F32),
        small=pltpu.VMEM((64, LANES), BF16),
        point=pltpu.VMEM((stem_point.shape[1], 2 * channels), F32),
        frames_wide=pltpu.VMEM((8 * frames, LANES), F32),
        feats=pltpu.VMEM((9, frames, LANES), F32),
        windows=pltpu.VMEM((GROUPS, 4 * frames, LANES), BF16),
        params=pltpu.VMEM((32, width), F32),
        kernels=pltpu.VMEM((32, channels), F32),
        band_wide=pltpu.VMEM((LANES, channels), F32),
        banded=pltpu.VMEM((LANES, 8 * channels), BF16),
        points=pltpu.VMEM((2, channels, channels), BF16),
        ones_wide=pltpu.VMEM((3, 4 * frames, channels), F32),
        ones=pltpu.VMEM((4, 4 * frames, channels), BF16),
        two_even=pltpu.VMEM((2 * frames, channels), F32),
        two_odd=pltpu.VMEM((2, 2 * frames, channels), F32),
        level_now=pltpu.VMEM((2 * frames, channels), BF16),
        level_two=pltpu.VMEM((bins_two, channels, 2 * frames), BF16),
        point_two=pltpu.VMEM((bins_two, 2 * frames, channels), BF16),
        level_three=pltpu.VMEM((bins_three, channels, frames), BF16),
        point_three=pltpu.VMEM((bins_three, frames, channels), BF16),
        weights=pltpu.VMEM((heads, frames, frames), F32),
        joined=pltpu.VMEM((frames, 3 * width), BF16),
        gated=pltpu.VMEM((frames, 2 * width), F32),
        hidden0=pltpu.VMEM((frames, hidden), BF16),
        hidden1=pltpu.VMEM((frames, hidden), BF16),
        active0=pltpu.VMEM((frames, hidden), BF16),
        active1=pltpu.VMEM((frames, hidden), BF16),
        after_stem=pltpu.VMEM(tokens, F32),
        after_ffn=pltpu.VMEM(tokens, F32),
        after_attn=pltpu.VMEM(tokens, F32),
        after_conv=pltpu.VMEM(tokens, F32),
        after_second=pltpu.VMEM(tokens, F32),
        merged=pltpu.VMEM(tokens, F32),
        depthwise=pltpu.VMEM(tokens, F32),
        standard=pltpu.VMEM(tokens, F32),
        batch_normed=pltpu.VMEM(tokens, F32),
        normed0=pltpu.VMEM(tokens, BF16),
        normed1=pltpu.VMEM(tokens, BF16),
        normed2=pltpu.VMEM(tokens, BF16),
        normed4=pltpu.VMEM(tokens, BF16),
        mixed=pltpu.VMEM(tokens, BF16),
        conv_active=pltpu.VMEM(tokens, BF16),
    )
    outputs = dict(
        activations=(tokens, BF16),
        mel_grad=((bins, 8 * frames), F32),
        grad_kernels=((3, channels // devices, 9), F32),
        grad_point=((2 * channels // devices, channels), F32),
        grad_stem=(stem_out.shape, F32),
        grad_inner=(ffn_in.shape, F32),
        grad_outer=(ffn_out.shape, F32),
        grad_qkv=(qkv.shape, F32),
        grad_attn=(attn_out.shape, F32),
        grad_conv_in=(conv_in.shape, F32),
        grad_depth=(conv_depth.shape, F32),
        grad_conv_out=(conv_out.shape, F32),
        grad_gains=(norm_gains.shape, F32),
        grad_shifts=(norm_shifts.shape, F32),
        grad_final=((1, width // devices), F32),
    )
    grads = [
        types.SimpleNamespace(weight=weight, product=weight > 0, block=block)
        for weight, block in [(weight, shards[weight]) for weight in range(10, 1, -1)]
        + [(0, (2 * channels // devices, channels)), (0, (32, LANES)), (0, (32, LANES))]
    ]
    lead = sizes[:3]
    columns, mates, right, parts, kept, landed, landed_z = {}, {}, {}, {}, {}, {}, {}
    for i, spec in enumerate(grads):
        rows, breadth = spec.block
        if spec.product:
            columns[i] = pltpu.VMEM(sizes + (rows, frames), BF16)
            mates[i] = pltpu.VMEM(lead + (rows, frames), BF16)
            right[i] = pltpu.VMEM((2 * frames, breadth), BF16)
        else:
            parts[i] = pltpu.VMEM(sizes + spec.block, BF16)
            kept[i] = pltpu.VMEM(lead + spec.block, BF16)
            mates[i] = pltpu.VMEM(lead + spec.block, BF16)
    sums = []
    for i, spec in enumerate(grads):
        large = spec.block[0] * spec.block[1] >= 2**14 + 2**12 and spec.block[1] % (4 * LANES) == 0
        sums += cut(i, spec.block[1], 2 if large else 1)
    for p, (i, _, breadth) in enumerate(sums):
        rows = grads[i].block[0]
        split = 2 if breadth // 2 % LANES == 0 else 1
        part = (rows, breadth // split)
        landed[p] = []
        for order in range(split):
            one, two = (1, 0) if order == 0 else (0, 1)
            steps = (max(1, sizes[one] - 1), max(1, sizes[two] - 1))
            landed[p].append(
                [
                    pltpu.VMEM((steps[0], sizes[two], sizes[2]) + part, BF16),
                    pltpu.VMEM((steps[1], sizes[2]) + part, BF16),
                ]
            )
        landed_z[p] = pltpu.VMEM((z_steps, rows, breadth), BF16)
    scratch |= dict(
        columns=columns,
        mates=mates,
        right=right,
        parts=parts,
        kept=kept,
        landed=landed,
        landed_z=landed_z,
        s_core=dma((2, len(grads), 2)),
        s_hop=dma((2, len(sums), 2, 2, wide)),
        s_z=dma((2, len(sums), z_steps)),
        stem_hidden=pltpu.VMEM((frames, bins_three * channels), BF16),
        sum_wide=pltpu.VMEM((32, LANES), F32),
        sum_taps=pltpu.VMEM((32, LANES), F32),
        d_params=pltpu.VMEM((32, width), F32),
        d_taps=pltpu.VMEM((32, channels), F32),
        stream=pltpu.VMEM(tokens, F32),
        grad_batch=pltpu.VMEM(tokens, F32),
        g_mixed=pltpu.VMEM(tokens, BF16),
        g_three=pltpu.VMEM((frames, bins_three * channels), BF16),
        g_two=pltpu.VMEM((2, 2 * frames, channels), BF16),
        g_one=pltpu.VMEM((4 * frames, 4 * channels), BF16),
        d_three=pltpu.VMEM((2, 2 * frames, channels), F32),
        d_two_even=pltpu.VMEM((2, 3 * frames, channels), BF16),
        d_two_odd=pltpu.VMEM((3 * frames, channels), BF16),
        d_kernels=pltpu.VMEM((27, 8, channels), F32),
        d_points=pltpu.VMEM((2, channels, channels), F32),
        d_windows=pltpu.VMEM((GROUPS, 4 * frames, LANES), F32),
        d_banded=pltpu.VMEM((LANES, 8 * channels), F32),
        window_turned=pltpu.VMEM((LANES, 4 * frames), BF16),
    )
    plan = types.SimpleNamespace(
        sizes=sizes,
        frames=frames,
        bins=bins,
        count=count,
        width=width,
        channels=channels,
        heads=heads,
        radius=conv_depth.shape[0] // 2,
        time_masks=time_spans.shape[1],
        freq_masks=freq_spans.shape[1],
        sources=gather_sources,
        grads=grads,
        pieces=pieces,
        turns=turns,
        sums=sums,
        steps=order_of_steps(sums, grads),
        small_moment=SMALL_MOMENT,
    )
    kinds = ({name: 0 for name in inputs}, {name: 0 for name in outputs}, scratch)
    plan.trees = [jax.tree.structure(kind) for kind in kinds]
    results = pl.pallas_call(
        functools.partial(layer_kernel, plan),
        out_shape=[jax.ShapeDtypeStruct(*spec) for _, spec in sorted(outputs.items())],
        in_specs=[pl.BlockSpec(memory_space=space) for _, (_, space) in sorted(inputs.items())],
        out_specs=[pl.BlockSpec(memory_space=pltpu.VMEM)] * len(outputs),
        scratch_shapes=jax.tree.leaves(scratch),
        compiler_params=pltpu.CompilerParams(
            collective_id=0, has_side_effects=True, vmem_limit_bytes=63 * 2**20
        ),
        name="layer",
    )(*[value for _, (value, _) in sorted(inputs.items())])
    made = types.SimpleNamespace(**dict(zip(sorted(outputs), results)))
    finals = [
        (made.mel_grad, made.mel_grad.shape),
        (made.activations, tokens),
        (made.grad_kernels, made.grad_kernels.shape),
        (made.grad_point, made.grad_point.shape),
        (made.grad_stem, stem_out.shape),
        (made.grad_inner, ffn_in.shape),
        (made.grad_outer, ffn_out.shape),
        (made.grad_qkv, qkv.shape),
        (made.grad_attn, attn_out.shape),
        (made.grad_conv_in, conv_in.shape),
        (made.grad_depth, conv_depth.shape),
        (made.grad_conv_out, conv_out.shape),
        (made.grad_gains, norm_gains.shape),
        (made.grad_shifts, norm_shifts.shape),
        (made.grad_final, made.grad_final.shape),
    ]
    done = pl.pallas_call(
        functools.partial(finish_kernel, len(finals)),
        out_shape=[jax.ShapeDtypeStruct(shape, value.dtype) for value, shape in finals],
        in_specs=[pl.BlockSpec(memory_space=pltpu.VMEM)] * len(finals),
        out_specs=[pl.BlockSpec(memory_space=pltpu.VMEM)] * len(finals),
        name="finish",
    )(*[value for value, _ in finals])
    return (
        done[1],
        done[0].T,
        done[2].swapaxes(1, 2),
        done[3].reshape(stem_point.shape),
        *done[4:14],
        done[14].reshape(final_shift.shape),
    )


def solution(mesh):
    return jax.shard_map(
        local,
        mesh=mesh,
        in_specs=(
            P(AXES, None),
            P(AXES, None),
            P(),
            P(),
            P(AXES, None, None),
            P(AXES, None, None),
            P(),
            P(None, None, AXES),
            P(None, AXES, None),
            P(AXES, None),
            P(None, AXES, None),
            P(None, AXES, None),
            P(AXES, None),
            P(AXES, None),
            P(AXES, None),
            P(None, AXES),
            P(AXES, None),
            P(None, AXES),
            P(None, AXES),
            P(AXES),
        ),
        out_specs=(
            P(AXES, None),
            P(AXES, None),
            P(None, None, AXES),
            P(None, AXES, None),
            P(AXES, None),
            P(None, AXES, None),
            P(None, AXES, None),
            P(AXES, None),
            P(AXES, None),
            P(AXES, None),
            P(None, AXES),
            P(AXES, None),
            P(None, AXES),
            P(None, AXES),
            P(AXES),
        ),
        check_vma=False,
    )
```

```python
import functools
import types

import jax
import jax.numpy as jnp
from jax import lax
from jax.experimental import pallas as pl
from jax.experimental.pallas import tpu as pltpu
from jax.sharding import PartitionSpec as P

CTX = 128


EPSILON = 1e-05
MASKED_LOGIT = -1e30
MESH = pl.DeviceIdType.MESH
CORES = 2
AXES = ("dp", "fsdp")
LANES = 128
BINS = 24
GROUPS = 5
TILE = 16
PART = 32
F32 = jnp.float32
BF16 = jnp.bfloat16


def grid_sizes():
    dp, fsdp = lax.axis_size(AXES[0]), lax.axis_size(AXES[1])
    high = 2 if dp % 2 == 0 else 1
    return (high, dp // high, fsdp // CORES, CORES)


def own_place(sizes):
    dp, fsdp = lax.axis_index(AXES[0]), lax.axis_index(AXES[1])
    return (dp // sizes[1], dp % sizes[1], fsdp // CORES, fsdp % CORES)


def peer_on(place, sizes, digit, step):
    other = list(place)
    other[digit] = (place[digit] + step) % sizes[digit]
    return tuple(other)


def device_of(place, sizes):
    return (place[0] * sizes[1] + place[1], place[2] * CORES + place[3])


def send(src, dst, device, send_sem, recv_sem):
    copy = pltpu.make_async_remote_copy(
        src_ref=src,
        dst_ref=dst,
        send_sem=send_sem,
        recv_sem=recv_sem,
        device_id=device,
        device_id_type=MESH,
    )
    copy.start()
    return copy


def group_peers(sizes):
    dp, fsdp = lax.axis_index(AXES[0]), lax.axis_index(AXES[1])
    dp_size, fsdp_size = sizes[0] * sizes[1], sizes[2] * CORES
    near = [(dp, (fsdp + step) % fsdp_size) for step in range(1, fsdp_size)]
    far = [((dp + step) % dp_size, fsdp) for step in range(1, dp_size)]
    return near, far


def greet(sizes):
    near, far = group_peers(sizes)
    for device in near + far:
        pl.semaphore_signal(
            pltpu.get_barrier_semaphore(), inc=1, device_id=device, device_id_type=MESH
        )


def await_greetings(sizes):
    near, far = group_peers(sizes)
    pl.semaphore_wait(pltpu.get_barrier_semaphore(), len(near) + len(far))


def iota(shape, axis):
    return lax.broadcasted_iota(jnp.int32, shape, axis)


def flags(condition):
    return jnp.where(condition, 1.0, 0.0)


def mm(left, right):
    return jnp.dot(left, right, preferred_element_type=F32)


def mm_t(left, right):
    return lax.dot_general(left, right, (((1,), (1,)), ((), ())), preferred_element_type=F32)


def rows_of(value):
    return value.reshape(-1, value.shape[-1])


def sigmoid(value):
    return 0.5 + 0.5 * jnp.tanh(0.5 * value)


def silu(value):
    half = 0.5 * value
    return half + half * jnp.tanh(half)


def silu_and_slope(value):
    gate = sigmoid(value)
    out = value * gate
    return out, gate + out * (1.0 - gate)


def normalized(value):
    centred = value - jnp.mean(value, axis=-1, keepdims=True)
    scale = lax.rsqrt(jnp.mean(centred * centred, axis=-1, keepdims=True) + EPSILON)
    return centred * scale, scale


def layer_norm(value, gain, shift):
    return normalized(value)[0] * gain + shift


def layer_norm_back(value, gain, grad):
    unit, scale = normalized(value)
    inner = grad * gain
    centre = jnp.mean(inner, axis=-1, keepdims=True)
    along = jnp.mean(inner * unit, axis=-1, keepdims=True)
    grad_value = scale * (inner - centre - unit * along)
    return grad_value, column_sum(grad * unit), column_sum(grad)


def column_sum(value):
    return jnp.sum(value, axis=0, keepdims=True)


def shift_rows(value, step):
    rows = value.shape[0]
    step = step % rows
    return value if step == 0 else pltpu.roll(value, step, 0)


TAP_ROW, GAIN_ROW, SHIFT_ROW, FINAL_ROW = 0, 9, 15, 20


def layer_kernel(plan, *refs):
    fields, at = {}, 0
    for tree in plan.trees:
        fields |= tree.unflatten(refs[at : at + tree.num_leaves])
        at += tree.num_leaves
    v = types.SimpleNamespace(**fields)
    sizes, frames, bins = plan.sizes, plan.frames, plan.bins
    place = own_place(sizes)
    a, b, z, c = place
    mate = device_of(peer_on(place, sizes, 3, 1), sizes)
    device = lax.axis_index(AXES[0]) * (sizes[2] * CORES) + lax.axis_index(AXES[1])
    count = plan.count
    pending = []

    def arrive(copies):
        for copy in copies:
            copy.wait_recv()
        pending.extend(copies)


    sources = plan.sources(v)
    held = v.held
    opened, first, second, third = {}, {}, {}, {}

    def halves(start, width):
        half = width // 2
        if half % LANES:
            return (pl.ds(start, width),)
        return (pl.ds(start, half), pl.ds(start + half, half))

    def open_piece(p):
        item, start, width = plan.pieces[p]
        lanes = pl.ds(start, width)
        source, own = sources[item].at[:, lanes], held[item].at[a, b, z, c, :, lanes]
        keep = pltpu.make_async_copy(source, own, v.g_local.at[p])
        keep.start()
        opened[p] = (
            keep,
            [
                send(
                    source,
                    own,
                    device_of(peer_on(place, sizes, 2, step), sizes),
                    v.g_z.at[0, p, step - 1],
                    v.g_z.at[1, p, step - 1],
                )
                for step in range(1, sizes[2])
            ],
        )

    def hop_piece(p, hop):
        item, start, width = plan.pieces[p]
        copies = []
        for order, lanes in enumerate(halves(start, width)):
            digit = 1 - order if hop == 0 else order
            if hop == 0:
                part = held[item].at[a, b, :, c, :, lanes]
            elif order == 0:
                part = held[item].at[a, :, :, c, :, lanes]
            else:
                part = held[item].at[:, b, :, c, :, lanes]
            for step in range(1, sizes[digit]):
                copies.append(
                    send(
                        part,
                        part,
                        device_of(peer_on(place, sizes, digit, step), sizes),
                        v.g_hop.at[0, p, hop, order, step - 1],
                        v.g_hop.at[1, p, hop, order, step - 1],
                    )
                )
        return copies

    state = types.SimpleNamespace(turn=0)
    turns = plan.turns

    def pieces_at(at):
        return turns[at] if 0 <= at < len(turns) else ()

    def turn():
        at = state.turn
        state.turn += 1
        for p in pieces_at(at + 2):
            open_piece(p)
        for p in pieces_at(at):
            opened[p][0].wait()
            arrive(opened[p][1])
            first[p] = hop_piece(p, 0)
        for p in pieces_at(at - 1):
            arrive(first[p])
            second[p] = hop_piece(p, 1)
        for p in pieces_at(at - 2):
            arrive(second[p])
            item, start, width = plan.pieces[p]
            part = held[item].at[:, :, :, c, :, pl.ds(start, width)]
            third[p] = [send(part, part, mate, v.g_core.at[0, p], v.g_core.at[1, p])]
        for p in pieces_at(at - 3):
            arrive(third[p])

    def need(item):
        last = max(
            at for at, ps in enumerate(turns) for p in ps if plan.pieces[p][0] == item
        )
        while state.turn < last + 4:
            turn()

    greet(sizes)
    v.packed[...] = jnp.zeros(v.packed.shape, F32)
    for row, piece in (
        (TAP_ROW, v.conv_depth),
        (GAIN_ROW, v.norm_gains),
        (SHIFT_ROW, v.norm_shifts),
        (FINAL_ROW, v.final_shift),
    ):
        v.packed[row : row + piece.shape[0], : piece.shape[1]] = piece[...].astype(F32)
    for layer in range(3):
        row = 32 + 9 * layer
        v.packed[row : row + 9, : v.stem_kernels.shape[1]] = v.stem_kernels[layer].astype(F32).T
    v.small[...] = v.packed[...].astype(BF16)
    for layer in range(2):
        at = layer * plan.channels
        v.point[:, at : at + plan.channels] = v.stem_point[layer].astype(F32)
    await_greetings(sizes)
    for at in range(2):
        for p in pieces_at(at):
            open_piece(p)


    own_len = jnp.where(v.assignment[...] == device, v.lengths[...], 0)
    utterances = own_len.shape[1]
    upto = flags(
        iota((utterances, utterances), 0) <= iota((utterances, utterances), 1)
    ).astype(BF16)
    own_low = jnp.broadcast_to(own_len.astype(F32), (TILE, utterances)).astype(BF16)
    finish = mm(own_low, upto)[:1]
    begin = finish - own_len.astype(F32)
    at_frame = iota((frames, utterances), 0).astype(F32)
    inside = flags((at_frame >= begin) & (at_frame < finish))
    same = mm_t(inside.astype(BF16), inside.astype(BF16))
    present = jnp.sum(inside, axis=1, keepdims=True)
    ahead = iota((frames, frames), 1) - iota((frames, frames), 0)

    def same_at(step):
        return jnp.sum(jnp.where(ahead == step, same, 0.0), axis=1, keepdims=True)

    joint = same_at(-1)
    counted = jnp.sum(v.lengths[...].astype(F32), axis=1, keepdims=True)


    bin_at = iota((1, LANES), 1)
    bin_keep = bin_at < bins
    for mask in range(plan.freq_masks):
        start, width = v.freq_spans[0, mask, 0], v.freq_spans[0, mask, 1]
        bin_keep = bin_keep & jnp.logical_not((bin_at >= start) & (bin_at < start + width))
    bin_keep = flags(bin_keep)

    def keep_of(phase):
        at = iota((frames, 1), 0) * 8 + phase
        keep = present
        for mask in range(plan.time_masks):
            start, width = v.time_spans[0, mask, 0], v.time_spans[0, mask, 1]
            keep = jnp.where((at >= start) & (at < start + width), 0.0, keep)
        return keep * bin_keep

    for phase in range(8):
        at = pl.ds(phase * frames, frames)
        v.frames_wide[at, :bins] = v.mel[:, at].astype(F32).T
    for phase in range(8):
        masked = jnp.where(
            keep_of(phase) > 0.5, v.frames_wide[pl.ds(phase, frames, stride=8), :], 0.0
        )
        v.feats[phase + 1] = masked
        if phase == 7:
            v.feats[0] = shift_rows(masked, 1) * joint
    lane = iota((1, LANES), 1)

    def band(tap):
        return (lane >= BINS * tap) & (lane < BINS * tap + 17)

    for group in range(GROUPS):
        if group % 2 == 0:
            turn()
        for phase in range(4):
            total = jnp.zeros((frames, LANES), F32)
            for tap in range(3):
                moved = pltpu.roll(
                    v.feats[2 * phase + tap], (BINS * tap - 16 * group + 1) % LANES, 1
                )
                total = jnp.where(band(tap), moved, total)
            v.windows[group, pl.ds(phase * frames, frames)] = total.astype(BF16)


    need(0)
    devices = sizes[0] * sizes[1] * sizes[2] * CORES

    def spread(rows, width, target):
        each = width // devices
        per_tile = LANES // each
        for tile in range(width // LANES):
            total = jnp.zeros((32, LANES), F32)
            for k in range(per_tile):
                d = tile * per_tile + k
                index = (
                    d // (sizes[1] * sizes[2] * CORES),
                    d // (sizes[2] * CORES) % sizes[1],
                    d // CORES % sizes[2],
                    d % CORES,
                )
                piece = held[0][index][rows : rows + 32].astype(F32)
                total = total + (pltpu.roll(piece, each * k, 1) if k else piece)
            target[:, tile * LANES : (tile + 1) * LANES] = total

    width = plan.width
    channels = plan.channels
    spread(0, width, v.params)
    spread(32, channels, v.kernels)

    def param(row):
        return v.params[row : row + 1]

    def kernel_row(layer, tap, lanes):
        return v.kernels[9 * layer + tap : 9 * layer + tap + 1, lanes]

    every = pl.ds(0, channels)
    for f in range(8):
        v.band_wide[...] = jnp.zeros((LANES, channels), F32)
        for tap in range(9):
            row = BINS * (tap // 3) + 2 * f + tap % 3
            v.band_wide[row : row + 1] = kernel_row(0, tap, every)
        v.banded[:, f * channels : (f + 1) * channels] = v.band_wide[...].astype(BF16)

    need(1)
    point = held[1][...]
    point = point.reshape(-1, point.shape[-1])
    v.points[0] = point[:, :channels].astype(BF16)
    v.points[1] = point[:, channels:].astype(BF16)

    def wide_chunks(extent):
        step = min(extent, 4 * LANES)
        return [slice(start, start + step) for start in range(0, extent, step)]


    grads = plan.grads
    left_sent = {}
    OUTER1, INNER1, CONV_OUT, CONV_IN, ATTN, QKV, OUTER0, INNER0, STEM, POINT, WIDE, TAPS = range(12)

    def transposed(value):
        return jnp.transpose(value.astype(F32)).astype(BF16)

    def start_left(i, left):
        columns = v.columns[i]
        per_part = left.shape[1] // (sizes[0] * sizes[1])
        for high in range(sizes[0]):
            for low in range(sizes[1]):
                start = (high * sizes[1] + low) * per_part
                part = transposed(left[:, start : start + per_part])
                columns[high, low] = part.reshape(columns.shape[2:])
        left_sent[i] = [
            send(
                columns.at[:, :, :, 1 - c],
                v.mates[i],
                mate,
                v.s_core.at[0, i, 0],
                v.s_core.at[1, i, 0],
            )
        ]


    def phase_rows(ref, phase, lanes):
        return ref[pl.ds(phase * frames, frames), lanes]

    chunks = [pl.ds(LANES * k, LANES) for k in range(channels // LANES)]
    v.ones_wide[2] = jnp.zeros(v.ones_wide.shape[1:], F32)
    v.two_odd[1] = jnp.zeros(v.two_odd.shape[1:], F32)

    def stem_step(group, half):
        three = 2 * group + half
        for side in range(2):
            two = 2 * three + side
            low = 4 * half + 2 * side
            window = v.windows[group]
            for f, slot in ((0, 0), (1, 1 + side)):
                at = pl.multiple_of((low + f) * channels, channels)
                value = silu(mm(window, v.banded[:, pl.ds(at, channels)]))
                v.ones_wide[slot] = value
            pieces = (v.ones_wide.at[2 - side], v.ones_wide.at[0], v.ones_wide.at[1 + side])
            for lanes in chunks:
                late = early = odd = None
                for column, piece in enumerate(pieces):
                    w0, w1, w2 = (kernel_row(1, 3 * row + column, lanes) for row in range(3))
                    p0, p1, p2, p3 = (phase_rows(piece, phase, lanes) for phase in range(4))
                    carried = w0 * p3
                    even = w1 * p0 + w2 * p1
                    after = w0 * p1 + w1 * p2 + w2 * p3
                    late = carried if late is None else late + carried
                    early = even if early is None else early + even
                    odd = after if odd is None else odd + after
                early = early + shift_rows(late, 1) * joint
                v.level_now[pl.ds(0, frames), lanes] = early.astype(BF16)
                v.level_now[pl.ds(frames, frames), lanes] = odd.astype(BF16)
            v.level_two[two] = transposed(v.level_now[...])
            point_two = mm(v.level_now[...], v.points[0])
            v.point_two[two] = point_two.astype(BF16)
            hidden = silu(point_two)
            if side == 0:
                v.two_even[...] = hidden
            else:
                v.two_odd[half] = hidden
        pieces = (v.two_odd.at[1 - half], v.two_even, v.two_odd.at[half])
        for lanes in chunks:
            late = total = None
            for column, piece in enumerate(pieces):
                w0, w1, w2 = (kernel_row(2, 3 * row + column, lanes) for row in range(3))
                p0, p1 = (phase_rows(piece, phase, lanes) for phase in range(2))
                carried = w0 * p1
                now = w1 * p0 + w2 * p1
                late = carried if late is None else late + carried
                total = now if total is None else total + now
            total = total + shift_rows(late, 1) * joint
            v.level_now[pl.ds(0, frames), lanes] = total.astype(BF16)
        level_three = v.level_now[pl.ds(0, frames)]
        v.level_three[three] = transposed(level_three)
        point_three = mm(level_three, v.points[1])
        v.point_three[three] = point_three.astype(BF16)
        at = pl.multiple_of(three * channels, channels)
        v.stem_hidden[:, pl.ds(at, channels)] = silu(point_three).astype(BF16)

    for group in range(GROUPS):
        lax.fori_loop(0, 2, lambda half, carry: (stem_step(group, half), carry)[1], 0)
        turn()

    bins_three = 2 * GROUPS


    start_left(STEM, v.stem_hidden)
    need(2)
    v.after_stem[...] = mm(v.stem_hidden[...], rows_of(held[2][...]))

    def ffn(stream, row, inner, outer, normed_ref, hidden_ref, active_ref, items):
        normed_ref[...] = layer_norm(stream, param(GAIN_ROW + row), param(SHIFT_ROW + row)).astype(BF16)
        start_left(items[0], normed_ref)
        need(inner)
        for lanes in wide_chunks(hidden_ref.shape[1]):
            hidden = mm(normed_ref[...], rows_of(held[inner][:, :, :, :, :, lanes]))
            hidden_ref[:, lanes] = hidden.astype(BF16)
            active_ref[:, lanes] = silu(hidden).astype(BF16)
        start_left(items[1], active_ref)
        need(outer)
        return mm(active_ref[...], rows_of(held[outer][...]))

    v.after_ffn[...] = v.after_stem[...] + 0.5 * ffn(
        v.after_stem[...], 0, 3, 4, v.normed0, v.hidden0, v.active0, (INNER0, OUTER0)
    )
    v.normed1[...] = layer_norm(
        v.after_ffn[...], param(GAIN_ROW + 1), param(SHIFT_ROW + 1)
    ).astype(BF16)
    start_left(QKV, v.normed1)
    need(5)
    for lanes in wide_chunks(3 * width):
        v.joined[:, lanes] = mm(v.normed1[...], rows_of(held[5][:, :, :, :, :, lanes])).astype(BF16)
    heads = plan.heads
    per_tile = LANES * heads // width
    head_width = width // heads
    apart = jnp.abs(ahead)

    def head_lanes(head):
        inner = head % per_tile
        return (lane >= inner * head_width) & (lane < (inner + 1) * head_width)

    def tile_of(ref, part, head):
        start = part * width + head // per_tile * LANES
        return ref[:, start : start + LANES]

    def only(value, head):
        return jnp.where(head_lanes(head), value.astype(F32), 0.0).astype(BF16)

    for tile in range(width // LANES):
        mixed = jnp.zeros((frames, LANES), F32)
        for head in range(tile * per_tile, (tile + 1) * per_tile):
            scores = mm_t(only(tile_of(v.joined, 0, head), head), tile_of(v.joined, 1, head))
            allowed = (same > 0.5) & (apart <= v.contexts[head])
            logits = jnp.where(allowed, scores * head_width ** (-0.5), MASKED_LOGIT)
            exponent = jnp.exp(logits - jnp.max(logits, axis=-1, keepdims=True))
            weights = exponent / jnp.sum(exponent, axis=-1, keepdims=True)
            v.weights[head] = weights
            out = mm(weights.astype(BF16), tile_of(v.joined, 2, head))
            mixed = jnp.where(head_lanes(head), out, mixed)
        v.mixed[:, tile * LANES : (tile + 1) * LANES] = mixed.astype(BF16)
    start_left(ATTN, v.mixed)
    need(6)
    v.after_attn[...] = v.after_ffn[...] + mm(v.mixed[...], rows_of(held[6][...]))
    v.normed2[...] = layer_norm(
        v.after_attn[...], param(GAIN_ROW + 2), param(SHIFT_ROW + 2)
    ).astype(BF16)
    start_left(CONV_IN, v.normed2)
    need(7)
    for lanes in wide_chunks(2 * width):
        v.gated[:, lanes] = mm(v.normed2[...], rows_of(held[7][:, :, :, :, :, lanes]))
    radius = plan.radius
    merged = v.gated[:, :width] * sigmoid(v.gated[:, width:])
    v.merged[...] = merged
    depthwise = jnp.zeros((frames, width), F32)
    for tap in range(2 * radius + 1):
        step = tap - radius
        depthwise = depthwise + shift_rows(merged, -step) * same_at(step) * param(TAP_ROW + tap)
    v.depthwise[...] = depthwise

    near, far = group_peers(sizes)
    blocks = width // LANES

    def open_total(which, rows):
        for row, value in enumerate(rows):
            for k in range(blocks):
                at = row * blocks + k
                v.t_own[which, at : at + 1] = value[:, k * LANES : (k + 1) * LANES]
        return [
            send(
                v.t_own.at[which],
                v.t_near.at[which, k],
                peer,
                v.t_sem.at[0, which, k],
                v.t_sem.at[1, which, k],
            )
            for k, peer in enumerate(near)
        ]

    def close_total(which, copies):
        arrive(copies)
        total = v.t_own[which]
        for k in range(len(near)):
            total = total + v.t_near[which, k]
        v.t_mid[which] = total
        copies = [
            send(
                v.t_mid.at[which],
                v.t_far.at[which, k],
                peer,
                v.t_sem.at[0, which, len(near) + k],
                v.t_sem.at[1, which, len(near) + k],
            )
            for k, peer in enumerate(far)
        ]
        arrive(copies)
        for k in range(len(far)):
            total = total + v.t_far[which, k]
        return [
            jnp.concatenate(
                [total[row * blocks + k : row * blocks + k + 1] for k in range(blocks)], axis=1
            )
            for row in range(2)
        ]

    counts = open_total(
        0, [column_sum(depthwise * present), column_sum(depthwise * depthwise * present)]
    )
    turn()
    first_sum, second_sum = close_total(0, counts)
    average = first_sum / counted
    spread_out = second_sum / counted - average * average
    inv_spread = lax.rsqrt(spread_out + EPSILON)
    v.standard[...] = (v.depthwise[...] - average) * inv_spread
    v.batch_normed[...] = v.standard[...] * param(GAIN_ROW + 3) + param(SHIFT_ROW + 3)
    v.conv_active[...] = silu(v.batch_normed[...]).astype(BF16)
    start_left(CONV_OUT, v.conv_active)
    need(8)
    v.after_conv[...] = v.after_attn[...] + mm(v.conv_active[...], rows_of(held[8][...]))
    v.after_second[...] = v.after_conv[...] + 0.5 * ffn(
        v.after_conv[...], 4, 9, 10, v.normed4, v.hidden1, v.active1, (INNER1, OUTER1)
    )
    gain_last, shift_last = param(GAIN_ROW + 5), param(FINAL_ROW)
    v.activations[...] = (
        layer_norm(v.after_second[...], gain_last, shift_last) * present
    ).astype(BF16)


    need(count - 1)
    for copy in pending:
        copy.wait_send()
    pending.clear()
    core_sent, hop_one, hop_two, z_sent = {}, {}, {}, {}
    sums = plan.sums

    def block_of(i):
        spec = grads[i]
        return held[spec.weight].at[:, :, :, 0] if spec.weight else v.kept[i]

    def right_of(i):
        return v.right[i].at[pl.ds(0, frames)]

    def start_product(i):
        core_sent[i] = left_sent[i] + [
            send(
                right_of(i),
                v.right[i].at[pl.ds(frames, frames)],
                mate,
                v.s_core.at[0, i, 1],
                v.s_core.at[1, i, 1],
            ),
        ]

    def start_sum(i):
        core_sent[i] = [
            send(
                v.parts[i].at[:, :, :, 1 - c],
                v.mates[i],
                mate,
                v.s_core.at[0, i, 0],
                v.s_core.at[1, i, 0],
            )
        ]

    def take_product(i):
        spec = grads[i]
        arrive(core_sent[i])
        block = block_of(i)
        if spec.product:
            own, mates, right = v.columns[i], v.mates[i], v.right[i]
            split = spec.block[0] > 2 * TILE
            columns = 2 * LANES
            steps = spec.block[1] // columns
            parts = sizes[0] * (sizes[1] if split else 1)

            def multiply(at, carry):
                part = at // steps
                lanes = pl.ds(pl.multiple_of(at % steps * columns, columns), columns)
                index = (part // sizes[1], part % sizes[1]) if split else (part,)
                middle = (slice(None),) * (3 - len(index))
                left = jnp.concatenate(
                    [rows_of(own[index + middle + (c,)]), rows_of(mates[index])], axis=1
                )
                product = mm(left, right[:, lanes]).astype(BF16)
                target = block.at[index + middle + (slice(None), lanes)]
                target[...] = product.reshape(target.shape)
                return carry

            lax.fori_loop(0, parts * steps, multiply, 0, unroll=4)
        else:
            own = v.parts[i][:, :, :, c].astype(F32)
            block[...] = (own + v.mates[i][...].astype(F32)).astype(BF16)

    def send_hop(p, hop):
        i, start, width = sums[p]
        block = block_of(i)
        copies = []
        for order, lanes in enumerate(halves(start, width)):
            digit = 1 - order if hop == 0 else order
            for step in range(1, sizes[digit]):
                other = peer_on(place, sizes, digit, step)
                if hop == 0:
                    part = block.at[:, other[1]] if order == 0 else block.at[other[0]]
                    part = part.at[:, :, :, lanes]
                else:
                    part = block.at[other[0], b] if order == 0 else block.at[a, other[1]]
                    part = part.at[:, :, lanes]
                copies.append(
                    send(
                        part,
                        v.landed[p][order][hop].at[step - 1],
                        device_of(other, sizes),
                        v.s_hop.at[0, p, hop, order, step - 1],
                        v.s_hop.at[1, p, hop, order, step - 1],
                    )
                )
        return copies

    def add_hop(p, hop):
        i, start, width = sums[p]
        block = block_of(i)
        for order, lanes in enumerate(halves(start, width)):
            digit = 1 - order if hop == 0 else order
            landed = v.landed[p][order][hop]
            if hop == 0:
                mine = block.at[:, b] if order == 0 else block.at[a]
                mine = mine.at[:, :, :, lanes]
            else:
                mine = block.at[a, b].at[:, :, lanes]
            lead = mine.shape[:-2]

            def add(at, carry):
                index = (at,) if len(lead) == 1 else (at // lead[1], at % lead[1])
                total = mine[index].astype(F32)
                for step in range(1, sizes[digit]):
                    total = total + landed[(step - 1,) + index].astype(F32)
                mine[index] = total.astype(BF16)
                return carry

            lax.fori_loop(
                0, lead[0] * (lead[1] if len(lead) > 1 else 1), add, 0, unroll=True
            )

    taken = set()

    def first_hop(p):
        if sums[p][0] not in taken:
            taken.add(sums[p][0])
            take_product(sums[p][0])
        hop_one[p] = send_hop(p, 0)

    def second_hop(p):
        arrive(hop_one[p])
        add_hop(p, 0)
        hop_two[p] = send_hop(p, 1)

    def third_hop(p):
        arrive(hop_two[p])
        add_hop(p, 1)
        i, start, width = sums[p]
        block = block_of(i)
        z_sent[p] = []
        for step in range(1, sizes[2]):
            other = peer_on(place, sizes, 2, step)
            z_sent[p].append(
                send(
                    block.at[a, b, other[2], :, pl.ds(start, width)],
                    v.landed_z[p].at[step - 1],
                    device_of(other, sizes),
                    v.s_z.at[0, p, step - 1],
                    v.s_z.at[1, p, step - 1],
                )
            )

    owned = (
        v.grad_outer.at[1],
        v.grad_inner.at[1],
        v.grad_conv_out,
        v.grad_conv_in,
        v.grad_attn,
        v.grad_qkv,
        v.grad_outer.at[0],
        v.grad_inner.at[0],
        v.grad_stem,
        v.grad_point,
        v.sum_wide,
        v.sum_taps,
    )

    def finish_sum(p):
        arrive(z_sent[p])
        i, start, width = sums[p]
        lanes = pl.ds(start, width)
        total = block_of(i)[a, b, z, :, lanes].astype(F32)
        for step in range(1, sizes[2]):
            total = total + v.landed_z[p][step - 1].astype(F32)
        owned[i][:, lanes] = total

    stages = (first_hop, second_hop, third_hop, finish_sum)
    progress = types.SimpleNamespace(at=0)

    def advance(moment):
        while progress.at < len(plan.steps) and plan.steps[progress.at][0] <= moment:
            _, stage, p = plan.steps[progress.at]
            stages[stage](p)
            progress.at += 1

    def add_param(row, value):
        v.d_params[row : row + 1] = value

    v.d_params[...] = jnp.zeros(v.d_params.shape, F32)

    grad = v.cotangent[...].astype(F32) * present
    grad_stream, gain_part, shift_part = layer_norm_back(v.after_second[...], gain_last, grad)
    add_param(GAIN_ROW + 5, gain_part)
    add_param(FINAL_ROW, shift_part)
    v.stream[...] = grad_stream

    def norm_back(row, value_ref, grad_normed):
        grad_value, gain_part, shift_part = layer_norm_back(
            value_ref[...], param(GAIN_ROW + row), grad_normed
        )
        add_param(GAIN_ROW + row, gain_part)
        add_param(SHIFT_ROW + row, shift_part)
        v.stream[...] = v.stream[...] + grad_value

    def ffn_back(row, stream_ref, inner, outer, hidden, items):
        out_grad, hidden_grad = right_of(items[0]), right_of(items[1])
        out_grad[...] = (0.5 * v.stream[...]).astype(BF16)
        start_product(items[0])
        start = 0
        for high in range(sizes[0]):
            for low in range(sizes[1]):
                rows = rows_of(held[outer][high, low])
                lanes = slice(start, start + rows.shape[0])
                start += rows.shape[0]
                slope = silu_and_slope(hidden[:, lanes].astype(F32))[1]
                hidden_grad[:, lanes] = (mm_t(out_grad[...], rows) * slope).astype(BF16)
        start_product(items[1])
        norm_back(row, stream_ref, mm_t(hidden_grad[...], rows_of(held[inner][...])))

    ffn_back(
        4,
        v.after_conv,
        9,
        10,
        v.hidden1,
        (OUTER1, INNER1),
    )
    right_of(CONV_OUT)[...] = v.stream[...].astype(BF16)
    start_product(CONV_OUT)
    grad_active = mm_t(right_of(CONV_OUT)[...], rows_of(held[8][...]))
    grad_batch = grad_active * silu_and_slope(v.batch_normed[...])[1] * present
    v.grad_batch[...] = grad_batch
    beta_own = column_sum(grad_batch)
    gamma_own = column_sum(grad_batch * v.standard[...])
    add_param(GAIN_ROW + 3, gamma_own)
    add_param(SHIFT_ROW + 3, beta_own)
    totals = open_total(1, [beta_own, gamma_own])
    advance(1)
    beta_sum, gamma_sum = close_total(1, totals)
    bn_gain = param(GAIN_ROW + 3)
    grad_first = (
        inv_spread * inv_spread * bn_gain * gamma_sum * average - inv_spread * bn_gain * beta_sum
    ) / counted
    grad_second = -0.5 * inv_spread * inv_spread * bn_gain * gamma_sum / counted
    grad_depth = bn_gain * inv_spread * v.grad_batch[...] + present * (
        grad_first + 2.0 * v.depthwise[...] * grad_second
    )
    grad_merged = jnp.zeros((frames, width), F32)
    for tap in range(2 * radius + 1):
        step = tap - radius
        part = grad_depth * same_at(step)
        add_param(TAP_ROW + tap, column_sum(part * shift_rows(v.merged[...], -step)))
        grad_merged = grad_merged + shift_rows(part, step) * param(TAP_ROW + tap)
    gate = sigmoid(v.gated[:, width:])
    right_of(CONV_IN)[:, :width] = (grad_merged * gate).astype(BF16)
    right_of(CONV_IN)[:, width:] = (grad_merged * v.merged[...] * (1.0 - gate)).astype(BF16)
    start_product(CONV_IN)
    norm_back(2, v.after_attn, mm_t(right_of(CONV_IN)[...], rows_of(held[7][...])))

    right_of(ATTN)[...] = v.stream[...].astype(BF16)
    start_product(ATTN)
    v.g_mixed[...] = mm_t(right_of(ATTN)[...], rows_of(held[6][...])).astype(BF16)
    for tile in range(width // LANES):
        advance(10 + tile)
        parts = [jnp.zeros((frames, LANES), F32) for _ in range(3)]
        mixed_grad = v.g_mixed[:, tile * LANES : (tile + 1) * LANES]
        for head in range(tile * per_tile, (tile + 1) * per_tile):
            weights = v.weights[head]
            grad_weights = mm_t(only(mixed_grad, head), tile_of(v.joined, 2, head))
            row_dot = jnp.sum(weights * grad_weights, axis=-1, keepdims=True)
            grad_scores = weights * (grad_weights - row_dot) * head_width ** (-0.5)
            pieces = (
                mm(grad_scores.astype(BF16), tile_of(v.joined, 1, head)),
                mm(transposed(grad_scores), tile_of(v.joined, 0, head)),
                mm(transposed(weights), mixed_grad),
            )
            parts = [
                jnp.where(head_lanes(head), piece, part) for piece, part in zip(pieces, parts)
            ]
        for k, part in enumerate(parts):
            start = k * width + tile * LANES
            right_of(QKV)[:, start : start + LANES] = part.astype(BF16)
    start_product(QKV)
    norm_back(1, v.after_ffn, mm_t(right_of(QKV)[...], rows_of(held[5][...])))
    ffn_back(
        0,
        v.after_stem,
        3,
        4,
        v.hidden0,
        (OUTER0, INNER0),
    )
    advance(15)
    right_of(STEM)[...] = v.stream[...].astype(BF16)
    start_product(STEM)
    start = 0
    for high in range(sizes[0]):
        for low in range(sizes[1]):
            rows = rows_of(held[2][high, low])
            lanes = slice(start, start + rows.shape[0])
            start += rows.shape[0]
            v.g_three[:, lanes] = mm_t(right_of(STEM)[...], rows).astype(BF16)
    def gather_columns(i, source, width):
        each = width // devices
        for d in range(devices):
            index = (
                d // (sizes[1] * sizes[2] * CORES),
                d // (sizes[2] * CORES) % sizes[1],
                d // CORES % sizes[2],
                d % CORES,
            )
            tile, k = d * each // LANES, d * each % LANES
            piece = source[:, tile * LANES : (tile + 1) * LANES]
            piece = pltpu.roll(piece, LANES - k, 1) if k else piece
            v.parts[i][index] = jnp.where(lane < each, piece, 0.0).astype(BF16)

    gather_columns(WIDE, v.d_params, width)
    start_sum(WIDE)
    advance(STEM_MOMENT)


    v.d_kernels[...] = jnp.zeros(v.d_kernels.shape, F32)
    v.d_points[...] = jnp.zeros(v.d_points.shape, F32)
    v.d_windows[...] = jnp.zeros(v.d_windows.shape, F32)
    v.d_banded[...] = jnp.zeros(v.d_banded.shape, F32)
    v.d_three[0] = jnp.zeros(v.d_three.shape[1:], F32)
    v.d_two_even[0] = jnp.zeros(v.d_two_even.shape[1:], BF16)

    def add_kernel(layer, tap, lanes, value):
        folded = jnp.sum(value.reshape(-1, 8, LANES), axis=0)
        v.d_kernels[9 * layer + tap, :, lanes] += folded

    def stem_back(group, half, moment):
        three = 2 * group + half
        at = pl.multiple_of(three * channels, channels)
        slope = silu_and_slope(v.point_three[three].astype(F32))[1]
        grad_point = (v.g_three[:, pl.ds(at, channels)].astype(F32) * slope).astype(BF16)
        v.d_points[1] += mm(v.level_three[three], grad_point)
        level_grad = mm_t(grad_point, v.points[1])
        v.d_three[half, pl.ds(0, frames)] = level_grad
        v.d_three[half, pl.ds(frames, frames)] = shift_rows(level_grad * joint, -1)
        here, above = v.d_three.at[half], v.d_three.at[1 - half]
        for lanes in chunks:
            k = [kernel_row(2, tap, lanes) for tap in range(9)]
            d, ds = (phase_rows(here, phase, lanes) for phase in range(2))
            n, ns = (phase_rows(above, phase, lanes) for phase in range(2))
            two = 2 * three
            h0, s0 = silu_and_slope(v.point_two[two, pl.ds(0, frames), lanes].astype(F32))
            h1, s1 = silu_and_slope(v.point_two[two, pl.ds(frames, frames), lanes].astype(F32))
            v.g_two[0, pl.ds(0, frames), lanes] = (k[4] * d * s0).astype(BF16)
            v.g_two[0, pl.ds(frames, frames), lanes] = ((k[7] * d + k[1] * ds) * s1).astype(BF16)
            add_kernel(2, 1, lanes, ds * h1)
            add_kernel(2, 4, lanes, d * h0)
            add_kernel(2, 7, lanes, d * h1)
            two = 2 * three + 1
            h0, s0 = silu_and_slope(v.point_two[two, pl.ds(0, frames), lanes].astype(F32))
            h1, s1 = silu_and_slope(v.point_two[two, pl.ds(frames, frames), lanes].astype(F32))
            v.g_two[1, pl.ds(0, frames), lanes] = ((k[5] * d + k[3] * n) * s0).astype(BF16)
            v.g_two[1, pl.ds(frames, frames), lanes] = (
                (k[8] * d + k[2] * ds + k[6] * n + k[0] * ns) * s1
            ).astype(BF16)
            add_kernel(2, 2, lanes, ds * h1)
            add_kernel(2, 5, lanes, d * h0)
            add_kernel(2, 8, lanes, d * h1)
            add_kernel(2, 0, lanes, ns * h1)
            add_kernel(2, 3, lanes, n * h0)
            add_kernel(2, 6, lanes, n * h1)
        for side in range(2):
            low_grad = v.g_two[side]
            v.d_points[0] += mm(v.level_two[2 * three + side], low_grad)
            level_grad = mm_t(low_grad, v.points[0])
            target = v.d_two_odd if side else v.d_two_even.at[half]
            target[pl.ds(0, 2 * frames)] = level_grad.astype(BF16)
            carried = shift_rows(level_grad[:frames] * joint, -1)
            target[pl.ds(2 * frames, frames)] = carried.astype(BF16)
        advance(moment + STEM_STEP / 3)
        low = 4 * half
        for f in range(4):
            at = (low + f) * channels
            v.ones[f] = mm(v.windows[group], v.banded[:, at : at + channels]).astype(BF16)
        for side in (1, 0):
            here = v.d_two_odd if side else v.d_two_even.at[half]
            above = v.d_two_even.at[1 - half] if side else v.d_two_odd
            for lanes in chunks:
                k = [
                    jnp.broadcast_to(kernel_row(1, tap, lanes), (PART, LANES)).astype(BF16)
                    for tap in range(9)
                ]

                def convolve_back(part, carry, k=k, lanes=lanes, side=side, here=here, above=above):
                    def rows_at(phase):
                        return pl.ds(pl.multiple_of(phase * frames + part * PART, PART), PART)

                    def level_one(f, phase):
                        half_value = v.ones[2 * side + f, rows_at(phase), lanes] * 0.5
                        bend = jnp.tanh(half_value)
                        gate = 0.5 + 0.5 * bend
                        out = half_value + half_value * bend
                        return out, gate + out * (1.0 - gate)

                    def put(f, phase, value):
                        at = pl.multiple_of((2 * side + f) * channels, channels)
                        at = pl.ds(at + lanes.start, LANES)
                        v.g_one[rows_at(phase), at] = value

                    def add(tap, value):
                        value = value.astype(F32).reshape(-1, 8, LANES)
                        v.d_kernels[9 + tap, :, lanes] += jnp.sum(value, axis=0)

                    d0, d1, ds = (here[rows_at(phase), lanes] for phase in range(3))
                    n0, n1, ns = (above[rows_at(phase), lanes] for phase in range(3))
                    h, s = level_one(0, 0)
                    put(0, 0, k[4] * d0 * s)
                    middle = d0 * h
                    h, s = level_one(0, 1)
                    put(0, 1, (k[7] * d0 + k[1] * d1) * s)
                    before, behind = d1 * h, d0 * h
                    h, s = level_one(0, 2)
                    put(0, 2, k[4] * d1 * s)
                    middle = middle + d1 * h
                    h, s = level_one(0, 3)
                    put(0, 3, (k[7] * d1 + k[1] * ds) * s)
                    add(1, before + ds * h)
                    add(4, middle)
                    add(7, behind + d1 * h)
                    h, s = level_one(1, 0)
                    put(1, 0, (k[5] * d0 + k[3] * n0) * s)
                    middle, middle_n = d0 * h, n0 * h
                    h, s = level_one(1, 1)
                    put(1, 1, (k[8] * d0 + k[2] * d1 + k[6] * n0 + k[0] * n1) * s)
                    before, behind = d1 * h, d0 * h
                    before_n, behind_n = n1 * h, n0 * h
                    h, s = level_one(1, 2)
                    put(1, 2, (k[5] * d1 + k[3] * n1) * s)
                    middle, middle_n = middle + d1 * h, middle_n + n1 * h
                    h, s = level_one(1, 3)
                    put(1, 3, (k[8] * d1 + k[2] * ds + k[6] * n1 + k[0] * ns) * s)
                    add(2, before + ds * h)
                    add(5, middle)
                    add(8, behind + d1 * h)
                    add(0, before_n + ns * h)
                    add(3, middle_n)
                    add(6, behind_n + n1 * h)
                    return carry

                lax.fori_loop(0, frames // PART, convolve_back, 0, unroll=True)
            advance(moment + STEM_STEP * (3 - side) / 3)
        at = pl.ds(low * channels, 4 * channels)
        v.d_windows[group] += mm_t(v.g_one[...], v.banded[:, at])
        v.d_banded[:, at] += mm(v.window_turned[...], v.g_one[...])

    for number in range(bins_three):
        three = bins_three - 1 - number
        if three % 2:
            v.window_turned[...] = transposed(v.windows[three // 2])
        stem_back(three // 2, three % 2, STEM_MOMENT + STEM_STEP * number)


    for layer in range(1, 3):
        for tap in range(9):
            row = 9 * layer + tap
            v.d_taps[row : row + 1] = column_sum(v.d_kernels[row])
    for tap in range(9):
        total = None
        for f in range(8):
            row = BINS * (tap // 3) + 2 * f + tap % 3
            piece = v.d_banded[row : row + 1, f * channels : (f + 1) * channels]
            total = piece if total is None else total + piece
        v.d_taps[tap : tap + 1] = total
    v.d_taps[27:32] = jnp.zeros((5, channels), F32)

    gather_columns(TAPS, v.d_taps, channels)
    shape = sizes + (channels // devices, channels)
    v.parts[POINT][...] = jnp.concatenate(
        [v.d_points[0].reshape(shape), v.d_points[1].reshape(shape)], axis=4
    ).astype(BF16)
    for i in (POINT, TAPS):
        start_sum(i)
    advance(plan.small_moment)


    for phase in range(9):
        v.feats[phase] = jnp.zeros((frames, LANES), F32)
    for group in range(GROUPS):
        for phase in range(4):
            rows = v.d_windows[group, pl.ds(phase * frames, frames)]
            for tap in range(3):
                piece = jnp.where(band(tap), rows, 0.0)
                back = (16 * group - 1 - BINS * tap) % LANES
                v.feats[2 * phase + tap] += pltpu.roll(piece, back, 1)
    for phase in range(8):
        total = v.feats[phase + 1]
        if phase == 7:
            total = total + shift_rows(v.feats[0] * joint, -1)
        v.frames_wide[pl.ds(phase, frames, stride=8), :] = total * keep_of(phase)

    for phase in range(8):
        at = pl.ds(phase * frames, frames)
        v.mel_grad[:, at] = v.frames_wide[at, :].T[:bins]

    advance(float("inf"))
    wide = v.sum_wide[...]
    each = width // devices
    v.grad_depth[...] = wide[TAP_ROW:GAIN_ROW, :each]
    v.grad_gains[...] = wide[GAIN_ROW:SHIFT_ROW, :each]
    v.grad_shifts[...] = wide[SHIFT_ROW:FINAL_ROW, :each]
    v.grad_final[...] = wide[FINAL_ROW : FINAL_ROW + 1, :each]
    taps = v.sum_taps[...].T
    for layer in range(3):
        v.grad_kernels[layer] = taps[: channels // devices, 9 * layer : 9 * layer + 9]
    for copy in pending:
        copy.wait_send()


def frame_segments(lengths, assignment, device, frames):
    belongs = assignment == device
    own_sizes = jnp.where(belongs, lengths, 0)
    finishes = jnp.cumsum(own_sizes, dtype=jnp.int32)
    beginnings = finishes - own_sizes
    position = jnp.arange(frames, dtype=jnp.int32)[:, None]
    inside = belongs[None, :] & (position >= beginnings[None, :]) & (position < finishes[None, :])
    number = jnp.arange(lengths.shape[0], dtype=jnp.int32)[None, :] + 1
    return jnp.sum(jnp.where(inside, number, 0), axis=1, dtype=jnp.int32) - 1


def feature_keep(segments, time_spans, freq_spans, mel_bins):
    frames = segments.shape[0] * 8
    position = jnp.arange(frames, dtype=jnp.int32)[:, None]
    covered = (position >= time_spans[None, :, 0]) & (
        position < time_spans[None, :, 0] + time_spans[None, :, 1]
    )
    time_keep = jnp.repeat(segments >= 0, 8) & jnp.logical_not(jnp.any(covered, axis=1))
    channel = jnp.arange(mel_bins, dtype=jnp.int32)[:, None]
    banned = (channel >= freq_spans[None, :, 0]) & (
        channel < freq_spans[None, :, 0] + freq_spans[None, :, 1]
    )
    freq_keep = jnp.logical_not(jnp.any(banned, axis=1))
    return (time_keep[:, None] & freq_keep[None, :]).astype(jnp.float32)


def time_taps(values, seg_in, seg_out):
    out_len = seg_out.shape[0]
    paired = values.reshape((out_len, 2) + values.shape[1:])
    even_part = paired[:, 0]
    odd_part = paired[:, 1]
    prior_part = jnp.concatenate([jnp.zeros_like(odd_part[:1]), odd_part[:-1]], axis=0)
    seg_pairs = seg_in.reshape(out_len, 2)
    prior_segs = jnp.concatenate([jnp.full((1,), -2, jnp.int32), seg_pairs[:-1, 1]])
    opening = ((prior_segs == seg_out) & (seg_out >= 0)).astype(values.dtype)
    opening = opening.reshape((out_len,) + (1,) * (values.ndim - 1))
    return (prior_part * opening, even_part, odd_part)


def freq_taps(values):
    frames, bins_in = (values.shape[0], values.shape[1])
    paired = values.reshape((frames, bins_in // 2, 2) + values.shape[2:])
    even_part = paired[:, :, 0]
    odd_part = paired[:, :, 1]
    prior_part = jnp.concatenate([jnp.zeros_like(odd_part[:, :1]), odd_part[:, :-1]], axis=1)
    return (prior_part, even_part, odd_part)


def strided_conv(values, kernel, seg_in, seg_out):
    summed = None
    for tap_row, tap_rows in enumerate(time_taps(values, seg_in, seg_out)):
        for tap_col, tap_piece in enumerate(freq_taps(tap_rows)):
            if tap_piece.ndim == 2:
                tap_piece = tap_piece[:, :, None]
            addend = tap_piece * kernel[3 * tap_row + tap_col]
            summed = addend if summed is None else summed + addend
    present = (seg_out >= 0).astype(summed.dtype)
    return summed * present[:, None, None]


def depth_glu(gated_rows, kernel, segments):
    model_width = gated_rows.shape[1] // 2
    merged = gated_rows[:, :model_width] * jax.nn.sigmoid(gated_rows[:, model_width:])
    radius = kernel.shape[0] // 2
    frames = gated_rows.shape[0]
    padded = jnp.pad(merged, ((radius, radius), (0, 0)))
    padded_segs = jnp.pad(segments, (radius, radius), constant_values=-2)
    summed = jnp.zeros_like(merged)
    for tap_index in range(kernel.shape[0]):
        same_segment = (padded_segs[tap_index : tap_index + frames] == segments).astype(
            merged.dtype
        )
        summed = (
            summed
            + padded[tap_index : tap_index + frames] * same_segment[:, None] * kernel[tap_index]
        )
    return summed


def stem_front(masked, first_kernel, second_kernel, segments):
    seg_zero = jnp.repeat(segments, 8)
    seg_one = jnp.repeat(segments, 4)
    seg_two = jnp.repeat(segments, 2)
    level_one = jax.nn.silu(strided_conv(masked, first_kernel, seg_zero, seg_one))
    return strided_conv(level_one, second_kernel, seg_one, seg_two)


def stem_middle(point_two, third_kernel, segments):
    frames = segments.shape[0]
    channels = point_two.shape[1]
    hidden = jax.nn.silu(point_two).reshape(frames * 2, -1, channels)
    return strided_conv(hidden, third_kernel, jnp.repeat(segments, 2), segments)


def matmul(operand, matrix):
    return jnp.dot(operand, matrix, preferred_element_type=jnp.float32)


def over_rows(operand, matrix):
    return lax.dot_general(
        operand, matrix, (((0,), (0,)), ((), ())), preferred_element_type=jnp.float32
    )


def against(operand, matrix):
    return lax.dot_general(
        operand, matrix, (((1,), (1,)), ((), ())), preferred_element_type=jnp.float32
    )


def ffn_forward(stream, norm_gain, norm_shift, inner_weight, outer_weight):
    normed = layer_norm(stream, norm_gain, norm_shift).astype(jnp.bfloat16)
    hidden = matmul(normed, inner_weight)
    active = jax.nn.silu(hidden).astype(jnp.bfloat16)
    return (matmul(active, outer_weight), (normed, hidden, active))


def ffn_backward(stream, norm_gain, norm_shift, inner_weight, outer_weight, kept_values, grad_out):
    normed, hidden, active = kept_values
    grad_outer = over_rows(active, grad_out)
    grad_active = against(grad_out, outer_weight)
    grad_hidden = jax.vjp(jax.nn.silu, hidden)[1](grad_active)[0].astype(jnp.bfloat16)
    grad_inner = over_rows(normed, grad_hidden)
    grad_normed = against(grad_hidden, inner_weight)
    pullback = jax.vjp(layer_norm, stream, norm_gain, norm_shift)[1]
    grad_stream, grad_gain, grad_shift = pullback(grad_normed)
    return (grad_stream, grad_gain, grad_shift, grad_inner, grad_outer)


def split_heads(joined, head_count):
    frames = joined.shape[0]
    model_width = joined.shape[1] // 3
    shaped = joined.reshape(frames, 3, head_count, model_width // head_count)
    return (shaped[:, 0], shaped[:, 1], shaped[:, 2])


def block_logits(queries, key_rows, query_segs, key_segs, anchor, frames, contexts):
    scores = jnp.einsum("qhd,khd->hqk", queries, key_rows, preferred_element_type=jnp.float32)
    radius = (key_rows.shape[0] - queries.shape[0]) // 2
    query_pos = anchor + jnp.arange(queries.shape[0], dtype=jnp.int32)
    key_pos = anchor - radius + jnp.arange(key_rows.shape[0], dtype=jnp.int32)
    distance = jnp.abs(query_pos[:, None] - key_pos[None, :])
    allowed = (
        (query_segs[:, None] == key_segs[None, :])
        & (key_pos[None, :] >= 0)
        & (key_pos[None, :] < frames)
    )
    allowed = allowed[None] & (distance[None] <= contexts[:, None, None])
    return jnp.where(allowed, scores * queries.shape[2] ** (-0.5), MASKED_LOGIT)


def attend_forward(joined, segments, contexts):
    frames = joined.shape[0]
    queries, key_rows, value_rows = split_heads(joined, contexts.shape[0])
    padded_keys = jnp.pad(key_rows, ((CTX, CTX), (0, 0), (0, 0)))
    padded_values = jnp.pad(value_rows, ((CTX, CTX), (0, 0), (0, 0)))
    padded_segs = jnp.pad(segments, (CTX, CTX), constant_values=-2)
    logits = block_logits(queries, padded_keys, segments, padded_segs, 0, frames, contexts)
    highest = jnp.max(logits, axis=-1, keepdims=True)
    exponent = jnp.exp(logits - highest)
    summed = jnp.sum(exponent, axis=-1, keepdims=True)
    weights = (exponent / summed).astype(jnp.bfloat16)
    outputs = jnp.einsum("hqk,khd->qhd", weights, padded_values, preferred_element_type=jnp.float32)
    log_parts = highest[:, :, 0] + jnp.log(summed[:, :, 0])
    return (outputs, log_parts)


def attend_backward(joined, segments, contexts, log_totals, grad_mixed):
    frames = joined.shape[0]
    queries, key_rows, value_rows = split_heads(joined, contexts.shape[0])
    padded_keys = jnp.pad(key_rows, ((CTX, CTX), (0, 0), (0, 0)))
    padded_values = jnp.pad(value_rows, ((CTX, CTX), (0, 0), (0, 0)))
    padded_segs = jnp.pad(segments, (CTX, CTX), constant_values=-2)
    block_rows = min(frames, 512)
    grad_keys = jnp.zeros(padded_keys.shape, jnp.float32)
    grad_values = jnp.zeros(padded_values.shape, jnp.float32)
    query_span = slice(0, block_rows)
    key_span = slice(0, block_rows + 2 * CTX)
    logits = block_logits(queries, padded_keys, segments, padded_segs, 0, frames, contexts)
    weights = jnp.exp(logits - log_totals[:, query_span, None])
    grad_weights = jnp.einsum(
        "qhd,khd->hqk", grad_mixed, padded_values, preferred_element_type=jnp.float32
    )
    row_dot = jnp.sum(weights * grad_weights, axis=-1, keepdims=True)
    grad_scores = (weights * (grad_weights - row_dot) * queries.shape[2] ** (-0.5)).astype(
        jnp.bfloat16
    )
    grad_queries = jnp.einsum(
        "hqk,khd->qhd", grad_scores, padded_keys, preferred_element_type=jnp.float32
    )
    grad_keys = grad_keys.at[key_span].add(
        jnp.einsum("hqk,qhd->khd", grad_scores, queries, preferred_element_type=jnp.float32)
    )
    grad_values = grad_values.at[key_span].add(
        jnp.einsum(
            "hqk,qhd->khd",
            weights.astype(jnp.bfloat16),
            grad_mixed,
            preferred_element_type=jnp.float32,
        )
    )
    stacked = jnp.stack(
        [grad_queries, grad_keys[CTX : CTX + frames], grad_values[CTX : CTX + frames]], axis=1
    )
    return stacked.reshape(frames, -1)


def local_plain(
    mel,
    cotangent,
    lengths,
    assignment,
    time_spans,
    freq_spans,
    contexts,
    stem_kernels,
    stem_point,
    stem_out,
    ffn_in,
    ffn_out,
    qkv,
    attn_out,
    conv_in,
    conv_depth,
    conv_out,
    norm_gains,
    norm_shifts,
    final_shift,
):
    device = lax.axis_index(AXES[0]) * lax.axis_size(AXES[1]) + lax.axis_index(AXES[1])
    frames = cotangent.shape[0]
    segments = frame_segments(lengths, assignment, device, frames)
    feature_mask = feature_keep(segments, time_spans[0], freq_spans[0], mel.shape[1])
    present = (segments >= 0).astype(jnp.float32)[:, None]
    counted = jnp.sum(lengths).astype(jnp.float32)
    gathered = (
        lax.all_gather(stem_kernels, AXES, axis=2, tiled=True),
        lax.all_gather(stem_point, AXES, axis=1, tiled=True),
        lax.all_gather(stem_out, AXES, axis=0, tiled=True),
        lax.all_gather(ffn_in, AXES, axis=1, tiled=True),
        lax.all_gather(ffn_out, AXES, axis=1, tiled=True),
        lax.all_gather(qkv, AXES, axis=0, tiled=True),
        lax.all_gather(attn_out, AXES, axis=0, tiled=True),
        lax.all_gather(conv_in, AXES, axis=0, tiled=True),
        lax.all_gather(conv_depth, AXES, axis=1, tiled=True),
        lax.all_gather(conv_out, AXES, axis=0, tiled=True),
        lax.all_gather(norm_gains, AXES, axis=1, tiled=True),
        lax.all_gather(norm_shifts, AXES, axis=1, tiled=True),
        lax.all_gather(final_shift, AXES, axis=0, tiled=True),
    )
    (
        kernels,
        point_weight,
        stem_weight,
        ffn_inner,
        ffn_outer,
        qkv_weight,
        out_weight,
        conv_inner,
        conv_taps,
        conv_outer,
        norm_rows,
        shift_rows,
        final_row,
    ) = gathered
    kernels_wide = kernels.astype(jnp.float32)
    gains_wide = norm_rows.astype(jnp.float32)
    shifts_wide = shift_rows.astype(jnp.float32)
    final_wide = final_row.astype(jnp.float32)
    masked = mel.astype(jnp.float32) * feature_mask
    level_two, front_pullback = jax.vjp(
        lambda masked_input, first_taps, second_taps: stem_front(
            masked_input, first_taps, second_taps, segments
        ),
        masked,
        kernels_wide[0],
        kernels_wide[1],
    )
    channels = level_two.shape[2]
    level_two_low = level_two.reshape(-1, channels).astype(jnp.bfloat16)
    point_two = matmul(level_two_low, point_weight[0])
    level_three, middle_pullback = jax.vjp(
        lambda point_input, third_taps: stem_middle(point_input, third_taps, segments),
        point_two,
        kernels_wide[2],
    )
    level_three_low = level_three.reshape(-1, channels).astype(jnp.bfloat16)
    point_three = matmul(level_three_low, point_weight[1])
    stem_hidden = jax.nn.silu(point_three).reshape(frames, -1).astype(jnp.bfloat16)
    after_stem = matmul(stem_hidden, stem_weight)
    ffn_result_one, ffn_kept_one = ffn_forward(
        after_stem, gains_wide[0], shifts_wide[0], ffn_inner[0], ffn_outer[0]
    )
    after_ffn = after_stem + 0.5 * ffn_result_one
    attn_normed = layer_norm(after_ffn, gains_wide[1], shifts_wide[1]).astype(jnp.bfloat16)
    joined = matmul(attn_normed, qkv_weight).astype(jnp.bfloat16)
    mixed_heads, log_totals = attend_forward(joined, segments, contexts)
    mixed_low = mixed_heads.reshape(frames, -1).astype(jnp.bfloat16)
    after_attn = after_ffn + matmul(mixed_low, out_weight)
    conv_normed = layer_norm(after_attn, gains_wide[2], shifts_wide[2]).astype(jnp.bfloat16)
    gated_rows = matmul(conv_normed, conv_inner)
    taps_wide = conv_taps.astype(jnp.float32)
    depthwise, depth_pullback = jax.vjp(
        lambda gate_input, taps_input: depth_glu(gate_input, taps_input, segments),
        gated_rows,
        taps_wide,
    )
    first_sum, second_sum = lax.psum(
        (jnp.sum(depthwise * present, axis=0), jnp.sum(depthwise * depthwise * present, axis=0)),
        AXES,
    )
    average = first_sum / counted
    spread = second_sum / counted - average * average
    inv_spread = lax.rsqrt(spread + EPSILON)
    standard = (depthwise - average) * inv_spread
    batch_normed = standard * gains_wide[3] + shifts_wide[3]
    conv_active = jax.nn.silu(batch_normed).astype(jnp.bfloat16)
    after_conv = after_attn + matmul(conv_active, conv_outer)
    ffn_result_two, ffn_kept_two = ffn_forward(
        after_conv, gains_wide[4], shifts_wide[4], ffn_inner[1], ffn_outer[1]
    )
    after_second = after_conv + 0.5 * ffn_result_two
    activations = (layer_norm(after_second, gains_wide[5], final_wide) * present).astype(
        jnp.bfloat16
    )
    weights_back = (
        lax.all_gather(stem_kernels, AXES, axis=2, tiled=True),
        lax.all_gather(stem_point, AXES, axis=1, tiled=True),
        lax.all_gather(stem_out, AXES, axis=0, tiled=True),
        lax.all_gather(ffn_in, AXES, axis=1, tiled=True),
        lax.all_gather(ffn_out, AXES, axis=1, tiled=True),
        lax.all_gather(qkv, AXES, axis=0, tiled=True),
        lax.all_gather(attn_out, AXES, axis=0, tiled=True),
        lax.all_gather(conv_in, AXES, axis=0, tiled=True),
        lax.all_gather(conv_depth, AXES, axis=1, tiled=True),
        lax.all_gather(conv_out, AXES, axis=0, tiled=True),
        lax.all_gather(norm_gains, AXES, axis=1, tiled=True),
        lax.all_gather(norm_shifts, AXES, axis=1, tiled=True),
        lax.all_gather(final_shift, AXES, axis=0, tiled=True),
    )
    (
        back_kernels,
        back_point,
        back_stem,
        back_inner,
        back_outer,
        back_qkv,
        back_attn,
        back_conv_in,
        back_taps,
        back_conv_out,
        back_gains,
        back_shifts,
        back_final,
    ) = weights_back
    back_gains_wide = back_gains.astype(jnp.float32)
    back_shifts_wide = back_shifts.astype(jnp.float32)
    back_final_wide = back_final.astype(jnp.float32)
    grad_final = cotangent.astype(jnp.float32) * present
    pullback = jax.vjp(layer_norm, after_second, back_gains_wide[5], back_final_wide)[1]
    grad_stream, grad_gain_final, grad_shift_final = pullback(grad_final)
    ffn_two = ffn_backward(
        after_conv,
        back_gains_wide[4],
        back_shifts_wide[4],
        back_inner[1],
        back_outer[1],
        ffn_kept_two,
        (0.5 * grad_stream).astype(jnp.bfloat16),
    )
    grad_stream = grad_stream + ffn_two[0]
    grad_conv_low = grad_stream.astype(jnp.bfloat16)
    grad_conv_out = over_rows(conv_active, grad_conv_low)
    grad_active = against(grad_conv_low, back_conv_out)
    grad_batch = jax.vjp(jax.nn.silu, batch_normed)[1](grad_active)[0]
    beta_sum, gamma_sum = lax.psum(
        (jnp.sum(grad_batch * present, axis=0), jnp.sum(grad_batch * standard * present, axis=0)),
        AXES,
    )
    bn_gain = back_gains_wide[3]
    grad_first = (
        inv_spread * inv_spread * bn_gain * gamma_sum * average - inv_spread * bn_gain * beta_sum
    ) / counted
    grad_second = -0.5 * inv_spread * inv_spread * bn_gain * gamma_sum / counted
    grad_depth = bn_gain * inv_spread * grad_batch + present * (
        grad_first + 2.0 * depthwise * grad_second
    )
    grad_gated, grad_taps = depth_pullback(grad_depth)
    grad_gated_low = grad_gated.astype(jnp.bfloat16)
    grad_conv_in = over_rows(conv_normed, grad_gated_low)
    pullback = jax.vjp(layer_norm, after_attn, back_gains_wide[2], back_shifts_wide[2])[1]
    conv_norm_grads = pullback(against(grad_gated_low, back_conv_in))
    grad_stream = grad_stream + conv_norm_grads[0]
    grad_attn_low = grad_stream.astype(jnp.bfloat16)
    grad_attn_out = over_rows(mixed_low, grad_attn_low)
    grad_mixed = against(grad_attn_low, back_attn).astype(jnp.bfloat16).reshape(mixed_heads.shape)
    grad_joined = attend_backward(joined, segments, contexts, log_totals, grad_mixed).astype(
        jnp.bfloat16
    )
    grad_qkv = over_rows(attn_normed, grad_joined)
    pullback = jax.vjp(layer_norm, after_ffn, back_gains_wide[1], back_shifts_wide[1])[1]
    attn_norm_grads = pullback(against(grad_joined, back_qkv))
    grad_stream = grad_stream + attn_norm_grads[0]
    ffn_one = ffn_backward(
        after_stem,
        back_gains_wide[0],
        back_shifts_wide[0],
        back_inner[0],
        back_outer[0],
        ffn_kept_one,
        (0.5 * grad_stream).astype(jnp.bfloat16),
    )
    grad_stream = grad_stream + ffn_one[0]
    grad_stem_low = grad_stream.astype(jnp.bfloat16)
    grad_stem_out = over_rows(stem_hidden, grad_stem_low)
    grad_hidden = against(grad_stem_low, back_stem).reshape(point_three.shape)
    grad_point_three = jax.vjp(jax.nn.silu, point_three)[1](grad_hidden)[0].astype(jnp.bfloat16)
    grad_third_point = over_rows(level_three_low, grad_point_three)
    grad_level_three = against(grad_point_three, back_point[1]).reshape(level_three.shape)
    grad_point_two, grad_third_kernel = middle_pullback(grad_level_three)
    grad_point_two_low = grad_point_two.astype(jnp.bfloat16)
    grad_second_point = over_rows(level_two_low, grad_point_two_low)
    grad_level_two = against(grad_point_two_low, back_point[0]).reshape(level_two.shape)
    grad_masked, grad_first_kernel, grad_second_kernel = front_pullback(grad_level_two)
    mel_grad = grad_masked * feature_mask
    zero_row = jnp.zeros_like(grad_gain_final)
    grad_gains = jnp.stack(
        [ffn_one[1], attn_norm_grads[1], conv_norm_grads[1], zero_row, ffn_two[1], grad_gain_final]
    )
    grad_shifts = jnp.stack(
        [ffn_one[2], attn_norm_grads[2], conv_norm_grads[2], zero_row, ffn_two[2]]
    )
    grad_kernels = jnp.stack([grad_first_kernel, grad_second_kernel, grad_third_kernel])
    grad_points = jnp.stack([grad_second_point, grad_third_point])
    grad_inner = jnp.stack([ffn_one[3], ffn_two[3]])
    grad_outer = jnp.stack([ffn_one[4], ffn_two[4]])
    owned_grads = (
        lax.psum_scatter(grad_kernels, AXES, scatter_dimension=2, tiled=True),
        lax.psum_scatter(grad_points, AXES, scatter_dimension=1, tiled=True),
        lax.psum_scatter(grad_stem_out, AXES, scatter_dimension=0, tiled=True),
        lax.psum_scatter(grad_inner, AXES, scatter_dimension=1, tiled=True),
        lax.psum_scatter(grad_outer, AXES, scatter_dimension=1, tiled=True),
        lax.psum_scatter(grad_qkv, AXES, scatter_dimension=0, tiled=True),
        lax.psum_scatter(grad_attn_out, AXES, scatter_dimension=0, tiled=True),
        lax.psum_scatter(grad_conv_in, AXES, scatter_dimension=0, tiled=True),
        lax.psum_scatter(grad_taps, AXES, scatter_dimension=1, tiled=True),
        lax.psum_scatter(grad_conv_out, AXES, scatter_dimension=0, tiled=True),
        lax.psum_scatter(grad_gains, AXES, scatter_dimension=1, tiled=True),
        lax.psum_scatter(grad_shifts, AXES, scatter_dimension=1, tiled=True),
        lax.psum_scatter(grad_shift_final, AXES, scatter_dimension=0, tiled=True),
    )
    share_width = gamma_sum.shape[0] // (lax.axis_size(AXES[0]) * lax.axis_size(AXES[1]))
    own_gamma = lax.dynamic_slice_in_dim(gamma_sum, device * share_width, share_width)
    own_beta = lax.dynamic_slice_in_dim(beta_sum, device * share_width, share_width)
    owned_gains = owned_grads[10].at[3].add(own_gamma)
    owned_shifts = owned_grads[11].at[3].add(own_beta)
    return (
        activations,
        mel_grad,
        owned_grads[0],
        owned_grads[1],
        owned_grads[2],
        owned_grads[3],
        owned_grads[4],
        owned_grads[5],
        owned_grads[6],
        owned_grads[7],
        owned_grads[8],
        owned_grads[9],
        owned_gains,
        owned_shifts,
        owned_grads[12],
    )


def gather_sources(v):
    return [
        v.small,
        v.point,
        v.stem_out,
        v.ffn_in.at[0],
        v.ffn_out.at[0],
        v.qkv,
        v.attn_out,
        v.conv_in,
        v.conv_out,
        v.ffn_in.at[1],
        v.ffn_out.at[1],
    ]


STEM_MOMENT = 17
STEM_STEP = 5.0
SMALL_MOMENT = 68
MOMENTS = (0, 0, 0, 10, 10, 14, 15, 15, 17, SMALL_MOMENT, 17, SMALL_MOMENT)
LINK_BYTES = 1e4
LATENCY = 8.0
AHEAD = 8.0


def order_of_steps(sums, grads):
    size = [grads[i].block[0] * width * 2 / LINK_BYTES for i, _, width in sums]
    waiting = list(range(len(sums)))
    hopped, steps = [], []
    now, z_free = 0.0, 0.0
    while waiting or hopped:
        ready = [entry for entry in hopped if entry[0] <= now]
        fresh = [p for p in waiting if MOMENTS[sums[p][0]] <= now]
        if ready:
            entry = ready[0]
            hopped.remove(entry)
            arrived, p = entry
            steps.append((max(arrived, now - AHEAD), 1, p))
            now += size[p] / 2
            landed = now + LATENCY
            steps.append((landed, 2, p))
            z_free = max(z_free, landed) + size[p]
            steps.append((z_free + 2 * LATENCY, 3, p))
        elif fresh:
            p = fresh[0]
            waiting.remove(p)
            steps.append((max(MOMENTS[sums[p][0]], now - AHEAD), 0, p))
            now += size[p]
            hopped.append((now + LATENCY, p))
        else:
            now = min([entry[0] for entry in hopped] + [MOMENTS[sums[p][0]] for p in waiting])
    return sorted(steps)


def finish_kernel(count, *refs):
    for i in range(count):
        refs[count + i][...] = refs[i][...]


def local(
    mel,
    cotangent,
    lengths,
    assignment,
    time_spans,
    freq_spans,
    contexts,
    stem_kernels,
    stem_point,
    stem_out,
    ffn_in,
    ffn_out,
    qkv,
    attn_out,
    conv_in,
    conv_depth,
    conv_out,
    norm_gains,
    norm_shifts,
    final_shift,
):
    arguments = (mel, cotangent, lengths, assignment, time_spans, freq_spans, contexts)
    arguments += (stem_kernels, stem_point, stem_out, ffn_in, ffn_out, qkv, attn_out)
    arguments += (conv_in, conv_depth, conv_out, norm_gains, norm_shifts, final_shift)
    if qkv.shape[0] % TILE or stem_out.shape[0] % TILE:
        return local_plain(*arguments)
    sizes = grid_sizes()
    devices = sizes[0] * sizes[1] * sizes[2] * sizes[3]
    frames, width = cotangent.shape
    bins = mel.shape[1]
    channels = stem_point.shape[2]
    hidden = ffn_in.shape[2]
    heads = contexts.shape[0]
    bins_two, bins_three = 4 * GROUPS, 2 * GROUPS
    inputs = dict(
        mel=(mel.T, pltpu.VMEM),
        stem_kernels=(stem_kernels.swapaxes(1, 2), pltpu.VMEM),
        stem_point=(stem_point, pltpu.VMEM),
        conv_depth=(conv_depth, pltpu.VMEM),
        norm_gains=(norm_gains, pltpu.VMEM),
        norm_shifts=(norm_shifts, pltpu.VMEM),
        final_shift=(final_shift.reshape(1, -1), pltpu.VMEM),
        cotangent=(cotangent, pltpu.VMEM),
        lengths=(lengths.reshape(1, -1), pltpu.VMEM),
        assignment=(assignment.reshape(1, -1), pltpu.VMEM),
        time_spans=(time_spans, pltpu.SMEM),
        freq_spans=(freq_spans, pltpu.SMEM),
        contexts=(contexts, pltpu.SMEM),
        stem_out=(stem_out, pl.ANY),
        ffn_in=(ffn_in, pl.ANY),
        ffn_out=(ffn_out, pl.ANY),
        qkv=(qkv, pl.ANY),
        attn_out=(attn_out, pl.ANY),
        conv_in=(conv_in, pl.ANY),
        conv_out=(conv_out, pl.ANY),
    )
    shards = [
        (64, LANES),
        (stem_point.shape[1], 2 * channels),
        stem_out.shape,
        ffn_in.shape[1:],
        ffn_out.shape[1:],
        qkv.shape,
        attn_out.shape,
        conv_in.shape,
        conv_out.shape,
        ffn_in.shape[1:],
        ffn_out.shape[1:],
    ]
    count = len(shards)

    def cut(item, width, pieces=2):
        return [(item, width // pieces * k, width // pieces) for k in range(pieces)]

    def whole(item):
        return cut(item, shards[item][1], 1)

    def halved(item):
        return cut(item, shards[item][1])

    groups = [whole(0) + whole(1) + whole(6), whole(8)]
    groups += [[piece] for item in (2, 3, 4, 5) for piece in halved(item)]
    groups += [whole(7)] + [[piece] for item in (9, 10) for piece in halved(item)]
    pieces = [piece for group in groups for piece in group]
    turns = [[pieces.index(piece) for piece in group] for group in groups]
    dma = pltpu.SemaphoreType.DMA
    z_steps = max(1, sizes[2] - 1)
    wide = max(1, sizes[0] - 1, sizes[1] - 1)
    near = sizes[2] * CORES - 1
    far = max(1, sizes[0] * sizes[1] - 1)
    tokens = (frames, width)
    total_rows = (max(8, 2 * width // LANES), LANES)
    scratch = dict(
        held=[pltpu.VMEM(sizes + s, F32 if i == 1 else BF16) for i, s in enumerate(shards)],
        g_local=dma((len(pieces),)),
        g_z=dma((2, len(pieces), z_steps)),
        g_hop=dma((2, len(pieces), 2, 2, wide)),
        g_core=dma((2, len(pieces))),
        t_own=pltpu.VMEM((2,) + total_rows, F32),
        t_mid=pltpu.VMEM((2,) + total_rows, F32),
        t_near=pltpu.VMEM((2, near) + total_rows, F32),
        t_far=pltpu.VMEM((2, far) + total_rows, F32),
        t_sem=dma((2, 2, near + far)),
        packed=pltpu.VMEM((64, LANES), F32),
        small=pltpu.VMEM((64, LANES), BF16),
        point=pltpu.VMEM((stem_point.shape[1], 2 * channels), F32),
        frames_wide=pltpu.VMEM((8 * frames, LANES), F32),
        feats=pltpu.VMEM((9, frames, LANES), F32),
        windows=pltpu.VMEM((GROUPS, 4 * frames, LANES), BF16),
        params=pltpu.VMEM((32, width), F32),
        kernels=pltpu.VMEM((32, channels), F32),
        band_wide=pltpu.VMEM((LANES, channels), F32),
        banded=pltpu.VMEM((LANES, 8 * channels), BF16),
        points=pltpu.VMEM((2, channels, channels), BF16),
        ones_wide=pltpu.VMEM((3, 4 * frames, channels), F32),
        ones=pltpu.VMEM((4, 4 * frames, channels), BF16),
        two_even=pltpu.VMEM((2 * frames, channels), F32),
        two_odd=pltpu.VMEM((2, 2 * frames, channels), F32),
        level_now=pltpu.VMEM((2 * frames, channels), BF16),
        level_two=pltpu.VMEM((bins_two, channels, 2 * frames), BF16),
        point_two=pltpu.VMEM((bins_two, 2 * frames, channels), BF16),
        level_three=pltpu.VMEM((bins_three, channels, frames), BF16),
        point_three=pltpu.VMEM((bins_three, frames, channels), BF16),
        weights=pltpu.VMEM((heads, frames, frames), F32),
        joined=pltpu.VMEM((frames, 3 * width), BF16),
        gated=pltpu.VMEM((frames, 2 * width), F32),
        hidden0=pltpu.VMEM((frames, hidden), BF16),
        hidden1=pltpu.VMEM((frames, hidden), BF16),
        active0=pltpu.VMEM((frames, hidden), BF16),
        active1=pltpu.VMEM((frames, hidden), BF16),
        after_stem=pltpu.VMEM(tokens, F32),
        after_ffn=pltpu.VMEM(tokens, F32),
        after_attn=pltpu.VMEM(tokens, F32),
        after_conv=pltpu.VMEM(tokens, F32),
        after_second=pltpu.VMEM(tokens, F32),
        merged=pltpu.VMEM(tokens, F32),
        depthwise=pltpu.VMEM(tokens, F32),
        standard=pltpu.VMEM(tokens, F32),
        batch_normed=pltpu.VMEM(tokens, F32),
        normed0=pltpu.VMEM(tokens, BF16),
        normed1=pltpu.VMEM(tokens, BF16),
        normed2=pltpu.VMEM(tokens, BF16),
        normed4=pltpu.VMEM(tokens, BF16),
        mixed=pltpu.VMEM(tokens, BF16),
        conv_active=pltpu.VMEM(tokens, BF16),
    )
    outputs = dict(
        activations=(tokens, BF16),
        mel_grad=((bins, 8 * frames), F32),
        grad_kernels=((3, channels // devices, 9), F32),
        grad_point=((2 * channels // devices, channels), F32),
        grad_stem=(stem_out.shape, F32),
        grad_inner=(ffn_in.shape, F32),
        grad_outer=(ffn_out.shape, F32),
        grad_qkv=(qkv.shape, F32),
        grad_attn=(attn_out.shape, F32),
        grad_conv_in=(conv_in.shape, F32),
        grad_depth=(conv_depth.shape, F32),
        grad_conv_out=(conv_out.shape, F32),
        grad_gains=(norm_gains.shape, F32),
        grad_shifts=(norm_shifts.shape, F32),
        grad_final=((1, width // devices), F32),
    )
    grads = [
        types.SimpleNamespace(weight=weight, product=weight > 0, block=block)
        for weight, block in [(weight, shards[weight]) for weight in range(10, 1, -1)]
        + [(0, (2 * channels // devices, channels)), (0, (32, LANES)), (0, (32, LANES))]
    ]
    lead = sizes[:3]
    columns, mates, right, parts, kept, landed, landed_z = {}, {}, {}, {}, {}, {}, {}
    for i, spec in enumerate(grads):
        rows, breadth = spec.block
        if spec.product:
            columns[i] = pltpu.VMEM(sizes + (rows, frames), BF16)
            mates[i] = pltpu.VMEM(lead + (rows, frames), BF16)
            right[i] = pltpu.VMEM((2 * frames, breadth), BF16)
        else:
            parts[i] = pltpu.VMEM(sizes + spec.block, BF16)
            kept[i] = pltpu.VMEM(lead + spec.block, BF16)
            mates[i] = pltpu.VMEM(lead + spec.block, BF16)
    sums = []
    for i, spec in enumerate(grads):
        large = spec.block[0] * spec.block[1] >= 2**14 + 2**12 and spec.block[1] % (4 * LANES) == 0
        sums += cut(i, spec.block[1], 2 if large else 1)
    for p, (i, _, breadth) in enumerate(sums):
        rows = grads[i].block[0]
        split = 2 if breadth // 2 % LANES == 0 else 1
        part = (rows, breadth // split)
        landed[p] = []
        for order in range(split):
            one, two = (1, 0) if order == 0 else (0, 1)
            steps = (max(1, sizes[one] - 1), max(1, sizes[two] - 1))
            landed[p].append(
                [
                    pltpu.VMEM((steps[0], sizes[two], sizes[2]) + part, BF16),
                    pltpu.VMEM((steps[1], sizes[2]) + part, BF16),
                ]
            )
        landed_z[p] = pltpu.VMEM((z_steps, rows, breadth), BF16)
    scratch |= dict(
        columns=columns,
        mates=mates,
        right=right,
        parts=parts,
        kept=kept,
        landed=landed,
        landed_z=landed_z,
        s_core=dma((2, len(grads), 2)),
        s_hop=dma((2, len(sums), 2, 2, wide)),
        s_z=dma((2, len(sums), z_steps)),
        stem_hidden=pltpu.VMEM((frames, bins_three * channels), BF16),
        sum_wide=pltpu.VMEM((32, LANES), F32),
        sum_taps=pltpu.VMEM((32, LANES), F32),
        d_params=pltpu.VMEM((32, width), F32),
        d_taps=pltpu.VMEM((32, channels), F32),
        stream=pltpu.VMEM(tokens, F32),
        grad_batch=pltpu.VMEM(tokens, F32),
        g_mixed=pltpu.VMEM(tokens, BF16),
        g_three=pltpu.VMEM((frames, bins_three * channels), BF16),
        g_two=pltpu.VMEM((2, 2 * frames, channels), BF16),
        g_one=pltpu.VMEM((4 * frames, 4 * channels), BF16),
        d_three=pltpu.VMEM((2, 2 * frames, channels), F32),
        d_two_even=pltpu.VMEM((2, 3 * frames, channels), BF16),
        d_two_odd=pltpu.VMEM((3 * frames, channels), BF16),
        d_kernels=pltpu.VMEM((27, 8, channels), F32),
        d_points=pltpu.VMEM((2, channels, channels), F32),
        d_windows=pltpu.VMEM((GROUPS, 4 * frames, LANES), F32),
        d_banded=pltpu.VMEM((LANES, 8 * channels), F32),
        window_turned=pltpu.VMEM((LANES, 4 * frames), BF16),
    )
    plan = types.SimpleNamespace(
        sizes=sizes,
        frames=frames,
        bins=bins,
        count=count,
        width=width,
        channels=channels,
        heads=heads,
        radius=conv_depth.shape[0] // 2,
        time_masks=time_spans.shape[1],
        freq_masks=freq_spans.shape[1],
        sources=gather_sources,
        grads=grads,
        pieces=pieces,
        turns=turns,
        sums=sums,
        steps=order_of_steps(sums, grads),
        small_moment=SMALL_MOMENT,
    )
    kinds = ({name: 0 for name in inputs}, {name: 0 for name in outputs}, scratch)
    plan.trees = [jax.tree.structure(kind) for kind in kinds]
    results = pl.pallas_call(
        functools.partial(layer_kernel, plan),
        out_shape=[jax.ShapeDtypeStruct(*spec) for _, spec in sorted(outputs.items())],
        in_specs=[pl.BlockSpec(memory_space=space) for _, (_, space) in sorted(inputs.items())],
        out_specs=[pl.BlockSpec(memory_space=pltpu.VMEM)] * len(outputs),
        scratch_shapes=jax.tree.leaves(scratch),
        compiler_params=pltpu.CompilerParams(
            collective_id=0, has_side_effects=True, vmem_limit_bytes=63 * 2**20
        ),
        name="layer",
    )(*[value for _, (value, _) in sorted(inputs.items())])
    made = types.SimpleNamespace(**dict(zip(sorted(outputs), results)))
    finals = [
        (made.mel_grad, made.mel_grad.shape),
        (made.activations, tokens),
        (made.grad_kernels, made.grad_kernels.shape),
        (made.grad_point, made.grad_point.shape),
        (made.grad_stem, stem_out.shape),
        (made.grad_inner, ffn_in.shape),
        (made.grad_outer, ffn_out.shape),
        (made.grad_qkv, qkv.shape),
        (made.grad_attn, attn_out.shape),
        (made.grad_conv_in, conv_in.shape),
        (made.grad_depth, conv_depth.shape),
        (made.grad_conv_out, conv_out.shape),
        (made.grad_gains, norm_gains.shape),
        (made.grad_shifts, norm_shifts.shape),
        (made.grad_final, made.grad_final.shape),
    ]
    done = pl.pallas_call(
        functools.partial(finish_kernel, len(finals)),
        out_shape=[jax.ShapeDtypeStruct(shape, value.dtype) for value, shape in finals],
        in_specs=[pl.BlockSpec(memory_space=pltpu.VMEM)] * len(finals),
        out_specs=[pl.BlockSpec(memory_space=pltpu.VMEM)] * len(finals),
        name="finish",
    )(*[value for value, _ in finals])
    return (
        done[1],
        done[0].T,
        done[2].swapaxes(1, 2),
        done[3].reshape(stem_point.shape),
        *done[4:14],
        done[14].reshape(final_shift.shape),
    )


def solution(mesh):
    return jax.shard_map(
        local,
        mesh=mesh,
        in_specs=(
            P(AXES, None),
            P(AXES, None),
            P(),
            P(),
            P(AXES, None, None),
            P(AXES, None, None),
            P(),
            P(None, None, AXES),
            P(None, AXES, None),
            P(AXES, None),
            P(None, AXES, None),
            P(None, AXES, None),
            P(AXES, None),
            P(AXES, None),
            P(AXES, None),
            P(None, AXES),
            P(AXES, None),
            P(None, AXES),
            P(None, AXES),
            P(AXES),
        ),
        out_specs=(
            P(AXES, None),
            P(AXES, None),
            P(None, None, AXES),
            P(None, AXES, None),
            P(AXES, None),
            P(None, AXES, None),
            P(None, AXES, None),
            P(AXES, None),
            P(AXES, None),
            P(AXES, None),
            P(None, AXES),
            P(AXES, None),
            P(None, AXES),
            P(None, AXES),
            P(AXES),
        ),
        check_vma=False,
    )
```
